256 devices in a mesh: dp: 16 (over z, x_lo), tensor: 16 (over x_hi, y, core).
Axes of the slice: x: 4 (x_hi: 2, x_lo: 2; x = x_hi * 2 + x_lo), y: 4, z: 8, core: 2. Of those that a mesh axis runs over, the one named last changes fastest.
Arguments:
- residual_in: bfloat16 [8192, 5120], P('dp'), may hold values from -6 to 6
- layernorm_gain: float32 [5120], replicated, may hold values from 0.2 to 8, as said below
- layernorm_bias: float32 [5120], replicated, may hold values from -3 to 3
- qkv_weight: bfloat16 [3, 5120, 4096], P(None, 'dp', 'tensor'), may hold values from -2.5 to 2.5, as said below
- out_weight: bfloat16 [4096, 5120], P('tensor', 'dp'), may hold values from -0.09375 to 0.09375
- encoder: bfloat16 [5120, 640], P('dp'), may hold values from -0.078125 to 0.078125
- decoder: bfloat16 [640, 5120], P(None, 'tensor'), may hold values from -0.25 to 0.25
- grad_output: bfloat16 [8192, 5120], P('dp', 'tensor'), may hold values from -6 to 6
Outputs:
- residual_out: bfloat16 [8192, 5120], P('dp', 'tensor')
- grad_input: bfloat16 [8192, 5120], P('dp', 'tensor')
- grad_qkv: float32 [3, 5120, 4096], P(None, 'dp', 'tensor')
- grad_out_weight: float32 [4096, 5120], P('tensor', 'dp')
- grad_gain: float32 [5120], P('tensor')
- grad_bias: float32 [5120], P('tensor')
The draws below stay inside these ranges and needn't reach their ends.
Inputs may be any that keep to these rules, and one draw needn't show every extreme that they name: `qkv_weight`: projections to queries, keys and values; entries of order 1 / sqrt(5120) or larger. `layernorm_gain`: positive gains.
All inputs are finite; a program needn't handle non-finite values.
Results may differ from the reference program's by a relative error of at most 0.035.
Values may be sent and summed in bfloat16 or wider, within the bound.
A program may use at most 192 MiB of HBM per device.

```python
import jax
import jax.numpy as jnp
from jax import lax

D = 5120
HDIM = 128
C = 640
HEADS_DEV = 2
SEQ = 512
HEADS = 32
TOKENS = 8192
N_DP = 16
N_TENSOR = 16


def draw_qkv_weight(key, part):
    key = jax.random.fold_in(key, 11)
    leading_part = jax.random.fold_in(key, 0)
    feature_width = HEADS * HDIM
    base = jax.random.truncated_normal(leading_part, -4.0, 4.0, (3, D, feature_width), jnp.float32) / jnp.sqrt(jnp.float32(D))
    return base.astype(jnp.bfloat16)


def gain_profile(position, lowest, highest, rough):
    return jnp.clip(lowest * jnp.exp(position * jnp.log(highest / lowest)) * rough, 0.2, 8.0)


def draw_layernorm_gain(key, part):
    key = jax.random.fold_in(key, 23)
    position = jnp.arange(D, dtype=jnp.float32) / jnp.float32(max(D - 1, 1))
    rough = jnp.exp(0.2 * jax.random.truncated_normal(key, -3.0, 3.0, (D,), jnp.float32))
    gain = gain_profile(position, 0.35, 3.5, rough)
    return gain.astype(jnp.float32)


def block_scale(stream_key, dims, pieces, least, top_value):
    def one(axis_at, shards_of):
        steps = jax.random.uniform(jax.random.fold_in(jax.random.fold_in(stream_key, 6), axis_at), (shards_of,), jnp.float32, least / len(pieces), top_value / len(pieces))
        return jnp.repeat(jnp.exp(steps), dims[axis_at] // shards_of).reshape((-1,) + (1,) * (len(dims) - axis_at - 1))

    level = one(*pieces[0])
    for cut in pieces[1:]:
        level = level * one(*cut)
    return level


def gaussian(rng, extent, deviation, bound, shards=(), kind=jnp.bfloat16):
    result = jax.random.normal(rng, extent, jnp.float32) * deviation
    if len(shards) > 0:
        result = block_scale(rng, extent, shards, -0.22, 0.18) * result
    return jnp.clip(result, min=-bound, max=bound).astype(kind)


def setup_inputs(seed: int = 0) -> dict:
    arg_keys = jax.random.split(jax.random.key(seed), 9)
    residual_in = gaussian(arg_keys[0], (TOKENS, D), 1.0, 6.0, ((0, 16),))
    layernorm_gain = draw_layernorm_gain(jax.random.fold_in(arg_keys[8], 71), 0)
    layernorm_bias = gaussian(arg_keys[2], (D,), 0.5, 3.0, (), jnp.float32)
    qkv_weight = draw_qkv_weight(jax.random.fold_in(arg_keys[8], 71), 0)
    out_weight = gaussian(arg_keys[4], (HEADS * HDIM, D), (HEADS * HDIM) ** -0.5, 0.09375, ((0, 16), (1, 16)))
    encoder = gaussian(arg_keys[5], (D, C), D ** -0.5, 0.078125, ((0, 16),))
    decoder = gaussian(arg_keys[6], (C, D), C ** -0.5, 0.25, ((1, 16),))
    grad_output = gaussian(arg_keys[7], (TOKENS, D), 1.0, 6.0, ((0, 16), (1, 16)))
    return dict(residual_in=residual_in, layernorm_gain=layernorm_gain, layernorm_bias=layernorm_bias, qkv_weight=qkv_weight, out_weight=out_weight, encoder=encoder, decoder=decoder, grad_output=grad_output)


EPS = 1e-05
HIGH = lax.Precision.HIGHEST

def attention_core(qkv, head_size):
    seq = qkv.shape[0]
    feature_width = qkv.shape[2]
    heads = feature_width // head_size
    split = qkv.reshape(seq, 3, heads, head_size)
    query = split[:, 0]
    keys = split[:, 1]
    values = split[:, 2]
    scores = jnp.einsum('qhd,khd->hqk', query, keys, preferred_element_type=jnp.float32) / jnp.sqrt(jnp.float32(head_size))
    rows = lax.broadcasted_iota(jnp.int32, (seq, seq), 0)
    column_list = lax.broadcasted_iota(jnp.int32, (seq, seq), 1)
    scores = jnp.where((column_list <= rows)[None], scores, jnp.float32(-1e+30))
    top = lax.optimization_barrier(jnp.max(scores, axis=2, keepdims=True))
    expo = jnp.exp(scores - top)
    probs = expo / lax.optimization_barrier(jnp.sum(expo, axis=2, keepdims=True))
    mixed = jnp.einsum('hqk,khd->qhd', probs.astype(jnp.bfloat16), values, preferred_element_type=jnp.float32)
    return mixed.reshape(seq, feature_width).astype(jnp.bfloat16)

def reference(residual_in, layernorm_gain, layernorm_bias, qkv_weight, out_weight, encoder, decoder, grad_output):
    feature_width = residual_in.shape[1]
    group = HEADS_DEV * HDIM
    folded = jnp.dot(out_weight, encoder, preferred_element_type=jnp.float32)
    inputs = residual_in.reshape(N_DP, SEQ, feature_width)
    grads = grad_output.reshape(N_DP, SEQ, feature_width)
    weight_groups = qkv_weight.reshape(3, feature_width, N_TENSOR, group)

    def one_sequence(carry, pair):
        acc_qkv, acc_mix, gain_accumulator, acc_bias = carry
        seq_in, sequence_gradient = pair
        input_float = seq_in.astype(jnp.float32)
        row_mean = lax.optimization_barrier(jnp.mean(input_float, axis=1, keepdims=True))
        var = lax.optimization_barrier(jnp.mean((input_float - row_mean) ** 2, axis=1, keepdims=True))
        inverse_deviation = lax.rsqrt(var + EPS)
        centered_input = (input_float - row_mean) * inverse_deviation
        normalized_rows = (centered_input * layernorm_gain + layernorm_bias).astype(jnp.bfloat16)
        qkv = jnp.einsum('td,jdq->tjq', normalized_rows, qkv_weight, preferred_element_type=jnp.float32).astype(jnp.bfloat16)
        attn = attention_core(qkv, HDIM)
        code = jnp.dot(attn.astype(jnp.float32), folded, precision=HIGH)
        decoded = jnp.dot(code.astype(jnp.bfloat16), decoder, preferred_element_type=jnp.float32)
        out_rows = (input_float + decoded).astype(jnp.bfloat16)
        code_grad = jnp.dot(sequence_gradient, decoder.T, preferred_element_type=jnp.float32)
        attn_grad = jnp.dot(code_grad, folded.T, precision=HIGH).astype(jnp.bfloat16)
        mixing = jnp.dot(attn.astype(jnp.float32).T, code_grad, precision=HIGH)
        _, pullback = jax.vjp(lambda t: attention_core(t, HDIM), qkv)
        qkv_grad = pullback(attn_grad)[0]
        grad_groups = qkv_grad.reshape(SEQ, 3, N_TENSOR, group)
        parts = jnp.einsum('tjnq,jdnq->ntd', grad_groups, weight_groups, preferred_element_type=jnp.float32)
        rounded = lax.optimization_barrier(parts.astype(jnp.bfloat16))
        layernorm_gradient = lax.optimization_barrier(jnp.sum(rounded.astype(jnp.float32), axis=0))
        scaled_rows = layernorm_gradient * layernorm_gain
        leading_part = lax.optimization_barrier(jnp.sum(scaled_rows, axis=1, keepdims=True)) / feature_width
        trailing_part = lax.optimization_barrier(jnp.sum(scaled_rows * centered_input, axis=1, keepdims=True)) / feature_width
        input_rows = (sequence_gradient.astype(jnp.float32) + inverse_deviation * (scaled_rows - leading_part - centered_input * trailing_part)).astype(jnp.bfloat16)
        gain_accumulator = gain_accumulator + lax.optimization_barrier(jnp.sum(layernorm_gradient * centered_input, axis=0))
        acc_bias = acc_bias + lax.optimization_barrier(jnp.sum(layernorm_gradient, axis=0))
        acc_qkv = acc_qkv + jnp.einsum('td,tjq->jdq', normalized_rows, qkv_grad, preferred_element_type=jnp.float32)
        acc_mix = acc_mix + mixing
        return ((acc_qkv, acc_mix, gain_accumulator, acc_bias), (out_rows, input_rows))
    start = (jnp.zeros(qkv_weight.shape, jnp.float32), jnp.zeros(folded.shape, jnp.float32), jnp.zeros((feature_width,), jnp.float32), jnp.zeros((feature_width,), jnp.float32))
    totals, rows_out = lax.scan(one_sequence, start, (inputs, grads))
    acc_qkv, acc_mix, gain_accumulator, acc_bias = totals
    residual_out = rows_out[0].reshape(N_DP * SEQ, feature_width)
    grad_input = rows_out[1].reshape(N_DP * SEQ, feature_width)
    grad_out_weight = jnp.dot(acc_mix, encoder.astype(jnp.float32).T, precision=HIGH) / N_DP
    return (residual_out, grad_input, acc_qkv / N_DP, grad_out_weight, gain_accumulator / N_DP, acc_bias / N_DP)
```

```python
import functools

import jax
import jax.numpy as jnp
from jax import lax
from jax.experimental import pallas as pl
from jax.experimental.pallas import tpu as pltpu
from jax.sharding import PartitionSpec as P

HDIM = 128
EPS = 1e-05
MESH = pl.DeviceIdType.MESH
F32, BF = jnp.float32, jnp.bfloat16

NZ, NY, NQ, NR = 8, 4, 8, 16
SEQ, D, C, W3 = 512, 5120, 640, 768
BLK = 320
SLAB = 640
LR = 192
RB = SLAB - LR
CH = RB // 2
BR = BLK - LR


def rem(a, n):
    return lax.rem(a, n)


def rows(start, size):
    return pl.ds(pl.multiple_of(start, 16), size)


def dot(a, b):
    return lax.dot_general(a, b, (((1,), (0,)), ((), ())), preferred_element_type=F32)


def dot_tn(a, b):
    return lax.dot_general(a, b, (((0,), (0,)), ((), ())), preferred_element_type=F32)


def remote(src, dst, ssem, rsem, **device):
    return pltpu.make_async_remote_copy(
        src_ref=src, dst_ref=dst, send_sem=ssem, recv_sem=rsem, device_id=device, device_id_type=MESH
    )


def enter():
    barrier = pltpu.get_barrier_semaphore()
    for axis in ("dp", "tensor"):
        me = lax.axis_index(axis)
        for k in range(1, NR):
            pl.semaphore_signal(barrier, inc=1, device_id={axis: rem(me + k, NR)}, device_id_type=MESH)
    pl.semaphore_wait(barrier, 2 * (NR - 1))


class Sum:
    def __init__(self, axis, part, got, half, ring, out, ssem, rsem):
        self.axis, self.part, self.got, self.half, self.ring, self.out = axis, part, got, half, ring, out
        self.ssem, self.rsem = ssem, rsem
        index = lax.axis_index(axis)
        self.a, self.q = rem(index, 2), index // 2
        self.h = part.shape[0] // 2
        self.b = self.h // NQ
        self.sent = []

    def pair(self):
        return {self.axis: self.q * 2 + 1 - self.a}

    def peer(self, k):
        return {self.axis: rem(self.q + k, NQ) * 2 + self.a}

    def go(self, copy):
        copy.start()
        self.sent.append(copy)

    def first(self):
        src = self.part.at[rows((1 - self.a) * self.h, self.h), :]
        self.go(remote(src, self.got, self.ssem.at[0], self.rsem.at[0], **self.pair()))

    def second(self):
        remote(self.got, self.got, self.ssem.at[0], self.rsem.at[0], **self.pair()).wait_recv()
        mine = self.part[rows(self.a * self.h, self.h), :].astype(F32)
        self.half[...] = (mine + self.got[...].astype(F32)).astype(BF)
        for k in range(1, NQ):
            to = rem(self.q + k, NQ)
            self.go(
                remote(
                    self.half.at[rows(to * self.b, self.b), :],
                    self.ring.at[self.q],
                    self.ssem.at[k],
                    self.rsem.at[k],
                    **self.peer(k),
                )
            )

    def third(self):
        total = self.half[rows(self.q * self.b, self.b), :].astype(F32)
        for k in range(1, NQ):
            source = rem(self.q + NQ - k, NQ)
            slot = self.ring.at[source]
            remote(slot, slot, self.ssem.at[k], self.rsem.at[k], **self.peer(k)).wait_recv()
            total = total + self.ring[source].astype(F32)
        here = rows(self.a * self.h + self.q * self.b, self.b)
        self.out[here, :] = total.astype(BF)
        for k in range(1, NQ):
            piece = self.out.at[here, :]
            self.go(remote(piece, piece, self.ssem.at[7 + k], self.rsem.at[7 + k], **self.peer(k)))

    def fourth(self):
        for k in range(1, NQ):
            source = rem(self.q + NQ - k, NQ)
            piece = self.out.at[rows(self.a * self.h + source * self.b, self.b), :]
            remote(piece, piece, self.ssem.at[7 + k], self.rsem.at[7 + k], **self.peer(k)).wait_recv()
        mine = self.out.at[rows(self.a * self.h, self.h), :]
        self.go(remote(mine, mine, self.ssem.at[15], self.rsem.at[15], **self.pair()))

    def last(self):
        other = self.out.at[rows((1 - self.a) * self.h, self.h), :]
        remote(other, other, self.ssem.at[15], self.rsem.at[15], **self.pair()).wait_recv()

    def drain(self):
        for copy in self.sent:
            copy.wait_send()


def sum_scratch(r):
    h = r // 2
    return [
        pltpu.VMEM((h, C), BF),
        pltpu.VMEM((h, C), BF),
        pltpu.VMEM((NQ, h // NQ, C), BF),
        pltpu.SemaphoreType.DMA((16,)),
        pltpu.SemaphoreType.DMA((16,)),
    ]


def forward_kernel(
    x, gain, bias, w_in, owt, enc, dect, got,
    qkv, w_out, nt_out, mu, rstd, code_grad, folded,
    w, norm, normt, acc, cg_part, fo_part,
    t_got, t_half, t_ring, t_ss, t_rs,
    d_got, d_half, d_ring, d_ss, d_rs,
    a_ss, a_rs, b_ss, b_rs, c_ss, c_rs, loc, outs,
):
    dp = lax.axis_index("dp")
    z, xl = dp // 2, rem(dp, 2)
    up, down = rem(z + 1, NZ) * 2 + xl, rem(z + NZ - 1, NZ) * 2 + xl
    other = z * 2 + 1 - xl
    sent = []

    def go(copy):
        copy.start()
        sent.append(copy)

    def block(zs, offset, size):
        return w.at[:, rows(zs * SLAB + offset, size), :]

    own = BLK * xl
    shared = BLK - BR * xl
    crossing = RB * xl
    incoming = RB * (1 - xl)

    enter()
    mine = pltpu.make_async_copy(w_in, block(z, own, BLK), loc)
    mine.start()
    first = LR * (1 - xl)
    go(remote(w_in.at[:, rows(first, BR), :], block(z, own + first, BR), b_ss.at[0], b_rs.at[0], dp=other))
    for way, to in ((0, up), (1, down)):
        go(remote(w_in, block(z, own, BLK), a_ss.at[way, 0], a_rs.at[way, 0], dp=to))
    go(remote(w_in.at[:, rows(BR * xl, LR), :], block(z, crossing, LR), c_ss.at[0], c_rs.at[0], dp=other))

    cg_part[...] = dot_tn(got[...], dect[...]).astype(BF)
    sum_t = Sum("tensor", cg_part, t_got, t_half, t_ring, code_grad, t_ss, t_rs)
    sum_t.first()
    fo_part[...] = dot_tn(owt[...], enc[...]).astype(BF)
    sum_d = Sum("dp", fo_part, d_got, d_half, d_ring, folded, d_ss, d_rs)
    sum_d.first()

    piece = block(z, shared, BR)
    remote(piece, piece, b_ss.at[0], b_rs.at[0], dp=other).wait_recv()
    for way, to in ((0, up), (1, down)):
        go(remote(piece, piece, b_ss.at[1 + way * 4], b_rs.at[1 + way * 4], dp=to))

    @pl.loop(0, SEQ // 16)
    def _(i):
        here = rows(i * 16, 16)
        v = x[here, :].astype(F32)
        mean = jnp.sum(v, axis=1, keepdims=True) * (1.0 / D)
        v = v - mean
        var = jnp.sum(v * v, axis=1, keepdims=True) * (1.0 / D)
        scale = lax.rsqrt(var + EPS)
        mu[here, :] = mean
        rstd[here, :] = scale
        v = (v * scale * gain[...] + bias[...]).astype(BF)
        for s in range(NZ):
            norm[s, here, :] = v[:, s * SLAB : (s + 1) * SLAB]

    def step(s):
        for way, to, zs in ((0, up, rem(z + NZ - s, NZ)), (1, down, rem(z + s, NZ))):
            part = block(zs, own, BLK)
            remote(part, part, a_ss.at[way, s - 1], a_rs.at[way, s - 1], dp=to).wait_recv()
            if s == 3:
                part = block(zs, own + way * (BLK // 2), BLK // 2)
            go(remote(part, part, a_ss.at[way, s], a_rs.at[way, s], dp=to))
            part = block(zs, crossing, LR)
            k = s + way * 3
            go(remote(part, part, c_ss.at[k], c_rs.at[k], dp=other))
        for way, to, zs in ((0, up, rem(z + NZ - s, NZ)), (1, down, rem(z + s, NZ))):
            part = block(zs, shared, BR)
            k = s + way * 4
            remote(part, part, b_ss.at[k], b_rs.at[k], dp=to).wait_recv()
            if s == 3:
                part = block(zs, shared + way * (BR // 2), BR // 2)
            go(remote(part, part, b_ss.at[k + 1], b_rs.at[k + 1], dp=to))

    def use(zs, k, begin=False):
        part = block(zs, incoming, LR)
        remote(part, part, c_ss.at[k], c_rs.at[k], dp=other).wait_recv()
        whole = block(zs, 0, SLAB)
        leaves.append(pltpu.make_async_copy(whole, w_out.at[:, rows(zs * SLAB, SLAB), :], outs.at[k]))
        leaves[-1].start()

        @pl.loop(0, 2)
        def _(i):
            here = rows(i * 256, 256)
            a = norm[zs, here, :]
            for j in range(3):
                cols = slice(j * 256, (j + 1) * 256)
                term = dot(a, w[j, rows(zs * SLAB, SLAB), :])
                if begin:
                    acc[here, cols] = term
                else:
                    acc[here, cols] += term

        @pl.loop(0, 4)
        def _(i):
            here = pl.ds(pl.multiple_of(i * 128, 128), 128)
            normt[zs, :, here] = norm[zs, here, :].T

        leaves.append(pltpu.make_async_copy(normt.at[zs], nt_out.at[zs], outs.at[8 + k]))
        leaves[-1].start()

    leaves = []
    sum_t.second()
    sum_d.second()
    step(1)
    mine.wait()
    use(z, 0, True)
    sum_t.third()
    sum_d.third()
    step(2)
    use(rem(z + NZ - 1, NZ), 1)
    use(rem(z + 1, NZ), 4)
    sum_t.fourth()
    sum_d.fourth()
    step(3)
    use(rem(z + NZ - 2, NZ), 2)
    use(rem(z + 2, NZ), 5)
    z4 = rem(z + 4, NZ)
    for way, to in ((0, up), (1, down)):
        part = block(z4, own + way * (BLK // 2), BLK // 2)
        remote(part, part, a_ss.at[way, 3], a_rs.at[way, 3], dp=to).wait_recv()
    part = block(z4, crossing, LR)
    go(remote(part, part, c_ss.at[7], c_rs.at[7], dp=other))
    use(rem(z + NZ - 3, NZ), 3)
    use(rem(z + 3, NZ), 6)
    for way, to in ((0, up), (1, down)):
        part = block(z4, shared + way * (BR // 2), BR // 2)
        remote(part, part, b_ss.at[4 + way * 4], b_rs.at[4 + way * 4], dp=to).wait_recv()
    use(z4, 7)
    qkv[...] = acc[...].astype(BF)
    sum_t.last()
    sum_d.last()
    sum_t.drain()
    sum_d.drain()
    for copy in sent:
        copy.wait_send()
    for copy in leaves:
        copy.wait()


def vmem():
    return pl.BlockSpec(memory_space=pltpu.VMEM)


def hbm():
    return pl.BlockSpec(memory_space=pl.ANY)


def dma(*shape):
    return pltpu.SemaphoreType.DMA(shape)


def shape(dims, kind):
    return jax.ShapeDtypeStruct(dims, kind)


def forward(x, gain, bias, w, owt, enc, dect, got):
    return pl.pallas_call(
        forward_kernel,
        out_shape=[
            shape((SEQ, W3), BF),
            shape((3, D, 256), BF),
            shape((NZ, SLAB, SEQ), BF),
            shape((SEQ, 1), F32),
            shape((SEQ, 1), F32),
            shape((SEQ, C), BF),
            shape((256, C), BF),
        ],
        in_specs=[vmem()] * 8,
        out_specs=[vmem(), hbm(), hbm(), vmem(), vmem(), vmem(), vmem()],
        scratch_shapes=[
            pltpu.VMEM((3, D, 256), BF),
            pltpu.VMEM((NZ, SEQ, SLAB), BF),
            pltpu.VMEM((NZ, SLAB, SEQ), BF),
            pltpu.VMEM((SEQ, W3), F32),
            pltpu.VMEM((SEQ, C), BF),
            pltpu.VMEM((256, C), BF),
        ]
        + sum_scratch(SEQ)
        + sum_scratch(256)
        + [dma(2, 4), dma(2, 4), dma(9), dma(9), dma(8), dma(8), pltpu.SemaphoreType.DMA, dma(16)],
        compiler_params=pltpu.CompilerParams(
            collective_id=0, has_side_effects=True, vmem_limit_bytes=56 * 2**20
        ),
    )(x, gain, bias, w, owt, enc, dect, got)


def add_rows(dst, src, count):
    @pl.loop(0, count // 32)
    def _(i):
        here = rows(i * 32, 32)
        dst[here, :] = (dst[here, :].astype(F32) + src[here, :].astype(F32)).astype(BF)


def backward_kernel(
    w_hbm, nt_hbm, qg, qgt, attn, attnt, cg, folded, xhat, gain, go_t, rstd,
    gq, gi_t, code, mixing, gb,
    w, nt, con, xr, rb1, rb, mr,
    cs, cr, ys, yr, xs, xv, ng, lt, gs,
    cp_part, mx_part,
    t_got, t_half, t_ring, t_ss, t_rs,
    d_got, d_half, d_ring, d_ss, d_rs,
    x_ss, x_rs, r1_ss, r1_rs, r_ss, r_rs, m_ss, m_rs,
    cs_ss, cs_rs, y_ss, y_rs, xh_ss, xh_rs, lt_ss, lt_rs, gs_ss, gs_rs, w_sem, nt_sem,
):
    dp, tensor = lax.axis_index("dp"), lax.axis_index("tensor")
    z, xl = dp // 2, rem(dp, 2)
    up, down = rem(z + 1, NZ) * 2 + xl, rem(z + NZ - 1, NZ) * 2 + xl
    other = z * 2 + 1 - xl
    core, q = rem(tensor, 2), tensor // 2
    xh, y = q // NY, rem(q, NY)
    sent = []

    def go(copy):
        copy.start()
        sent.append(copy)

    def order(i):
        odd = rem(i, 2)
        return rem(z + odd * (4 - (i + 1) // 2) + (1 - odd) * (4 + i // 2), NZ)

    def nt_copy(i):
        return pltpu.make_async_copy(nt_hbm.at[order(i)], nt.at[order(i)], nt_sem.at[i])

    for i in range(NZ):
        nt_copy(i).start()
    w_copy = pltpu.make_async_copy(w_hbm, w, w_sem)
    w_copy.start()
    enter()

    base = LR * xl
    crossing, incoming = RB * (1 - xl), RB * xl

    def cross(i):
        return remote(con.at[order(i), rows(crossing, LR), :], xr.at[i], x_ss.at[i], x_rs.at[i], dp=other)

    @pl.loop(0, NZ)
    def _(i):
        nt_copy(i).wait()
        zd = order(i)

        @pl.loop(0, 5)
        def _(k):
            here = rows(k * 128, 128)
            con[zd, here, :] = dot(nt[zd, here, :], qg[...]).astype(BF)

        cross(i).start()

    def add_crossed(i):
        remote(xr.at[i], xr.at[i], x_ss.at[i], x_rs.at[i], dp=other).wait_recv()
        add_rows(con.at[order(i), rows(incoming, LR), :], xr.at[i], LR)

    def chunk(zd, c):
        return con.at[zd, rows(base + c * CH, CH), :]

    ways = ((0, up), (1, down))
    add_crossed(0)
    for way, to in ways:
        go(remote(chunk(order(0), way), rb1.at[way], r1_ss.at[way], r1_rs.at[way], dp=to))

    def ring(s):
        for way, to in ways:
            i = 2 * s - 3 + way
            zd = order(i)
            add_crossed(i)
            for c in (way, 1 - way):
                if s == 2:
                    if c == way:
                        remote(rb1.at[way], rb1.at[way], r1_ss.at[way], r1_rs.at[way], dp=to).wait_recv()
                        add_rows(chunk(zd, c), rb1.at[way], CH)
                else:
                    slot = rb.at[way, s - 3, c]
                    remote(slot, slot, r_ss.at[way, s - 3, c], r_rs.at[way, s - 3, c], dp=to).wait_recv()
                    add_rows(chunk(zd, c), slot, CH)
                go(remote(chunk(zd, c), rb.at[way, s - 2, c], r_ss.at[way, s - 2, c], r_rs.at[way, s - 2, c], dp=to))

    w_copy.wait()

    def feature(i):
        return rem(i, 2) * NY + rem(y + 1 + i // 2, NY)

    def term(block):
        here = rows(block * BLK, BLK)
        out = dot(w[0, here, :], qgt[0:256, :])
        out = out + dot(w[1, here, :], qgt[256:512, :])
        return out + dot(w[2, here, :], qgt[512:768, :])

    def to_core(i):
        return remote(cs.at[i], cr.at[i], cs_ss.at[i], cs_rs.at[i], tensor=q * 2 + 1 - core)

    def to_y(i):
        return remote(
            ys.at[i], yr.at[i], y_ss.at[i], y_rs.at[i], tensor=(xh * NY + rem(y + 1 + i // 2, NY)) * 2 + core
        )

    @pl.loop(0, NQ)
    def _(i):
        cs[i] = term(feature(i) * 2 + 1 - core).astype(BF)
        to_core(i).start()

    def own_block(i):
        total = term(feature(i) * 2 + core)
        to_core(i).wait_recv()
        ys[i] = (total + cr[i].astype(F32)).astype(BF)

    @pl.loop(0, NQ - 2)
    def _(i):
        own_block(i)
        to_y(i).start()

    @pl.loop(NQ - 2, NQ)
    def _(i):
        own_block(i)

    ring(2)
    cp_part[...] = dot(attn[...], folded[...]).astype(BF)
    sum_t = Sum("tensor", cp_part, t_got, t_half, t_ring, code, t_ss, t_rs)
    sum_t.first()
    mx_part[...] = dot(attnt[...], cg[...]).astype(BF)
    sum_d = Sum("dp", mx_part, d_got, d_half, d_ring, mixing, d_ss, d_rs)
    sum_d.first()
    ring(3)

    for i in range(NQ - 2):
        remote(yr.at[i], yr.at[i], y_ss.at[i], y_rs.at[i], tensor=tensor).wait_recv()

    def y_sum(which):
        total = ys[6 + which].astype(F32)
        for k in range(3):
            total = total + yr[2 * k + which].astype(F32)
        return total

    xs[...] = y_sum(1 - xh).astype(BF)
    swap = remote(xs, xv, xh_ss, xh_rs, tensor=((1 - xh) * NY + y) * 2 + core)
    swap.start()
    ng[...] = y_sum(xh)
    sum_t.second()
    sum_d.second()
    swap.wait_recv()

    grad = ng[...] + xv[...].astype(F32)
    ng[...] = grad
    scaled = grad * gain[...]
    hat = xhat[...]
    lt[tensor, 0:1, :] = jnp.sum(scaled, axis=0, keepdims=True)
    lt[tensor, 1:2, :] = jnp.sum(scaled * hat, axis=0, keepdims=True)
    for k in range(1, NR):
        slot = lt.at[tensor]
        go(remote(slot, slot, lt_ss.at[k], lt_rs.at[k], tensor=rem(tensor + k, NR)))

    def fold(v):
        v = v[:, 0:128] + v[:, 128:256] + v[:, 256:384] + v[:, 384:512]
        v = jnp.concatenate([v, jnp.zeros((64, 128), F32)], axis=0)
        return jnp.sum(v.T, axis=0, keepdims=True)

    gs[dp, 0:1, :] = fold(grad * hat)
    gs[dp, 1:2, :] = fold(grad)
    for k in range(1, NR):
        slot = gs.at[dp]
        go(remote(slot, slot, gs_ss.at[k], gs_rs.at[k], dp=rem(dp + k, NR)))

    ring(4)
    sum_t.third()
    sum_d.third()

    for k in range(1, NR):
        slot = lt.at[rem(tensor + NR - k, NR)]
        remote(slot, slot, lt_ss.at[k], lt_rs.at[k], tensor=tensor).wait_recv()
    sums = jnp.sum(lt[...], axis=0)
    lead, trail = sums[0:1, :] * (1.0 / D), sums[1:2, :] * (1.0 / D)
    gi_t[...] = (
        go_t[...].astype(F32) + rstd[...] * (ng[...] * gain[...] - lead - xhat[...] * trail)
    ).astype(BF)
    for k in range(1, NR):
        slot = gs.at[rem(dp + NR - k, NR)]
        remote(slot, slot, gs_ss.at[k], gs_rs.at[k], dp=dp).wait_recv()
    gb[...] = jnp.sum(gs[...], axis=0) * (1.0 / NR)
    sum_t.fourth()
    sum_d.fourth()

    add_crossed(7)
    for c in range(2):
        for way, to in ways:
            slot = rb.at[way, 2, c]
            remote(slot, slot, r_ss.at[way, 2, c], r_rs.at[way, 2, c], dp=to).wait_recv()
            add_rows(chunk(z, c), slot, CH)
    last = remote(con.at[z, rows(BLK - BR * xl, BR), :], mr, m_ss, m_rs, dp=other)
    last.start()
    last.wait_recv()
    add_rows(con.at[z, rows(LR + BR * xl, BR), :], mr, BR)
    for j in range(3):
        gq[j] = con[z, rows(BLK * xl, BLK), j * 256 : (j + 1) * 256].astype(F32) * (1.0 / NR)

    sum_t.last()
    sum_d.last()
    sum_t.drain()
    sum_d.drain()
    last.wait_send()
    swap.wait_send()
    for copy in sent:
        copy.wait_send()

    @pl.loop(0, NZ)
    def _(i):
        cross(i).wait_send()
        to_core(i).wait_send()

    @pl.loop(0, NQ - 2)
    def _(i):
        to_y(i).wait_send()


def backward(*args):
    return pl.pallas_call(
        backward_kernel,
        out_shape=[
            shape((3, BLK, 256), F32),
            shape((BLK, SEQ), BF),
            shape((SEQ, C), BF),
            shape((256, C), BF),
            shape((8, 384), F32),
        ],
        in_specs=[hbm(), hbm()] + [vmem()] * 10,
        out_specs=[vmem()] * 5,
        scratch_shapes=[
            pltpu.VMEM((3, D, 256), BF),
            pltpu.VMEM((NZ, SLAB, SEQ), BF),
            pltpu.VMEM((NZ, SLAB, W3), BF),
            pltpu.VMEM((NZ, LR, W3), BF),
            pltpu.VMEM((2, CH, W3), BF),
            pltpu.VMEM((2, 3, 2, CH, W3), BF),
            pltpu.VMEM((BR, W3), BF),
            pltpu.VMEM((NQ, BLK, SEQ), BF),
            pltpu.VMEM((NQ, BLK, SEQ), BF),
            pltpu.VMEM((NQ, BLK, SEQ), BF),
            pltpu.VMEM((NQ - 2, BLK, SEQ), BF),
            pltpu.VMEM((BLK, SEQ), BF),
            pltpu.VMEM((BLK, SEQ), BF),
            pltpu.VMEM((BLK, SEQ), F32),
            pltpu.VMEM((NR, 8, SEQ), F32),
            pltpu.VMEM((NR, 8, 384), F32),
            pltpu.VMEM((SEQ, C), BF),
            pltpu.VMEM((256, C), BF),
        ]
        + sum_scratch(SEQ)
        + sum_scratch(256)
        + [
            dma(NZ), dma(NZ), dma(2), dma(2), dma(2, 3, 2), dma(2, 3, 2),
            pltpu.SemaphoreType.DMA, pltpu.SemaphoreType.DMA,
            dma(NQ), dma(NQ), dma(NQ), dma(NQ),
            pltpu.SemaphoreType.DMA, pltpu.SemaphoreType.DMA,
            dma(NR), dma(NR), dma(NR), dma(NR), pltpu.SemaphoreType.DMA, dma(NZ),
        ],
        compiler_params=pltpu.CompilerParams(
            collective_id=1, has_side_effects=True, vmem_limit_bytes=60 * 2**20
        ),
    )(*args)


def attention_core(qkv, head_size):
    seq = qkv.shape[0]
    feature_width = qkv.shape[2]
    heads = feature_width // head_size
    split = qkv.reshape(seq, 3, heads, head_size)
    query = split[:, 0]
    keys = split[:, 1]
    values = split[:, 2]
    scores = jnp.einsum("qhd,khd->hqk", query, keys, preferred_element_type=jnp.float32) / jnp.sqrt(
        jnp.float32(head_size)
    )
    row_list = lax.broadcasted_iota(jnp.int32, (seq, seq), 0)
    column_list = lax.broadcasted_iota(jnp.int32, (seq, seq), 1)
    scores = jnp.where((column_list <= row_list)[None], scores, jnp.float32(-1e30))
    top = jnp.max(scores, axis=2, keepdims=True)
    expo = jnp.exp(scores - top)
    probs = expo / jnp.sum(expo, axis=2, keepdims=True)
    mixed = jnp.einsum(
        "hqk,khd->qhd", probs.astype(jnp.bfloat16), values, preferred_element_type=jnp.float32
    )
    return mixed.reshape(seq, feature_width).astype(jnp.bfloat16)


def local(
    residual_in,
    layernorm_gain,
    layernorm_bias,
    qkv_weight,
    out_weight,
    encoder,
    decoder,
    grad_output,
):
    start = lax.axis_index("tensor") * BLK
    qkv, weights, normt, mean, rstd, code_grad, folded = forward(
        residual_in,
        layernorm_gain[None, :],
        layernorm_bias[None, :],
        qkv_weight,
        out_weight.T,
        encoder,
        decoder.T,
        grad_output.T,
    )
    attn, pullback = jax.vjp(lambda t: attention_core(t, HDIM), qkv.reshape(SEQ, 3, 256))
    attn_grad = jnp.dot(code_grad, folded.T, preferred_element_type=F32).astype(BF)
    qkv_grad = pullback(attn_grad)[0].reshape(SEQ, W3)
    columns = lax.dynamic_slice_in_dim(residual_in, start, BLK, 1)
    xhat = ((columns.astype(F32) - mean) * rstd).T
    gain = lax.dynamic_slice_in_dim(layernorm_gain, start, BLK, 0)
    grad_qkv, grad_input, code, mixing, sums = backward(
        weights, normt, qkv_grad, qkv_grad.T, attn, attn.T, code_grad, folded,
        xhat, gain[:, None], grad_output.T, rstd.reshape(1, SEQ),
    )
    residual_out = (columns.astype(F32) + jnp.dot(code, decoder, preferred_element_type=F32)).astype(BF)
    grad_out_weight = lax.dot_general(
        mixing, encoder, (((1,), (1,)), ((), ())), preferred_element_type=F32
    ) * (1.0 / NR)
    return residual_out, grad_input.T, grad_qkv, grad_out_weight, sums[0, :BLK], sums[1, :BLK]


def solution(mesh):
    in_specs = (
        P("dp", None),
        P(),
        P(),
        P(None, "dp", "tensor"),
        P("tensor", "dp"),
        P("dp", None),
        P(None, "tensor"),
        P("dp", "tensor"),
    )
    out_specs = (
        P("dp", "tensor"),
        P("dp", "tensor"),
        P(None, "dp", "tensor"),
        P("tensor", "dp"),
        P("tensor"),
        P("tensor"),
    )
    return jax.shard_map(local, mesh=mesh, in_specs=in_specs, out_specs=out_specs, check_vma=False)
```

```python
import functools

import jax
import jax.numpy as jnp
from jax import lax
from jax.experimental import pallas as pl
from jax.experimental.pallas import tpu as pltpu
from jax.sharding import PartitionSpec as P

HDIM = 128
EPS = 1e-05
MESH = pl.DeviceIdType.MESH
F32, BF = jnp.float32, jnp.bfloat16

NZ, NY, NQ, NR = 8, 4, 8, 16
SEQ, D, C, W3 = 512, 5120, 640, 768
BLK = 320
SLAB = 640
LR = 160
RB = SLAB - LR
CH = RB // 2
BR = BLK - LR


def rem(a, n):
    return lax.rem(a, n)


def rows(start, size):
    return pl.ds(pl.multiple_of(start, 16), size)


def dot(a, b):
    return lax.dot_general(a, b, (((1,), (0,)), ((), ())), preferred_element_type=F32)


def dot_nt(a, b):
    return lax.dot_general(a, b, (((1,), (1,)), ((), ())), preferred_element_type=F32)


def dot_tn(a, b):
    return lax.dot_general(a, b, (((0,), (0,)), ((), ())), preferred_element_type=F32)


def remote(src, dst, ssem, rsem, **device):
    return pltpu.make_async_remote_copy(
        src_ref=src, dst_ref=dst, send_sem=ssem, recv_sem=rsem, device_id=device, device_id_type=MESH
    )


def enter():
    barrier = pltpu.get_barrier_semaphore()
    for axis in ("dp", "tensor"):
        me = lax.axis_index(axis)
        for k in range(1, NR):
            pl.semaphore_signal(barrier, inc=1, device_id={axis: rem(me + k, NR)}, device_id_type=MESH)
    pl.semaphore_wait(barrier, 2 * (NR - 1))


class Sum:
    def __init__(self, axis, part, out, buffers):
        self.axis, self.part, self.out = axis, part, out
        self.got, self.half, self.ring, self.mid, self.mid_got, self.ssem, self.rsem = buffers
        index = lax.axis_index(axis)
        self.n = self.ring.shape[0]
        self.a = rem(index, 2)
        self.q = rem(index // 2, self.n)
        self.top = index // (2 * self.n)
        self.h = part.shape[0] // 2
        self.b = self.h // self.n
        self.sent = []

    def at(self, top, q, a):
        return {self.axis: (top * self.n + q) * 2 + a}

    def pair(self):
        return self.at(self.top, self.q, 1 - self.a)

    def peer(self, k):
        return self.at(self.top, rem(self.q + k, self.n), self.a)

    def over(self):
        return self.at(1 - self.top, self.q, self.a)

    def go(self, copy):
        copy.start()
        self.sent.append(copy)

    def first(self):
        src = self.part.at[rows((1 - self.a) * self.h, self.h), :]
        self.go(remote(src, self.got, self.ssem.at[0], self.rsem.at[0], **self.pair()))

    def second(self):
        remote(self.got, self.got, self.ssem.at[0], self.rsem.at[0], **self.pair()).wait_recv()
        mine = self.part[rows(self.a * self.h, self.h), :].astype(F32)
        self.half[...] = (mine + self.got[...].astype(F32)).astype(BF)
        for k in range(1, self.n):
            to = rem(self.q + k, self.n)
            src = self.half.at[rows(to * self.b, self.b), :]
            self.go(remote(src, self.ring.at[self.q], self.ssem.at[k], self.rsem.at[k], **self.peer(k)))

    def reduced(self):
        total = self.half[rows(self.q * self.b, self.b), :].astype(F32)
        for k in range(1, self.n):
            source = rem(self.q + self.n - k, self.n)
            slot = self.ring.at[source]
            remote(slot, slot, self.ssem.at[k], self.rsem.at[k], **self.peer(k)).wait_recv()
            total = total + self.ring[source].astype(F32)
        return total

    def spread(self, total):
        here = rows(self.a * self.h + self.q * self.b, self.b)
        self.out[here, :] = total.astype(BF)
        piece = self.out.at[here, :]
        for k in range(1, self.n):
            self.go(remote(piece, piece, self.ssem.at[7 + k], self.rsem.at[7 + k], **self.peer(k)))

    def third(self):
        if self.mid is None:
            self.spread(self.reduced())
        else:
            self.mid[...] = self.reduced().astype(BF)
            self.go(remote(self.mid, self.mid_got, self.ssem.at[16], self.rsem.at[16], **self.over()))

    def across(self):
        remote(self.mid, self.mid_got, self.ssem.at[16], self.rsem.at[16], **self.over()).wait_recv()
        self.spread(self.mid[...].astype(F32) + self.mid_got[...].astype(F32))

    def fourth(self):
        for k in range(1, self.n):
            source = rem(self.q + self.n - k, self.n)
            piece = self.out.at[rows(self.a * self.h + source * self.b, self.b), :]
            remote(piece, piece, self.ssem.at[7 + k], self.rsem.at[7 + k], **self.peer(k)).wait_recv()
        mine = self.out.at[rows(self.a * self.h, self.h), :]
        self.go(remote(mine, mine, self.ssem.at[15], self.rsem.at[15], **self.pair()))

    def last(self):
        other = self.out.at[rows((1 - self.a) * self.h, self.h), :]
        remote(other, other, self.ssem.at[15], self.rsem.at[15], **self.pair()).wait_recv()

    def drain(self):
        for copy in self.sent:
            copy.wait_send()


def dma(*shape):
    return pltpu.SemaphoreType.DMA(shape)


def sum_buffers(r, n):
    h = r // 2
    cut = pltpu.VMEM((h // n, C), BF)
    mids = [cut, cut] if n == NY else [None, None]
    return [pltpu.VMEM((h, C), BF), pltpu.VMEM((h, C), BF), pltpu.VMEM((n, h // n, C), BF)] + mids + [dma(17), dma(17)]


def add_rows(dst, src, count):
    @pl.loop(0, count // 80)
    def _(i):
        here = rows(i * 80, 80)
        dst[here, :] = (dst[here, :].astype(F32) + src[here, :].astype(F32)).astype(BF)


def kernel(
    x_hbm, gain, bias, w_in, owt, enc, dect, got,
    ro_t, gi_t, gq, gow_t, gb,
    x, w, nt, acc, mu, rstd, xt, gcol, hat, st,
    cg_part, fo_part, cg, folded, qkv, ag, attn, qg, qgt, dkv,
    con, xr, rb1, rb, mr, cs, cr, ys, yr, xs, xv, ng, lt, gs, cp_part, mx_part, code, mixing,
    t1, d1, t2, d2,
    x_sem, loc, a_ss, a_rs, b_ss, b_rs, c_ss, c_rs,
    x_ss, x_rs, r1_ss, r1_rs, r_ss, r_rs, m_ss, m_rs,
    cs_ss, cs_rs, y_ss, y_rs, xh_ss, xh_rs, lt_ss, lt_rs, gs_ss, gs_rs,
):
    dp, tensor = lax.axis_index("dp"), lax.axis_index("tensor")
    z, xl = dp // 2, rem(dp, 2)
    up, down = rem(z + 1, NZ) * 2 + xl, rem(z + NZ - 1, NZ) * 2 + xl
    other = z * 2 + 1 - xl
    core, q = rem(tensor, 2), tensor // 2
    xh, y = q // NY, rem(q, NY)
    ways = ((0, up), (1, down))
    sent = []

    def go(copy):
        copy.start()
        sent.append(copy)

    x_copies = [
        pltpu.make_async_copy(x_hbm.at[pl.ds(i * 256, 256), :], x.at[pl.ds(i * 256, 256), :], x_sem.at[i])
        for i in range(2)
    ]
    for copy in x_copies:
        copy.start()

    def block(zs, offset, size):
        return w.at[:, rows(zs * SLAB + offset, size), :]

    own = BLK * xl
    shared = BLK - BR * xl
    crossing = RB * xl
    incoming = RB * (1 - xl)

    enter()
    mine = pltpu.make_async_copy(w_in, block(z, own, BLK), loc)
    mine.start()
    first = LR * (1 - xl)
    go(remote(w_in.at[:, rows(first, BR), :], block(z, own + first, BR), b_ss.at[0], b_rs.at[0], dp=other))
    for way, to in ways:
        go(remote(w_in, block(z, own, BLK), a_ss.at[way, 0], a_rs.at[way, 0], dp=to))
    go(remote(w_in.at[:, rows(BR * xl, LR), :], block(z, crossing, LR), c_ss.at[0], c_rs.at[0], dp=other))

    def slab_cols(zs):
        return pl.ds(pl.multiple_of(zs * SLAB, 128), SLAB)

    def norm(lo, hi):
        @pl.loop(lo, hi)
        def _(i):
            here = rows(i * 16, 16)
            v = x[here, :].astype(F32)
            mean = jnp.sum(v, axis=1, keepdims=True) * (1.0 / D)
            v = v - mean
            var = jnp.sum(v * v, axis=1, keepdims=True) * (1.0 / D)
            scale = lax.rsqrt(var + EPS)
            mu[here, :] = jnp.broadcast_to(mean, (16, 128))
            rstd[here, :] = jnp.broadcast_to(scale, (16, 128))
            x[here, :] = (v * scale * gain[...] + bias[...]).astype(BF)

    for copy in x_copies:
        copy.wait()

    @pl.loop(0, 4)
    def _(i):
        here = pl.ds(pl.multiple_of(i * 128, 128), 128)
        xt[:, here] = x[here, slab_cols(q)].T

    norm(0, 14)
    piece = block(z, shared, BR)
    remote(piece, piece, b_ss.at[0], b_rs.at[0], dp=other).wait_recv()
    for way, to in ways:
        go(remote(piece, piece, b_ss.at[1 + way * 4], b_rs.at[1 + way * 4], dp=to))
    norm(14, 32)

    def slabs(s):
        return ((0, up, rem(z + NZ - s, NZ)), (1, down, rem(z + s, NZ)))

    def step_a(s):
        for way, to, zs in slabs(s):
            part = block(zs, own, BLK)
            remote(part, part, a_ss.at[way, s - 1], a_rs.at[way, s - 1], dp=to).wait_recv()
            if s == 3:
                part = block(zs, own + way * (BLK // 2), BLK // 2)
            go(remote(part, part, a_ss.at[way, s], a_rs.at[way, s], dp=to))
            part = block(zs, crossing, LR)
            k = s + way * 3
            go(remote(part, part, c_ss.at[k], c_rs.at[k], dp=other))

    def step_b(s):
        for way, to, zs in slabs(s):
            part = block(zs, shared, BR)
            k = s + way * 4
            remote(part, part, b_ss.at[k], b_rs.at[k], dp=to).wait_recv()
            if s == 3:
                part = block(zs, shared + way * (BR // 2), BR // 2)
            go(remote(part, part, b_ss.at[k + 1], b_rs.at[k + 1], dp=to))

    def use(zs, k, begin=False):
        part = block(zs, incoming, LR)
        remote(part, part, c_ss.at[k], c_rs.at[k], dp=other).wait_recv()

        @pl.loop(0, 2)
        def _(i):
            here = rows(i * 256, 256)
            a = x[here, slab_cols(zs)]
            for j in range(3):
                cols = slice(j * 256, (j + 1) * 256)
                term = dot(a, w[j, rows(zs * SLAB, SLAB), :])
                if begin:
                    acc[here, cols] = term
                else:
                    acc[here, cols] += term

    def turn(zs):
        @pl.loop(0, 4)
        def _(i):
            here = pl.ds(pl.multiple_of(i * 128, 128), 128)
            nt[zs, :, here] = x[here, slab_cols(zs)].T

    step_a(1)
    cg_part[...] = dot_tn(got[...], dect[...]).astype(BF)
    sum_t = Sum("tensor", cg_part, cg, t1)
    sum_t.first()
    fo_part[...] = dot_tn(owt[...], enc[...]).astype(BF)
    sum_d = Sum("dp", fo_part, folded, d1)
    sum_d.first()
    step_b(1)
    mine.wait()
    use(z, 0, True)
    sum_t.second()
    turn(z)
    turn(rem(z + 4, NZ))
    step_a(2)
    sum_d.second()
    sum_t.third()
    use(rem(z + NZ - 1, NZ), 1)
    use(rem(z + 1, NZ), 4)
    step_b(2)
    sum_t.across()
    for k in (1, 2, 3):
        turn(rem(z + NZ - k, NZ))
        turn(rem(z + k, NZ))
    mu_row = mu[...].T[0:1, :]
    rs_row = rstd[...].T[0:1, :]
    gcol[...] = jnp.broadcast_to(gain[0:1, slab_cols(q)], (128, SLAB)).T
    mine_rows = rows(core * BLK, BLK)
    hat[...] = (xt[mine_rows, :].astype(F32) - mu_row) * rs_row
    st[0:1, :] = rs_row
    step_a(3)
    sum_d.third()
    sum_t.fourth()
    use(rem(z + NZ - 2, NZ), 2)
    use(rem(z + 2, NZ), 5)
    step_b(3)
    sum_d.fourth()
    sum_t.last()
    z4 = rem(z + 4, NZ)
    for way, to in ways:
        part = block(z4, own + way * (BLK // 2), BLK // 2)
        remote(part, part, a_ss.at[way, 3], a_rs.at[way, 3], dp=to).wait_recv()
    part = block(z4, crossing, LR)
    go(remote(part, part, c_ss.at[7], c_rs.at[7], dp=other))
    use(rem(z + NZ - 3, NZ), 3)
    use(rem(z + 3, NZ), 6)
    sum_d.last()
    ag[...] = dot_nt(cg[...], folded[...]).astype(BF)
    for way, to in ways:
        part = block(z4, shared + way * (BR // 2), BR // 2)
        remote(part, part, b_ss.at[4 + way * 4], b_rs.at[4 + way * 4], dp=to).wait_recv()
    use(z4, 7)
    qkv[...] = acc[...].astype(BF)

    dkv[...] = jnp.zeros_like(dkv)
    rate = HDIM**-0.5
    for h in range(2):
        cq = slice(h * HDIM, (h + 1) * HDIM)
        ck = slice(256 + h * HDIM, 256 + (h + 1) * HDIM)
        cv = slice(512 + h * HDIM, 512 + (h + 1) * HDIM)
        for r in range(4):
            here, n = slice(r * 128, (r + 1) * 128), 128 * (r + 1)
            qb, kb, vb = qkv[here, cq], qkv[0:n, ck], qkv[0:n, cv]
            s = dot_nt(qb, kb) * rate
            at_row = lax.broadcasted_iota(jnp.int32, (128, n), 0) + r * 128
            at_col = lax.broadcasted_iota(jnp.int32, (128, n), 1)
            s = jnp.where(at_col <= at_row, s, -1e30)
            e = jnp.exp(s - jnp.max(s, axis=1, keepdims=True))
            p = e * (1.0 / jnp.sum(e, axis=1, keepdims=True))
            pb = p.astype(BF)
            attn[here, cq] = dot(pb, vb).astype(BF)
            da = ag[here, cq]
            dpr = dot_nt(da, vb).astype(BF).astype(F32)
            ds = p * (dpr - jnp.sum(p * dpr, axis=1, keepdims=True))
            ds = (ds * rate).astype(BF)
            qg[here, cq] = dot(ds, kb).astype(BF)
            dkv[0:n, cq] += dot_tn(ds, qb)
            dkv[0:n, ck] += dot_tn(pb, da)
    qg[:, 256:768] = dkv[...].astype(BF)

    def order(i):
        odd = rem(i, 2)
        return rem(z + odd * (4 - (i + 1) // 2) + (1 - odd) * (4 + i // 2), NZ)

    base = LR * xl
    leaving, arriving = RB * (1 - xl), RB * xl

    def cross(i):
        return remote(con.at[order(i), rows(leaving, LR), :], xr.at[i], x_ss.at[i], x_rs.at[i], dp=other)

    def contribute(lo, hi):
        @pl.loop(lo, hi)
        def _(i):
            zd = order(i)

            @pl.loop(0, 5)
            def _(k):
                here = rows(k * 128, 128)
                con[zd, here, :] = dot(nt[zd, here, :], qg[...]).astype(BF)

            cross(i).start()

    def add_crossed(i):
        remote(xr.at[i], xr.at[i], x_ss.at[i], x_rs.at[i], dp=other).wait_recv()
        add_rows(con.at[order(i), rows(arriving, LR), :], xr.at[i], LR)

    def chunk(zd, n):
        c = (1 - xl) * (1 - n) + xl * n
        return con.at[zd, rows(base + c * CH, CH), :]

    def begin(way, to):
        go(remote(chunk(order(0), way), rb1.at[way], r1_ss.at[way], r1_rs.at[way], dp=to))

    def ring(s, n):
        for way, to in ways:
            i = 2 * s - 3 + way
            zd = order(i)
            if n == 1:
                add_crossed(i)
            if s == 2:
                if n == way:
                    remote(rb1.at[way], rb1.at[way], r1_ss.at[way], r1_rs.at[way], dp=to).wait_recv()
                    add_rows(chunk(zd, n), rb1.at[way], CH)
            else:
                slot = rb.at[way, s - 3, n]
                remote(slot, slot, r_ss.at[way, s - 3, n], r_rs.at[way, s - 3, n], dp=to).wait_recv()
                add_rows(chunk(zd, n), slot, CH)
            go(remote(chunk(zd, n), rb.at[way, s - 2, n], r_ss.at[way, s - 2, n], r_rs.at[way, s - 2, n], dp=to))

    def feature(i):
        return rem(i, 2) * NY + rem(y + 1 + i // 2, NY)

    def term(index):
        here = rows(index * BLK, BLK)
        out = dot(w[0, here, :], qgt[0:256, :])
        out = out + dot(w[1, here, :], qgt[256:512, :])
        return out + dot(w[2, here, :], qgt[512:768, :])

    def to_core(i):
        return remote(cs.at[i], cr.at[i], cs_ss.at[i], cs_rs.at[i], tensor=q * 2 + 1 - core)

    def to_y(i):
        there = (xh * NY + rem(y + 1 + i // 2, NY)) * 2 + core
        return remote(ys.at[i], yr.at[i], y_ss.at[i], y_rs.at[i], tensor=there)

    def other_blocks(lo, hi):
        @pl.loop(lo, hi)
        def _(i):
            cs[i] = term(feature(i) * 2 + 1 - core).astype(BF)
            to_core(i).start()

    def own_block(i):
        total = term(feature(i) * 2 + core)
        to_core(i).wait_recv()
        ys[i] = (total + cr[i].astype(F32)).astype(BF)

    contribute(0, 1)
    begin(0, up)
    contribute(1, 4)

    @pl.loop(0, 6)
    def _(i):
        here = pl.ds(pl.multiple_of(i * 128, 128), 128)
        qgt[here, :] = qg[:, here].T

    add_crossed(0)
    begin(1, down)
    contribute(4, NZ)
    other_blocks(0, NQ)
    ring(2, 0)
    ring(2, 1)

    @pl.loop(0, NQ - 2)
    def _(i):
        own_block(i)
        to_y(i).start()

    @pl.loop(NQ - 2, NQ)
    def _(i):
        own_block(i)

    ring(3, 0)
    cp_part[...] = dot(attn[...], folded[...]).astype(BF)
    sum_t2 = Sum("tensor", cp_part, code, t2)
    sum_t2.first()
    mx_part[...] = dot_tn(attn[...], cg[...]).astype(BF)
    sum_d2 = Sum("dp", mx_part, mixing, d2)
    sum_d2.first()
    ring(3, 1)
    sum_t2.second()
    sum_d2.second()
    ring(4, 0)
    sum_t2.third()

    for i in range(NQ - 2):
        remote(yr.at[i], yr.at[i], y_ss.at[i], y_rs.at[i], tensor=tensor).wait_recv()

    def y_sum(which):
        total = ys[6 + which].astype(F32)
        for k in range(3):
            total = total + yr[2 * k + which].astype(F32)
        return total

    xs[...] = y_sum(1 - xh).astype(BF)
    swap = remote(xs, xv, xh_ss, xh_rs, tensor=((1 - xh) * NY + y) * 2 + core)
    swap.start()
    ng[...] = y_sum(xh)
    sum_d2.third()
    ring(4, 1)
    sum_t2.across()
    swap.wait_recv()

    grad = ng[...] + xv[...].astype(F32)
    ng[...] = grad
    scaled = grad * gcol[mine_rows, 0:1]
    lt[tensor, 0:1, :] = jnp.sum(scaled, axis=0, keepdims=True)
    lt[tensor, 1:2, :] = jnp.sum(scaled * hat[...], axis=0, keepdims=True)
    slot = lt.at[tensor]
    for k in range(1, NR):
        go(remote(slot, slot, lt_ss.at[k], lt_rs.at[k], tensor=rem(tensor + k, NR)))

    def fold(v):
        v = v[:, 0:128] + v[:, 128:256] + v[:, 256:384] + v[:, 384:512]
        v = jnp.concatenate([v, jnp.zeros((64, 128), F32)], axis=0)
        return jnp.sum(v.T, axis=0, keepdims=True)

    gs[dp, 0:1, :] = fold(ng[...] * hat[...])
    gs[dp, 1:2, :] = fold(ng[...])
    slot = gs.at[dp]
    for k in range(1, NR):
        go(remote(slot, slot, gs_ss.at[k], gs_rs.at[k], dp=rem(dp + k, NR)))
    sum_d2.fourth()
    sum_t2.fourth()

    for k in range(1, NR):
        slot = lt.at[rem(tensor + NR - k, NR)]
        remote(slot, slot, lt_ss.at[k], lt_rs.at[k], tensor=tensor).wait_recv()
    sums = jnp.sum(lt[...], axis=0)
    lead, trail = sums[0:1, :] * (1.0 / D), sums[1:2, :] * (1.0 / D)
    scaled = ng[...] * gcol[mine_rows, 0:1]
    gi_t[...] = (got[...].astype(F32) + st[0:1, :] * (scaled - lead - hat[...] * trail)).astype(BF)

    def close(n):
        for way, to in ways:
            slot = rb.at[way, 2, n]
            remote(slot, slot, r_ss.at[way, 2, n], r_rs.at[way, 2, n], dp=to).wait_recv()
            add_rows(chunk(z, n), slot, CH)

    close(0)
    last = remote(con.at[z, rows(BLK - BR * xl, BR), :], mr, m_ss, m_rs, dp=other)
    last.start()
    sum_t2.last()
    ro_t[...] = (xt[mine_rows, :].astype(F32) + dot_nt(dect[...], code[...])).astype(BF)
    sum_d2.last()
    gow_t[...] = dot_nt(enc[...], mixing[...]) * (1.0 / NR)
    for k in range(1, NR):
        slot = gs.at[rem(dp + NR - k, NR)]
        remote(slot, slot, gs_ss.at[k], gs_rs.at[k], dp=dp).wait_recv()
    gb[...] = jnp.sum(gs[...], axis=0) * (1.0 / NR)
    add_crossed(7)
    close(1)
    last.wait_recv()
    add_rows(con.at[z, rows(LR + BR * xl, BR), :], mr, BR)
    for j in range(3):
        gq[j] = con[z, rows(BLK * xl, BLK), j * 256 : (j + 1) * 256].astype(F32) * (1.0 / NR)

    for total in (sum_t, sum_d, sum_t2, sum_d2):
        total.drain()
    last.wait_send()
    swap.wait_send()
    for copy in sent:
        copy.wait_send()

    @pl.loop(0, NZ)
    def _(i):
        cross(i).wait_send()
        to_core(i).wait_send()

    @pl.loop(0, NQ - 2)
    def _(i):
        to_y(i).wait_send()


def sublayer(*args):
    def shape(dims, kind):
        return jax.ShapeDtypeStruct(dims, kind)

    def v(kind, *dims):
        return pltpu.VMEM(dims, kind)

    one = pltpu.SemaphoreType.DMA
    whole = pl.BlockSpec(memory_space=pltpu.VMEM)
    far = pl.BlockSpec(memory_space=pl.ANY)
    scratch = [
        v(BF, SEQ, D), v(BF, 3, D, 256), v(BF, NZ, SLAB, SEQ), v(F32, SEQ, W3), v(F32, SEQ, 128), v(F32, SEQ, 128),
        v(BF, SLAB, SEQ), v(F32, SLAB, 128), v(F32, BLK, SEQ), v(F32, 8, SEQ),
        v(BF, SEQ, C), v(BF, 256, C), v(BF, SEQ, C), v(BF, 256, C), v(BF, SEQ, W3), v(BF, SEQ, 256),
        v(BF, SEQ, 256), v(BF, SEQ, W3), v(BF, W3, SEQ), v(F32, SEQ, 512),
        v(BF, NZ, SLAB, W3), v(BF, NZ, LR, W3), v(BF, 2, CH, W3), v(BF, 2, 3, 2, CH, W3), v(BF, BR, W3),
        v(BF, NQ, BLK, SEQ), v(BF, NQ, BLK, SEQ), v(BF, NQ, BLK, SEQ), v(BF, NQ - 2, BLK, SEQ),
        v(BF, BLK, SEQ), v(BF, BLK, SEQ), v(F32, BLK, SEQ), v(F32, NR, 8, SEQ), v(F32, NR, 8, 384),
        v(BF, SEQ, C), v(BF, 256, C), v(BF, SEQ, C), v(BF, 256, C),
        sum_buffers(SEQ, NY), sum_buffers(256, NZ), sum_buffers(SEQ, NY), sum_buffers(256, NZ),
        dma(2), one, dma(2, 4), dma(2, 4), dma(9), dma(9), dma(8), dma(8),
        dma(NZ), dma(NZ), dma(2), dma(2), dma(2, 3, 2), dma(2, 3, 2), one, one,
        dma(NQ), dma(NQ), dma(NQ), dma(NQ), one, one, dma(NR), dma(NR), dma(NR), dma(NR),
    ]
    return pl.pallas_call(
        kernel,
        out_shape=[
            shape((BLK, SEQ), BF),
            shape((BLK, SEQ), BF),
            shape((3, BLK, 256), F32),
            shape((BLK, 256), F32),
            shape((8, 384), F32),
        ],
        in_specs=[far, whole, whole, far, whole, whole, whole, whole],
        out_specs=[whole] * 5,
        scratch_shapes=scratch,
        compiler_params=pltpu.CompilerParams(
            collective_id=0, has_side_effects=True, vmem_limit_bytes=62 * 2**20
        ),
    )(*args)


def local(
    residual_in,
    layernorm_gain,
    layernorm_bias,
    qkv_weight,
    out_weight,
    encoder,
    decoder,
    grad_output,
):
    residual_out, grad_input, grad_qkv, grad_out_weight, sums = sublayer(
        residual_in,
        layernorm_gain[None, :],
        layernorm_bias[None, :],
        qkv_weight,
        out_weight.T,
        encoder,
        decoder.T,
        grad_output.T,
    )
    return residual_out.T, grad_input.T, grad_qkv, grad_out_weight.T, sums[0, :BLK], sums[1, :BLK]


def solution(mesh):
    in_specs = (
        P("dp", None),
        P(),
        P(),
        P(None, "dp", "tensor"),
        P("tensor", "dp"),
        P("dp", None),
        P(None, "tensor"),
        P("dp", "tensor"),
    )
    out_specs = (
        P("dp", "tensor"),
        P("dp", "tensor"),
        P(None, "dp", "tensor"),
        P("tensor", "dp"),
        P("tensor"),
        P("tensor"),
    )
    return jax.shard_map(local, mesh=mesh, in_specs=in_specs, out_specs=out_specs, check_vma=False)
```

```python
import functools

import jax
import jax.numpy as jnp
from jax import lax
from jax.experimental import pallas as pl
from jax.experimental.pallas import tpu as pltpu
from jax.sharding import PartitionSpec as P

HDIM = 128
EPS = 1e-05
MESH = pl.DeviceIdType.MESH
F32, BF = jnp.float32, jnp.bfloat16

NZ, NY, NQ, NR = 8, 4, 8, 16
SEQ, D, C, W3 = 512, 5120, 640, 768
BLK = 320
SLAB = 640
HB = BLK // 2


def rem(a, n):
    return lax.rem(a, n)


def rows(start, size):
    return pl.ds(pl.multiple_of(start, 16), size)


def dot(a, b):
    return lax.dot_general(a, b, (((1,), (0,)), ((), ())), preferred_element_type=F32)


def dot_nt(a, b):
    return lax.dot_general(a, b, (((1,), (1,)), ((), ())), preferred_element_type=F32)


def dot_tn(a, b):
    return lax.dot_general(a, b, (((0,), (0,)), ((), ())), preferred_element_type=F32)


def remote(src, dst, ssem, rsem, **device):
    return pltpu.make_async_remote_copy(
        src_ref=src, dst_ref=dst, send_sem=ssem, recv_sem=rsem, device_id=device, device_id_type=MESH
    )


def enter():
    barrier = pltpu.get_barrier_semaphore()
    for axis in ("dp", "tensor"):
        me = lax.axis_index(axis)
        for k in range(1, NR):
            pl.semaphore_signal(barrier, inc=1, device_id={axis: rem(me + k, NR)}, device_id_type=MESH)
    dp, tensor = lax.axis_index("dp"), lax.axis_index("tensor")
    across = {"dp": dp + 1 - 2 * rem(dp, 2), "tensor": tensor + 1 - 2 * rem(tensor, 2)}
    pl.semaphore_signal(barrier, inc=1, device_id=across, device_id_type=MESH)
    pl.semaphore_wait(barrier, 2 * (NR - 1) + 1)


class Sum:
    def __init__(self, axis, part, out, buffers):
        self.axis, self.part, self.out = axis, part, out
        self.got, self.half, self.ring, self.mid, self.mid_got, self.ssem, self.rsem = buffers
        index = lax.axis_index(axis)
        self.n = self.ring.shape[0]
        self.a = rem(index, 2)
        self.q = rem(index // 2, self.n)
        self.top = index // (2 * self.n)
        self.h = part.shape[0] // 2
        self.b = self.h // self.n
        self.sent = []

    def at(self, top, q, a):
        return {self.axis: (top * self.n + q) * 2 + a}

    def pair(self):
        return self.at(self.top, self.q, 1 - self.a)

    def peer(self, k):
        return self.at(self.top, rem(self.q + k, self.n), self.a)

    def over(self):
        return self.at(1 - self.top, self.q, self.a)

    def go(self, copy):
        copy.start()
        self.sent.append(copy)

    def first(self):
        src = self.part.at[rows((1 - self.a) * self.h, self.h), :]
        self.go(remote(src, self.got, self.ssem.at[0], self.rsem.at[0], **self.pair()))

    def second(self):
        remote(self.got, self.got, self.ssem.at[0], self.rsem.at[0], **self.pair()).wait_recv()
        mine = self.part[rows(self.a * self.h, self.h), :].astype(F32)
        self.half[...] = (mine + self.got[...].astype(F32)).astype(BF)
        for k in range(1, self.n):
            to = rem(self.q + k, self.n)
            src = self.half.at[rows(to * self.b, self.b), :]
            self.go(remote(src, self.ring.at[self.q], self.ssem.at[k], self.rsem.at[k], **self.peer(k)))

    def reduced(self):
        total = self.half[rows(self.q * self.b, self.b), :].astype(F32)
        for k in range(1, self.n):
            source = rem(self.q + self.n - k, self.n)
            slot = self.ring.at[source]
            remote(slot, slot, self.ssem.at[k], self.rsem.at[k], **self.peer(k)).wait_recv()
            total = total + self.ring[source].astype(F32)
        return total

    def spread(self, total):
        here = rows(self.a * self.h + self.q * self.b, self.b)
        self.out[here, :] = total.astype(BF)
        piece = self.out.at[here, :]
        for k in range(1, self.n):
            self.go(remote(piece, piece, self.ssem.at[7 + k], self.rsem.at[7 + k], **self.peer(k)))

    def third(self):
        if self.mid is None:
            self.spread(self.reduced())
        else:
            self.mid[...] = self.reduced().astype(BF)
            self.go(remote(self.mid, self.mid_got, self.ssem.at[16], self.rsem.at[16], **self.over()))

    def across(self):
        remote(self.mid, self.mid_got, self.ssem.at[16], self.rsem.at[16], **self.over()).wait_recv()
        self.spread(self.mid[...].astype(F32) + self.mid_got[...].astype(F32))

    def fourth(self):
        for k in range(1, self.n):
            source = rem(self.q + self.n - k, self.n)
            piece = self.out.at[rows(self.a * self.h + source * self.b, self.b), :]
            remote(piece, piece, self.ssem.at[7 + k], self.rsem.at[7 + k], **self.peer(k)).wait_recv()
        mine = self.out.at[rows(self.a * self.h, self.h), :]
        self.go(remote(mine, mine, self.ssem.at[15], self.rsem.at[15], **self.pair()))

    def last(self):
        other = self.out.at[rows((1 - self.a) * self.h, self.h), :]
        remote(other, other, self.ssem.at[15], self.rsem.at[15], **self.pair()).wait_recv()

    def drain(self):
        for copy in self.sent:
            copy.wait_send()


def dma(*shape):
    return pltpu.SemaphoreType.DMA(shape)


def sum_buffers(r, n):
    h = r // 2
    cut = pltpu.VMEM((h // n, C), BF)
    mids = [cut, cut] if n == NY else [None, None]
    return [pltpu.VMEM((h, C), BF), pltpu.VMEM((h, C), BF), pltpu.VMEM((n, h // n, C), BF)] + mids + [dma(17), dma(17)]


def add_rows(dst, src):
    @pl.loop(0, dst.shape[0] // 80)
    def _(i):
        here = rows(i * 80, 80)
        dst[here, :] = (dst[here, :].astype(F32) + src[here, :].astype(F32)).astype(BF)


def kernel(
    x_hbm, gain, bias, w_in, owt, enc, dect, got,
    ro_t, gi_t, gq, gow_t, gb,
    x, w, nb, no, acc, mu, rstd, xt, gcol, hat, st,
    cg_part, fo_part, cg, folded, ps, pr, qkvt, qkv, ag, attn, qg, qo, qgt, dkv,
    con, rb1, rb, po, px, cr, ys, yr, xs, xv, fs, fv, ng, lt, gs, cp_part, mx_part, code, mixing,
    t1, d1, t2, d2,
    x_sem, loc, a_ss, a_rs, n_ss, n_rs, f_ss, f_rs, p_ss, p_rs, q_ss, q_rs,
    r1_ss, r1_rs, r_ss, r_rs, cs_ss, cs_rs, y_ss, y_rs, xh_ss, xh_rs, fs_ss, fs_rs, lt_ss, lt_rs, gs_ss, gs_rs,
):
    dp, tensor = lax.axis_index("dp"), lax.axis_index("tensor")
    z, xl = dp // 2, rem(dp, 2)
    up, down = rem(z + 1, NZ) * 2 + xl, rem(z + NZ - 1, NZ) * 2 + xl
    other = z * 2 + 1 - xl
    core, q = rem(tensor, 2), tensor // 2
    xh, y = q // NY, rem(q, NY)
    sibling = q * 2 + 1 - core
    ways = ((0, up), (1, down))
    sent = []

    def go(copy):
        copy.start()
        sent.append(copy)

    x_copies = [
        pltpu.make_async_copy(x_hbm.at[pl.ds(i * 128, 128), :], x.at[pl.ds(i * 128, 128), :], x_sem.at[i])
        for i in range(4)
    ]
    for copy in x_copies:
        copy.start()
    enter()

    def block(j, zs, offset=0, size=BLK):
        return w.at[j, rows(zs * BLK + offset, size), :]

    mine = pltpu.make_async_copy(w_in, w.at[:, rows(z * BLK, BLK), :], loc)
    mine.start()

    def send_own(j):
        for way, to in ways:
            go(remote(w_in.at[j], block(j, z), a_ss.at[way, j, 0], a_rs.at[way, j, 0], dp=to))

    def relay(j, s):
        for way, to in ways:
            zs = rem(z + (NZ - s if way == 0 else s), NZ)
            if s < 4:
                part = block(j, zs)
                remote(part, part, a_ss.at[way, j, s - 1], a_rs.at[way, j, s - 1], dp=to).wait_recv()
                if s == 3:
                    part = block(j, zs, way * HB, HB)
                go(remote(part, part, a_ss.at[way, j, s], a_rs.at[way, j, s], dp=to))
            else:
                part = block(j, zs, way * HB, HB)
                remote(part, part, a_ss.at[way, j, 3], a_rs.at[way, j, 3], dp=to).wait_recv()

    send_own(0)
    send_own(1)
    fo_part[...] = dot_tn(owt[...], enc[...]).astype(BF)
    sum_d = Sum("dp", fo_part, folded, d1)
    sum_d.first()

    def slab_cols(zs):
        return pl.ds(pl.multiple_of(zs * SLAB, 128), SLAB)

    def near(i):
        odd = rem(i, 2)
        return rem(z + odd * ((i + 1) // 2) + (1 - odd) * (NZ - i // 2), NZ)

    def tokens(r):
        return pl.ds(r * 128, 128)

    def cross(k, r):
        zs = near(2 * k + core)
        src, dst = nb.at[1, zs, :, tokens(r)], no.at[zs, :, tokens(r)]
        return remote(src, dst, n_ss.at[k, r], n_rs.at[k, r], dp=other)

    def pass_on(k, r):
        part = no.at[near(2 * k + core), :, tokens(r)]
        return remote(part, part, f_ss.at[k, r], f_rs.at[k, r], tensor=sibling)

    def norm(r):
        x_copies[r].wait()
        xt[:, r * 128 : (r + 1) * 128] = x[r * 128 : (r + 1) * 128, slab_cols(q)].T

        @pl.loop(0, 8)
        def _(i):
            here = rows(r * 128 + i * 16, 16)
            v = x[here, :].astype(F32)
            mean = jnp.sum(v, axis=1, keepdims=True) * (1.0 / D)
            v = v - mean
            var = jnp.sum(v * v, axis=1, keepdims=True) * (1.0 / D)
            scale = lax.rsqrt(var + EPS)
            mu[here, :] = jnp.broadcast_to(mean, (16, 128))
            rstd[here, :] = jnp.broadcast_to(scale, (16, 128))
            x[here, :] = (v * scale * gain[...] + bias[...]).astype(BF)

        @pl.loop(0, NZ)
        def _(zs):
            v = x[r * 128 : (r + 1) * 128, slab_cols(zs)].T
            nb[xl, zs, :, r * 128 : (r + 1) * 128] = v[0:BLK]
            nb[1 - xl, zs, :, r * 128 : (r + 1) * 128] = v[BLK:SLAB]

        for k in range(4):
            go(cross(k, r))

    def forward_on(r):
        for k in range(4):
            cross(k, r).wait_recv()
            go(pass_on(k, r))

    def use(j, i, part):
        zs = near(i)
        here = slice(j * 256, (j + 1) * 256)
        source = nb.at[0, zs] if part == 0 else no.at[zs]
        acc[part, here, :] += dot_tn(block(j, zs)[...], source[...])

    def use_all(j, lo, hi, part):
        @pl.loop(lo, hi)
        def _(i):
            use(j, i, part)

    acc[...] = jnp.zeros_like(acc)
    norm(0)
    relay(0, 1)
    norm(1)
    relay(1, 1)
    sum_d.second()
    cg_part[...] = dot_tn(got[...], dect[...]).astype(BF)
    sum_t = Sum("tensor", cg_part, cg, t1)
    sum_t.first()
    relay(0, 2)
    norm(2)
    relay(1, 2)
    forward_on(0)
    norm(3)
    relay(0, 3)
    send_own(2)
    sum_t.second()
    forward_on(1)
    mine.wait()
    sum_d.third()
    use_all(0, 0, 5, 0)
    relay(1, 3)
    sum_t.third()
    use_all(1, 0, 5, 0)
    relay(2, 1)
    relay(0, 4)
    forward_on(2)
    sum_d.fourth()
    sum_t.across()
    use_all(0, 5, 8, 0)
    relay(2, 2)
    use_all(1, 5, 7, 0)
    relay(1, 4)
    use_all(1, 7, 8, 0)
    sum_t.fourth()
    forward_on(3)
    use_all(2, 0, 5, 0)
    relay(2, 3)
    for r in range(4):
        for k in range(4):
            part = no.at[near(2 * k + 1 - core), :, tokens(r)]
            remote(part, part, f_ss.at[k, r], f_rs.at[k, r], tensor=sibling).wait_recv()

    def partial(j):
        here = pl.ds(j * 256, 256)
        return remote(ps.at[here, :], pr.at[here, :], p_ss.at[j], p_rs.at[j], dp=other)

    def give(j):
        here = slice(j * 256, (j + 1) * 256)
        ps[here, :] = acc[1, here, :].astype(BF)
        go(partial(j))

    def take(j):
        here = slice(j * 256, (j + 1) * 256)
        partial(j).wait_recv()
        qkvt[here, :] = (acc[0, here, :] + pr[here, :].astype(F32)).astype(BF)
        qkv[:, here] = qkvt[here, :].T

    use_all(0, 0, 8, 1)
    give(0)
    relay(2, 4)
    use_all(1, 0, 8, 1)
    give(1)
    use_all(2, 0, 8, 1)
    give(2)
    sum_d.last()
    sum_t.last()
    use_all(2, 5, 8, 0)
    ag[...] = dot_nt(cg[...], folded[...]).astype(BF)
    mine_rows = rows(core * BLK, BLK)
    rs_row = rstd[...].T[0:1, :]
    hat[...] = (xt[mine_rows, :].astype(F32) - mu[...].T[0:1, :]) * rs_row
    st[0:1, :] = rs_row
    gcol[...] = jnp.broadcast_to(gain[0:1, slab_cols(q)], (128, SLAB)).T
    dkv[...] = jnp.zeros_like(dkv)
    for j in range(3):
        take(j)

    rate = HDIM**-0.5
    for h in range(2):
        cq = slice(h * HDIM, (h + 1) * HDIM)
        ck = slice(256 + h * HDIM, 256 + (h + 1) * HDIM)
        cv = slice(512 + h * HDIM, 512 + (h + 1) * HDIM)
        for r in range(4):
            here, n = slice(r * 128, (r + 1) * 128), 128 * (r + 1)
            qb, kb, vb = qkv[here, cq], qkv[0:n, ck], qkv[0:n, cv]
            s = dot_nt(qb, kb) * rate
            at_row = lax.broadcasted_iota(jnp.int32, (128, n), 0) + r * 128
            at_col = lax.broadcasted_iota(jnp.int32, (128, n), 1)
            s = jnp.where(at_col <= at_row, s, -1e30)
            e = jnp.exp(s - jnp.max(s, axis=1, keepdims=True))
            p = e * (1.0 / jnp.sum(e, axis=1, keepdims=True))
            pb = p.astype(BF)
            attn[here, cq] = dot(pb, vb).astype(BF)
            da = ag[here, cq]
            dpr = dot_nt(da, vb).astype(BF).astype(F32)
            ds = p * (dpr - jnp.sum(p * dpr, axis=1, keepdims=True))
            ds = (ds * rate).astype(BF)
            qg[here, cq] = dot(ds, kb).astype(BF)
            dkv[0:n, cq] += dot_tn(ds, qb)
            dkv[0:n, ck] += dot_tn(pb, da)
    qg[:, 256:768] = dkv[...].astype(BF)

    def swap_grad(j):
        here = pl.ds(j * 256, 256)
        return remote(qg.at[:, here], qo.at[:, here], q_ss.at[j], q_rs.at[j], dp=other)

    for j in (2, 0, 1):
        go(swap_grad(j))

    def contribute(zs):
        for j in range(3):
            con[zs, j] = dot(nb[0, zs], qg[:, j * 256 : (j + 1) * 256]).astype(BF)

    @pl.loop(0, NZ)
    def _(zs):
        contribute(zs)

    def turn(part, source):
        @pl.loop(0, 6)
        def _(i):
            here = pl.ds(pl.multiple_of(i * 128, 128), 128)
            qgt[part, here, :] = source[:, here].T

    turn(0, qg)

    def term(zs, part):
        here = rows(zs * BLK, BLK)
        out = dot(w[0, here, :], qgt[part, 0:256, :])
        out = out + dot(w[1, here, :], qgt[part, 256:512, :])
        return out + dot(w[2, here, :], qgt[part, 512:768, :])

    def feature(i):
        return rem(i, 2) * NY + rem(y + 1 + i // 2, NY)

    keeps = core == xl

    def to_core(buffer, i):
        return remote(buffer.at[i], cr.at[i], cs_ss.at[i], cs_rs.at[i], tensor=sibling)

    def to_y(i):
        there = (xh * NY + rem(y + 1 + i // 2, NY)) * 2 + core
        return remote(ys.at[i], yr.at[i], y_ss.at[i], y_rs.at[i], tensor=there)

    def parts(buffer, part):
        @pl.loop(0, NQ)
        def _(i):
            buffer[i] = term(feature(i), part).astype(BF)

    def pass_core(buffer):
        @pl.loop(0, NQ)
        def _(i):
            to_core(buffer, i).start()

    def join(buffer):
        def one(i):
            to_core(buffer, i).wait_recv()
            ys[i] = (buffer[i].astype(F32) + cr[i].astype(F32)).astype(BF)

        @pl.loop(0, NQ - 2)
        def _(i):
            one(i)
            to_y(i).start()

        @pl.loop(NQ - 2, NQ)
        def _(i):
            one(i)

    parts(po, 0)

    @pl.when(jnp.logical_not(keeps))
    def _():
        pass_core(po)

    def complete(j):
        swap_grad(j).wait_recv()

        @pl.loop(0, NZ)
        def _(zs):
            here = slice(j * 256, (j + 1) * 256)
            con[zs, j] = (con[zs, j].astype(F32) + dot(no[zs], qo[:, here])).astype(BF)

    def ring(j, s):
        for way, to in ways:
            if s == 1:
                half = con.at[rem(z + 4, NZ), j, pl.ds(way * HB, HB), :]
                go(remote(half, rb1.at[j, way], r1_ss.at[j, way], r1_rs.at[j, way], dp=to))
                continue
            zs = rem(z + (5 - s if way == 0 else NZ + s - 5), NZ)
            if s == 2:
                remote(rb1.at[j, way], rb1.at[j, way], r1_ss.at[j, way], r1_rs.at[j, way], dp=to).wait_recv()
                add_rows(con.at[zs, j, pl.ds(way * HB, HB), :], rb1.at[j, way])
            else:
                slot = rb.at[j, way, s - 3]
                remote(slot, slot, r_ss.at[j, way, s - 3], r_rs.at[j, way, s - 3], dp=to).wait_recv()
                add_rows(con.at[zs, j], slot)
            if s < 5:
                slot = rb.at[j, way, s - 2]
                go(remote(con.at[zs, j], slot, r_ss.at[j, way, s - 2], r_rs.at[j, way, s - 2], dp=to))
        if s == 5:
            gq[j] = con[z, j].astype(F32) * (1.0 / NR)

    complete(2)
    ring(2, 1)
    cp_part[...] = dot(attn[...], folded[...]).astype(BF)
    sum_t2 = Sum("tensor", cp_part, code, t2)
    sum_t2.first()
    mx_part[...] = dot_tn(attn[...], cg[...]).astype(BF)
    sum_d2 = Sum("dp", mx_part, mixing, d2)
    sum_d2.first()
    ring(2, 2)
    complete(0)
    ring(0, 1)

    @pl.when(keeps)
    def _():
        join(po)

    ring(2, 3)
    ring(0, 2)
    complete(1)
    ring(1, 1)
    turn(1, qo)
    parts(px, 1)

    @pl.when(keeps)
    def _():
        pass_core(px)

    ring(2, 4)
    ring(0, 3)
    ring(1, 2)

    @pl.when(jnp.logical_not(keeps))
    def _():
        join(px)

    sum_t2.second()
    sum_d2.second()
    ring(2, 5)
    ring(0, 4)
    ring(1, 3)
    sum_t2.third()

    for i in range(NQ - 2):
        remote(yr.at[i], yr.at[i], y_ss.at[i], y_rs.at[i], tensor=tensor).wait_recv()

    def y_sum(which):
        total = ys[6 + which].astype(F32)
        for k in range(3):
            total = total + yr[2 * k + which].astype(F32)
        return total

    xs[...] = y_sum(1 - xh).astype(BF)
    swap = remote(xs, xv, xh_ss, xh_rs, tensor=((1 - xh) * NY + y) * 2 + core)
    swap.start()
    ng[...] = y_sum(xh)
    sum_d2.third()
    ring(0, 5)
    ring(1, 4)
    sum_t2.across()
    swap.wait_recv()
    ng[...] = ng[...] + xv[...].astype(F32)
    home = remote(fs, fv, fs_ss, fs_rs, dp=other, tensor=sibling)

    @pl.when(jnp.logical_not(keeps))
    def _():
        fs[...] = ng[...].astype(BF)
        home.start()
        home.wait_recv()
        ng[...] = fv[...].astype(F32)

    grad = ng[...]
    scaled = grad * gcol[mine_rows, 0:1]
    lt[tensor, 0:1, :] = jnp.sum(scaled, axis=0, keepdims=True)
    lt[tensor, 1:2, :] = jnp.sum(scaled * hat[...], axis=0, keepdims=True)
    slot = lt.at[tensor]
    for k in range(1, NR):
        go(remote(slot, slot, lt_ss.at[k], lt_rs.at[k], tensor=rem(tensor + k, NR)))

    def fold(v):
        v = v[:, 0:128] + v[:, 128:256] + v[:, 256:384] + v[:, 384:512]
        v = jnp.concatenate([v, jnp.zeros((64, 128), F32)], axis=0)
        return jnp.sum(v.T, axis=0, keepdims=True)

    gs[dp, 0:1, :] = fold(ng[...] * hat[...])
    gs[dp, 1:2, :] = fold(ng[...])
    slot = gs.at[dp]
    for k in range(1, NR):
        go(remote(slot, slot, gs_ss.at[k], gs_rs.at[k], dp=rem(dp + k, NR)))
    sum_d2.fourth()
    sum_t2.fourth()
    ring(1, 5)
    sum_t2.last()
    ro_t[...] = (xt[mine_rows, :].astype(F32) + dot_nt(dect[...], code[...])).astype(BF)

    for k in range(1, NR):
        slot = lt.at[rem(tensor + NR - k, NR)]
        remote(slot, slot, lt_ss.at[k], lt_rs.at[k], tensor=tensor).wait_recv()
    sums = jnp.sum(lt[...], axis=0)
    lead, trail = sums[0:1, :] * (1.0 / D), sums[1:2, :] * (1.0 / D)
    scaled = ng[...] * gcol[mine_rows, 0:1]
    gi_t[...] = (got[...].astype(F32) + st[0:1, :] * (scaled - lead - hat[...] * trail)).astype(BF)
    sum_d2.last()
    gow_t[...] = dot_nt(enc[...], mixing[...]) * (1.0 / NR)
    for k in range(1, NR):
        slot = gs.at[rem(dp + NR - k, NR)]
        remote(slot, slot, gs_ss.at[k], gs_rs.at[k], dp=dp).wait_recv()
    gb[...] = jnp.sum(gs[...], axis=0) * (1.0 / NR)

    for total in (sum_t, sum_d, sum_t2, sum_d2):
        total.drain()
    swap.wait_send()
    for copy in sent:
        copy.wait_send()

    @pl.when(jnp.logical_not(keeps))
    def _():
        home.wait_send()

    @pl.loop(0, NQ)
    def _(i):
        to_core(po, i).wait_send()

    @pl.loop(0, NQ - 2)
    def _(i):
        to_y(i).wait_send()


def sublayer(*args):
    def shape(dims, kind):
        return jax.ShapeDtypeStruct(dims, kind)

    def v(kind, *dims):
        return pltpu.VMEM(dims, kind)

    one = pltpu.SemaphoreType.DMA
    whole = pl.BlockSpec(memory_space=pltpu.VMEM)
    far = pl.BlockSpec(memory_space=pl.ANY)
    scratch = [
        v(BF, SEQ, D), v(BF, 3, NZ * BLK, 256), v(BF, 2, NZ, BLK, SEQ), v(BF, NZ, BLK, SEQ), v(F32, 2, W3, SEQ),
        v(F32, SEQ, 128), v(F32, SEQ, 128), v(BF, SLAB, SEQ), v(F32, SLAB, 128), v(F32, BLK, SEQ), v(F32, 8, SEQ),
        v(BF, SEQ, C), v(BF, 256, C), v(BF, SEQ, C), v(BF, 256, C), v(BF, W3, SEQ), v(BF, W3, SEQ), v(BF, W3, SEQ),
        v(BF, SEQ, W3), v(BF, SEQ, 256), v(BF, SEQ, 256), v(BF, SEQ, W3), v(BF, SEQ, W3), v(BF, 2, W3, SEQ),
        v(F32, SEQ, 512),
        v(BF, NZ, 3, BLK, 256), v(BF, 3, 2, HB, 256), v(BF, 3, 2, 3, BLK, 256),
        v(BF, NQ, BLK, SEQ), v(BF, NQ, BLK, SEQ), v(BF, NQ, BLK, SEQ), v(BF, NQ, BLK, SEQ), v(BF, NQ - 2, BLK, SEQ),
        v(BF, BLK, SEQ), v(BF, BLK, SEQ), v(BF, BLK, SEQ), v(BF, BLK, SEQ), v(F32, BLK, SEQ),
        v(F32, NR, 8, SEQ), v(F32, NR, 8, 384), v(BF, SEQ, C), v(BF, 256, C), v(BF, SEQ, C), v(BF, 256, C),
        sum_buffers(SEQ, NY), sum_buffers(256, NZ), sum_buffers(SEQ, NY), sum_buffers(256, NZ),
        dma(4), one, dma(2, 3, 4), dma(2, 3, 4), dma(4, 4), dma(4, 4), dma(4, 4), dma(4, 4), dma(3), dma(3), dma(3), dma(3),
        dma(3, 2), dma(3, 2), dma(3, 2, 3), dma(3, 2, 3), dma(NQ), dma(NQ), dma(NQ), dma(NQ), one, one, one, one,
        dma(NR), dma(NR), dma(NR), dma(NR),
    ]
    return pl.pallas_call(
        kernel,
        out_shape=[
            shape((BLK, SEQ), BF),
            shape((BLK, SEQ), BF),
            shape((3, BLK, 256), F32),
            shape((BLK, 256), F32),
            shape((8, 384), F32),
        ],
        in_specs=[far, whole, whole, far, whole, whole, whole, whole],
        out_specs=[whole] * 5,
        scratch_shapes=scratch,
        compiler_params=pltpu.CompilerParams(
            collective_id=0, has_side_effects=True, vmem_limit_bytes=62 * 2**20
        ),
    )(*args)


def local(
    residual_in,
    layernorm_gain,
    layernorm_bias,
    qkv_weight,
    out_weight,
    encoder,
    decoder,
    grad_output,
):
    residual_out, grad_input, grad_qkv, grad_out_weight, sums = sublayer(
        residual_in,
        layernorm_gain[None, :],
        layernorm_bias[None, :],
        qkv_weight,
        out_weight.T,
        encoder,
        decoder.T,
        grad_output.T,
    )
    return residual_out.T, grad_input.T, grad_qkv, grad_out_weight.T, sums[0, :BLK], sums[1, :BLK]


def solution(mesh):
    in_specs = (
        P("dp", None),
        P(),
        P(),
        P(None, "dp", "tensor"),
        P("tensor", "dp"),
        P("dp", None),
        P(None, "tensor"),
        P("dp", "tensor"),
    )
    out_specs = (
        P("dp", "tensor"),
        P("dp", "tensor"),
        P(None, "dp", "tensor"),
        P("tensor", "dp"),
        P("tensor"),
        P("tensor"),
    )
    return jax.shard_map(local, mesh=mesh, in_specs=in_specs, out_specs=out_specs, check_vma=False)
```

```python
import functools
from collections import deque

import jax
import jax.numpy as jnp
from jax import lax
from jax.experimental import pallas as pl
from jax.experimental.pallas import tpu as pltpu
from jax.sharding import PartitionSpec as P

HDIM = 128
EPS = 1e-05
MESH = pl.DeviceIdType.MESH
F32, BF = jnp.float32, jnp.bfloat16

NZ, NY, NQ, NR = 8, 4, 8, 16
SEQ, D, C, W3 = 512, 5120, 640, 768
BLK = 320
SLAB = 640
HB = BLK // 2


def rem(a, n):
    return lax.rem(a, n)


def rows(start, size):
    return pl.ds(pl.multiple_of(start, 16), size)


def dot(a, b):
    return lax.dot_general(a, b, (((1,), (0,)), ((), ())), preferred_element_type=F32)


def dot_nt(a, b):
    return lax.dot_general(a, b, (((1,), (1,)), ((), ())), preferred_element_type=F32)


def dot_tn(a, b):
    return lax.dot_general(a, b, (((0,), (0,)), ((), ())), preferred_element_type=F32)


def remote(src, dst, ssem, rsem, **device):
    return pltpu.make_async_remote_copy(
        src_ref=src, dst_ref=dst, send_sem=ssem, recv_sem=rsem, device_id=device, device_id_type=MESH
    )


def enter():
    barrier = pltpu.get_barrier_semaphore()
    for axis in ("dp", "tensor"):
        me = lax.axis_index(axis)
        for k in range(1, NR):
            pl.semaphore_signal(barrier, inc=1, device_id={axis: rem(me + k, NR)}, device_id_type=MESH)
    dp, tensor = lax.axis_index("dp"), lax.axis_index("tensor")
    across = {"dp": dp + 1 - 2 * rem(dp, 2), "tensor": tensor + 1 - 2 * rem(tensor, 2)}
    pl.semaphore_signal(barrier, inc=1, device_id=across, device_id_type=MESH)
    pl.semaphore_wait(barrier, 2 * (NR - 1) + 1)


class Sum:
    def __init__(self, axis, part, out, buffers):
        self.axis, self.part, self.out = axis, part, out
        self.got, self.half, self.ring, self.mid, self.mid_got, self.ssem, self.rsem = buffers
        index = lax.axis_index(axis)
        self.n = self.ring.shape[0]
        self.a = rem(index, 2)
        self.q = rem(index // 2, self.n)
        self.top = index // (2 * self.n)
        self.h = part.shape[0] // 2
        self.b = self.h // self.n
        self.sent = []

    def at(self, top, q, a):
        return {self.axis: (top * self.n + q) * 2 + a}

    def pair(self):
        return self.at(self.top, self.q, 1 - self.a)

    def peer(self, k):
        return self.at(self.top, rem(self.q + k, self.n), self.a)

    def over(self):
        return self.at(1 - self.top, self.q, self.a)

    def go(self, copy):
        copy.start()
        self.sent.append(copy)

    def first(self):
        src = self.part.at[rows((1 - self.a) * self.h, self.h), :]
        self.go(remote(src, self.got, self.ssem.at[0], self.rsem.at[0], **self.pair()))

    def second(self):
        remote(self.got, self.got, self.ssem.at[0], self.rsem.at[0], **self.pair()).wait_recv()
        mine = self.part[rows(self.a * self.h, self.h), :].astype(F32)
        self.half[...] = (mine + self.got[...].astype(F32)).astype(BF)
        for k in range(1, self.n):
            to = rem(self.q + k, self.n)
            src = self.half.at[rows(to * self.b, self.b), :]
            self.go(remote(src, self.ring.at[self.q], self.ssem.at[k], self.rsem.at[k], **self.peer(k)))

    def reduced(self):
        total = self.half[rows(self.q * self.b, self.b), :].astype(F32)
        for k in range(1, self.n):
            source = rem(self.q + self.n - k, self.n)
            slot = self.ring.at[source]
            remote(slot, slot, self.ssem.at[k], self.rsem.at[k], **self.peer(k)).wait_recv()
            total = total + self.ring[source].astype(F32)
        return total

    def spread(self, total):
        here = rows(self.a * self.h + self.q * self.b, self.b)
        self.out[here, :] = total.astype(BF)
        piece = self.out.at[here, :]
        for k in range(1, self.n):
            self.go(remote(piece, piece, self.ssem.at[7 + k], self.rsem.at[7 + k], **self.peer(k)))

    def third(self):
        if self.mid is None:
            self.spread(self.reduced())
        else:
            self.mid[...] = self.reduced().astype(BF)
            self.go(remote(self.mid, self.mid_got, self.ssem.at[16], self.rsem.at[16], **self.over()))

    def across(self):
        remote(self.mid, self.mid_got, self.ssem.at[16], self.rsem.at[16], **self.over()).wait_recv()
        self.spread(self.mid[...].astype(F32) + self.mid_got[...].astype(F32))

    def fourth(self):
        for k in range(1, self.n):
            source = rem(self.q + self.n - k, self.n)
            piece = self.out.at[rows(self.a * self.h + source * self.b, self.b), :]
            remote(piece, piece, self.ssem.at[7 + k], self.rsem.at[7 + k], **self.peer(k)).wait_recv()
        mine = self.out.at[rows(self.a * self.h, self.h), :]
        self.go(remote(mine, mine, self.ssem.at[15], self.rsem.at[15], **self.pair()))

    def last(self):
        other = self.out.at[rows((1 - self.a) * self.h, self.h), :]
        remote(other, other, self.ssem.at[15], self.rsem.at[15], **self.pair()).wait_recv()

    def drain(self):
        for copy in self.sent:
            copy.wait_send()


def dma(*shape):
    return pltpu.SemaphoreType.DMA(shape)


def sum_buffers(r, n):
    h = r // 2
    cut = pltpu.VMEM((h // n, C), BF)
    mids = [cut, cut] if n == NY else [None, None]
    return [pltpu.VMEM((h, C), BF), pltpu.VMEM((h, C), BF), pltpu.VMEM((n, h // n, C), BF)] + mids + [dma(17), dma(17)]


def add_rows(dst, src):
    @pl.loop(0, dst.shape[0] // 80)
    def _(i):
        here = rows(i * 80, 80)
        dst[here, :] = (dst[here, :].astype(F32) + src[here, :].astype(F32)).astype(BF)


def kernel(
    x_hbm, gain, bias, w_in, owt, enc, dect, got,
    ro_t, gi_t, gq, gow_t, gb,
    x, w, nb, no, acc, mu, rstd, xt, gcol, hat, st,
    cg_part, fo_part, cg, folded, ps, pr, qkvt, qkv, ag, attn, qg, qo, qgt, dkv,
    con, rb1, rb, po, px, cr, ys, yh, yr, xs, xv, fs, fv, ng, lt, gs, cp_part, mx_part, code, mixing,
    t1, d1, t2, d2,
    x_sem, loc, a_ss, a_rs, n_ss, n_rs, f_ss, f_rs, p_ss, p_rs, q_ss, q_rs,
    r1_ss, r1_rs, r_ss, r_rs, cs_ss, cs_rs, yh_ss, yh_rs, y_ss, y_rs, xh_ss, xh_rs, fs_ss, fs_rs, lt_ss, lt_rs, gs_ss, gs_rs,
):
    dp, tensor = lax.axis_index("dp"), lax.axis_index("tensor")
    z, xl = dp // 2, rem(dp, 2)
    up, down = rem(z + 1, NZ) * 2 + xl, rem(z + NZ - 1, NZ) * 2 + xl
    other = z * 2 + 1 - xl
    core, q = rem(tensor, 2), tensor // 2
    xh, y = q // NY, rem(q, NY)
    sibling = q * 2 + 1 - core
    ways = ((0, up), (1, down))
    sent = []

    def go(copy):
        copy.start()
        sent.append(copy)

    x_copies = [
        pltpu.make_async_copy(x_hbm.at[pl.ds(i * 128, 128), :], x.at[pl.ds(i * 128, 128), :], x_sem.at[i])
        for i in range(4)
    ]
    for copy in x_copies:
        copy.start()
    enter()

    def block(j, zs, offset=0, size=BLK):
        return w.at[j, rows(zs * BLK + offset, size), :]

    mine = pltpu.make_async_copy(w_in, w.at[:, rows(z * BLK, BLK), :], loc)
    mine.start()

    def send_own(j):
        for way, to in ways:
            go(remote(w_in.at[j], block(j, z), a_ss.at[way, j, 0], a_rs.at[way, j, 0], dp=to))

    def relay(j, s):
        for way, to in ways:
            zs = rem(z + (NZ - s if way == 0 else s), NZ)
            if s < 4:
                part = block(j, zs)
                remote(part, part, a_ss.at[way, j, s - 1], a_rs.at[way, j, s - 1], dp=to).wait_recv()
                if s == 3:
                    part = block(j, zs, way * HB, HB)
                go(remote(part, part, a_ss.at[way, j, s], a_rs.at[way, j, s], dp=to))
            else:
                part = block(j, zs, way * HB, HB)
                remote(part, part, a_ss.at[way, j, 3], a_rs.at[way, j, 3], dp=to).wait_recv()

    send_own(0)
    send_own(1)
    sum_d = Sum("dp", fo_part, folded, d1)
    sum_t = Sum("tensor", cg_part, cg, t1)

    def start_folded():
        fo_part[...] = dot_tn(owt[...], enc[...]).astype(BF)
        sum_d.first()

    def start_code_grad():
        cg_part[...] = dot_tn(got[...], dect[...]).astype(BF)
        sum_t.first()

    def slab_cols(zs):
        return pl.ds(pl.multiple_of(zs * SLAB, 128), SLAB)

    def near(i):
        odd = rem(i, 2)
        return rem(z + odd * ((i + 1) // 2) + (1 - odd) * (NZ - i // 2), NZ)

    def tokens(r):
        return pl.ds(r * 128, 128)

    def cross(k, r):
        zs = near(2 * k + core)
        src, dst = nb.at[1, zs, :, tokens(r)], no.at[zs, :, tokens(r)]
        return remote(src, dst, n_ss.at[k, r], n_rs.at[k, r], dp=other)

    def pass_on(k, r):
        part = no.at[near(2 * k + core), :, tokens(r)]
        return remote(part, part, f_ss.at[k, r], f_rs.at[k, r], tensor=sibling)

    def norm(r, lo, hi):
        if lo == 0:
            x_copies[r].wait()
            xt[:, r * 128 : (r + 1) * 128] = x[r * 128 : (r + 1) * 128, slab_cols(q)].T

        @pl.loop(lo, hi)
        def _(i):
            here = rows(r * 128 + i * 16, 16)
            v = x[here, :].astype(F32)
            mean = jnp.sum(v, axis=1, keepdims=True) * (1.0 / D)
            v = v - mean
            var = jnp.sum(v * v, axis=1, keepdims=True) * (1.0 / D)
            scale = lax.rsqrt(var + EPS)
            mu[here, :] = jnp.broadcast_to(mean, (16, 128))
            rstd[here, :] = jnp.broadcast_to(scale, (16, 128))
            x[here, :] = (v * scale * gain[...] + bias[...]).astype(BF)

    def spread(r):
        @pl.loop(0, NZ)
        def _(zs):
            v = x[r * 128 : (r + 1) * 128, slab_cols(zs)].T
            nb[xl, zs, :, r * 128 : (r + 1) * 128] = v[0:BLK]
            nb[1 - xl, zs, :, r * 128 : (r + 1) * 128] = v[BLK:SLAB]

        for k in range(4):
            go(cross(k, r))

    def forward_on(r):
        for k in range(4):
            cross(k, r).wait_recv()
            go(pass_on(k, r))

    def use(j, i, part):
        zs = near(i)
        here = slice(j * 256, (j + 1) * 256)
        source = nb.at[0, zs] if part == 0 else no.at[zs]
        acc[part, here, :] += dot_tn(block(j, zs)[...], source[...])

    def use_all(j, lo, hi, part):
        @pl.loop(lo, hi)
        def _(i):
            use(j, i, part)

    def partial(j):
        here = pl.ds(j * 256, 256)
        return remote(ps.at[here, :], pr.at[here, :], p_ss.at[j], p_rs.at[j], dp=other)

    def give(j):
        here = slice(j * 256, (j + 1) * 256)
        ps[here, :] = acc[1, here, :].astype(BF)
        go(partial(j))

    def take(j):
        here = slice(j * 256, (j + 1) * 256)
        partial(j).wait_recv()
        qkvt[here, :] = (acc[0, here, :] + pr[here, :].astype(F32)).astype(BF)
        qkv[:, here] = qkvt[here, :].T

    def collect():
        for r in range(4):
            for k in range(4):
                part = no.at[near(2 * k + 1 - core), :, tokens(r)]
                remote(part, part, f_ss.at[k, r], f_rs.at[k, r], tensor=sibling).wait_recv()

    work = deque()

    def add(cost, f, *args):
        work.append((cost, functools.partial(f, *args)))

    def clear():
        acc[...] = jnp.zeros_like(acc)

    def relay_use(j, s):
        relay(j, s)
        lo, hi = (7, 8) if s == 4 else (2 * s - 1, 2 * s + 1)
        add(0.33 * (hi - lo), use_all, j, lo, hi, 0)

    def own_use():
        mine.wait()
        for j in range(3):
            add(0.33, use_all, j, 0, 1, 0)

    def far_use(j):
        use_all(j, 0, 8, 1)
        give(j)

    add(1.2, start_folded)
    for r in range(4):
        add(1.3, norm, r, 0, 4)
        add(1.3, norm, r, 4, 8)
        add(1.1, spread, r)
        if r == 0:
            add(0.8, clear)
        if r == 2:
            add(1.5, start_code_grad)
    events = [
        (5.0, relay_use, 0, 1),
        (7.0, sum_d.second),
        (8.3, relay_use, 1, 1),
        (11.6, relay_use, 0, 2),
        (13.5, forward_on, 0),
        (16.5, relay_use, 1, 2),
        (16.6, send_own, 2),
        (19.0, sum_d.third),
        (20.0, relay_use, 0, 3),
        (20.5, forward_on, 1),
        (21.0, own_use),
        (21.5, sum_t.second),
        (24.0, relay_use, 2, 1),
        (25.5, sum_t.third),
        (28.0, relay_use, 1, 3),
        (28.0, forward_on, 2),
        (29.5, sum_t.across),
        (31.0, relay_use, 0, 4),
        (31.5, sum_d.fourth),
        (34.0, relay_use, 2, 2),
        (34.2, sum_t.fourth),
        (35.0, forward_on, 3),
        (36.0, relay_use, 1, 4),
        (37.5, collect),
        (38.0, far_use, 0),
        (39.5, relay_use, 2, 3),
        (40.0, far_use, 1),
        (43.0, relay_use, 2, 4),
        (43.0, far_use, 2),
    ]
    now = 0.0
    for when, f, *args in events:
        while work and now + work[0][0] <= when + 0.3:
            cost, g = work.popleft()
            g()
            now += cost
        f(*args)
        now = max(now, when) + (2.8 if f is far_use else 0.2)
    while work:
        work.popleft()[1]()
    sum_d.last()
    sum_t.last()
    ag[...] = dot_nt(cg[...], folded[...]).astype(BF)
    mine_rows = rows(core * BLK, BLK)
    rs_row = rstd[...].T[0:1, :]
    hat[...] = (xt[mine_rows, :].astype(F32) - mu[...].T[0:1, :]) * rs_row
    st[0:1, :] = rs_row
    gcol[...] = jnp.broadcast_to(gain[0:1, slab_cols(q)], (128, SLAB)).T
    dkv[...] = jnp.zeros_like(dkv)
    for j in range(3):
        take(j)

    rate = HDIM**-0.5
    for h in range(2):
        cq = slice(h * HDIM, (h + 1) * HDIM)
        ck = slice(256 + h * HDIM, 256 + (h + 1) * HDIM)
        cv = slice(512 + h * HDIM, 512 + (h + 1) * HDIM)
        for r in range(4):
            here, n = slice(r * 128, (r + 1) * 128), 128 * (r + 1)
            qb, kb, vb = qkv[here, cq], qkv[0:n, ck], qkv[0:n, cv]
            s = dot_nt(qb, kb) * rate
            at_row = lax.broadcasted_iota(jnp.int32, (128, n), 0) + r * 128
            at_col = lax.broadcasted_iota(jnp.int32, (128, n), 1)
            s = jnp.where(at_col <= at_row, s, -1e30)
            e = jnp.exp(s - jnp.max(s, axis=1, keepdims=True))
            p = e * (1.0 / jnp.sum(e, axis=1, keepdims=True))
            pb = p.astype(BF)
            attn[here, cq] = dot(pb, vb).astype(BF)
            da = ag[here, cq]
            dpr = dot_nt(da, vb).astype(BF).astype(F32)
            ds = p * (dpr - jnp.sum(p * dpr, axis=1, keepdims=True))
            ds = (ds * rate).astype(BF)
            qg[here, cq] = dot(ds, kb).astype(BF)
            dkv[0:n, cq] += dot_tn(ds, qb)
            dkv[0:n, ck] += dot_tn(pb, da)
    qg[:, 256:768] = dkv[...].astype(BF)

    def swap_grad(j):
        here = pl.ds(j * 256, 256)
        return remote(qg.at[:, here], qo.at[:, here], q_ss.at[j], q_rs.at[j], dp=other)

    for j in (2, 0, 1):
        go(swap_grad(j))

    def contribute(j):
        @pl.loop(0, NZ)
        def _(zs):
            con[zs, j] = dot(nb[0, zs], qg[:, j * 256 : (j + 1) * 256]).astype(BF)

    def turn(part, source):
        @pl.loop(0, 6)
        def _(i):
            here = pl.ds(pl.multiple_of(i * 128, 128), 128)
            qgt[part, here, :] = source[:, here].T

    def term(zs, part):
        here = rows(zs * BLK, BLK)
        out = dot(w[0, here, :], qgt[part, 0:256, :])
        out = out + dot(w[1, here, :], qgt[part, 256:512, :])
        return out + dot(w[2, here, :], qgt[part, 512:768, :])

    def feature(i):
        return i % 2 * NY + rem(y + (2, 1, 3, 0)[i // 2], NY)

    keeps = core == xl

    def to_core(buffer, i):
        return remote(buffer.at[i], cr.at[i], cs_ss.at[i], cs_rs.at[i], tensor=sibling)

    def y_device(way):
        return (xh * NY + rem(y + 1 + 2 * way, NY)) * 2 + core

    def y_half(way, side):
        src = ys.at[side, pl.ds(way * HB, HB), :]
        return remote(src, yh.at[way, side], yh_ss.at[way, side], yh_rs.at[way, side], tensor=y_device(way))

    def y_full(way, side):
        src = ys.at[2 + 2 * way + side]
        return remote(src, yr.at[way, side], y_ss.at[way, side], y_rs.at[way, side], tensor=y_device(way))

    def join(buffer, i):
        to_core(buffer, i).wait_recv()
        ys[i] = (buffer[i].astype(F32) + cr[i].astype(F32)).astype(BF)
        if i < 2:
            for way in range(2):
                y_half(way, i).start()

    def y_second():
        for way in range(2):
            for side in range(2):
                y_half(way, side).wait_recv()
                add_rows(ys.at[2 + 2 * way + side, pl.ds(way * HB, HB), :], yh.at[way, side])
                y_full(way, side).start()

    def parts(buffer, part, sums, lo, hi):
        for i in range(lo, hi):
            buffer[i] = term(feature(i), part).astype(BF)

            @pl.when(sums)
            def _(i=i):
                if i > 0:
                    join(buffer, i - 1)
                if i == NQ - 1:
                    join(buffer, i)

            @pl.when(jnp.logical_not(sums))
            def _(i=i):
                to_core(buffer, i).start()

    def y_sum(which):
        total = ys[6 + which].astype(F32)
        for way in range(2):
            total = total + yr[way, which].astype(F32)
        return total

    swap = remote(xs, xv, xh_ss, xh_rs, tensor=((1 - xh) * NY + y) * 2 + core)

    def y_third():
        for way in range(2):
            for side in range(2):
                y_full(way, side).wait_recv()
        xs[...] = y_sum(1 - xh).astype(BF)
        swap.start()
        ng[...] = y_sum(xh)

    def x_last():
        swap.wait_recv()
        ng[...] = ng[...] + xv[...].astype(F32)

    away = jnp.logical_not(keeps)

    def complete(j):
        if j != 1:
            swap_grad(j).wait_recv()

        @pl.loop(0, NZ)
        def _(zs):
            here = slice(j * 256, (j + 1) * 256)
            con[zs, j] = (con[zs, j].astype(F32) + dot(no[zs], qo[:, here])).astype(BF)

    def ring(j, s):
        for way, to in ways:
            if s == 1:
                half = con.at[rem(z + 4, NZ), j, pl.ds(way * HB, HB), :]
                go(remote(half, rb1.at[j, way], r1_ss.at[j, way], r1_rs.at[j, way], dp=to))
                continue
            zs = rem(z + (5 - s if way == 0 else NZ + s - 5), NZ)
            if s == 2:
                remote(rb1.at[j, way], rb1.at[j, way], r1_ss.at[j, way], r1_rs.at[j, way], dp=to).wait_recv()
                add_rows(con.at[zs, j, pl.ds(way * HB, HB), :], rb1.at[j, way])
            else:
                slot = rb.at[j, way, s - 3]
                remote(slot, slot, r_ss.at[j, way, s - 3], r_rs.at[j, way, s - 3], dp=to).wait_recv()
                add_rows(con.at[zs, j], slot)
            if s < 5:
                slot = rb.at[j, way, s - 2]
                go(remote(con.at[zs, j], slot, r_ss.at[j, way, s - 2], r_rs.at[j, way, s - 2], dp=to))
        if s == 5:
            gq[j] = con[z, j].astype(F32) * (1.0 / NR)

    contribute(2)
    turn(0, qg)
    parts(po, 0, keeps, 0, NQ)
    complete(2)
    ring(2, 1)

    @pl.when(keeps)
    def _():
        y_second()

    contribute(0)
    ring(2, 2)
    complete(0)
    ring(0, 1)
    contribute(1)
    swap_grad(1).wait_recv()
    turn(1, qo)
    parts(px, 1, away, 0, 4)
    ring(2, 3)
    ring(0, 2)
    parts(px, 1, away, 4, NQ)
    complete(1)
    ring(1, 1)
    ring(2, 4)

    @pl.when(away)
    def _():
        y_second()

    ring(0, 3)
    cp_part[...] = dot(attn[...], folded[...]).astype(BF)
    sum_t2 = Sum("tensor", cp_part, code, t2)
    sum_t2.first()
    mx_part[...] = dot_tn(attn[...], cg[...]).astype(BF)
    sum_d2 = Sum("dp", mx_part, mixing, d2)
    sum_d2.first()

    @pl.when(keeps)
    def _():
        y_third()

    ring(1, 2)
    ring(2, 5)
    ring(0, 4)
    sum_t2.second()
    sum_d2.second()

    @pl.when(away)
    def _():
        y_third()

    ring(1, 3)
    sum_t2.third()

    @pl.when(keeps)
    def _():
        x_last()

    ring(0, 5)
    sum_d2.third()
    ring(1, 4)
    sum_t2.across()
    home = remote(fs, fv, fs_ss, fs_rs, dp=other, tensor=sibling)

    @pl.when(jnp.logical_not(keeps))
    def _():
        x_last()
        fs[...] = ng[...].astype(BF)
        home.start()
        home.wait_recv()
        ng[...] = fv[...].astype(F32)

    grad = ng[...]
    scaled = grad * gcol[mine_rows, 0:1]
    lt[tensor, 0:1, :] = jnp.sum(scaled, axis=0, keepdims=True)
    lt[tensor, 1:2, :] = jnp.sum(scaled * hat[...], axis=0, keepdims=True)
    slot = lt.at[tensor]
    for k in range(1, NR):
        go(remote(slot, slot, lt_ss.at[k], lt_rs.at[k], tensor=rem(tensor + k, NR)))

    def fold(v):
        v = v[:, 0:128] + v[:, 128:256] + v[:, 256:384] + v[:, 384:512]
        v = jnp.concatenate([v, jnp.zeros((64, 128), F32)], axis=0)
        return jnp.sum(v.T, axis=0, keepdims=True)

    gs[dp, 0:1, :] = fold(ng[...] * hat[...])
    gs[dp, 1:2, :] = fold(ng[...])
    slot = gs.at[dp]
    for k in range(1, NR):
        go(remote(slot, slot, gs_ss.at[k], gs_rs.at[k], dp=rem(dp + k, NR)))
    sum_d2.fourth()
    sum_t2.fourth()
    ring(1, 5)
    sum_t2.last()
    ro_t[...] = (xt[mine_rows, :].astype(F32) + dot_nt(dect[...], code[...])).astype(BF)

    for k in range(1, NR):
        slot = lt.at[rem(tensor + NR - k, NR)]
        remote(slot, slot, lt_ss.at[k], lt_rs.at[k], tensor=tensor).wait_recv()
    sums = jnp.sum(lt[...], axis=0)
    lead, trail = sums[0:1, :] * (1.0 / D), sums[1:2, :] * (1.0 / D)
    scaled = ng[...] * gcol[mine_rows, 0:1]
    gi_t[...] = (got[...].astype(F32) + st[0:1, :] * (scaled - lead - hat[...] * trail)).astype(BF)
    sum_d2.last()
    gow_t[...] = dot_nt(enc[...], mixing[...]) * (1.0 / NR)
    for k in range(1, NR):
        slot = gs.at[rem(dp + NR - k, NR)]
        remote(slot, slot, gs_ss.at[k], gs_rs.at[k], dp=dp).wait_recv()
    gb[...] = jnp.sum(gs[...], axis=0) * (1.0 / NR)

    for total in (sum_t, sum_d, sum_t2, sum_d2):
        total.drain()
    swap.wait_send()
    for copy in sent:
        copy.wait_send()

    @pl.when(jnp.logical_not(keeps))
    def _():
        home.wait_send()

    @pl.loop(0, NQ)
    def _(i):
        to_core(po, i).wait_send()

    for way in range(2):
        for side in range(2):
            y_half(way, side).wait_send()
            y_full(way, side).wait_send()


def sublayer(*args):
    def shape(dims, kind):
        return jax.ShapeDtypeStruct(dims, kind)

    def v(kind, *dims):
        return pltpu.VMEM(dims, kind)

    one = pltpu.SemaphoreType.DMA
    whole = pl.BlockSpec(memory_space=pltpu.VMEM)
    far = pl.BlockSpec(memory_space=pl.ANY)
    scratch = [
        v(BF, SEQ, D), v(BF, 3, NZ * BLK, 256), v(BF, 2, NZ, BLK, SEQ), v(BF, NZ, BLK, SEQ), v(F32, 2, W3, SEQ),
        v(F32, SEQ, 128), v(F32, SEQ, 128), v(BF, SLAB, SEQ), v(F32, SLAB, 128), v(F32, BLK, SEQ), v(F32, 8, SEQ),
        v(BF, SEQ, C), v(BF, 256, C), v(BF, SEQ, C), v(BF, 256, C), v(BF, W3, SEQ), v(BF, W3, SEQ), v(BF, W3, SEQ),
        v(BF, SEQ, W3), v(BF, SEQ, 256), v(BF, SEQ, 256), v(BF, SEQ, W3), v(BF, SEQ, W3), v(BF, 2, W3, SEQ),
        v(F32, SEQ, 512),
        v(BF, NZ, 3, BLK, 256), v(BF, 3, 2, HB, 256), v(BF, 3, 2, 3, BLK, 256),
        v(BF, NQ, BLK, SEQ), v(BF, NQ, BLK, SEQ), v(BF, NQ, BLK, SEQ), v(BF, NQ, BLK, SEQ), v(BF, 2, 2, HB, SEQ), v(BF, 2, 2, BLK, SEQ),
        v(BF, BLK, SEQ), v(BF, BLK, SEQ), v(BF, BLK, SEQ), v(BF, BLK, SEQ), v(F32, BLK, SEQ),
        v(F32, NR, 8, SEQ), v(F32, NR, 8, 384), v(BF, SEQ, C), v(BF, 256, C), v(BF, SEQ, C), v(BF, 256, C),
        sum_buffers(SEQ, NY), sum_buffers(256, NZ), sum_buffers(SEQ, NY), sum_buffers(256, NZ),
        dma(4), one, dma(2, 3, 4), dma(2, 3, 4), dma(4, 4), dma(4, 4), dma(4, 4), dma(4, 4), dma(3), dma(3), dma(3), dma(3),
        dma(3, 2), dma(3, 2), dma(3, 2, 3), dma(3, 2, 3), dma(NQ), dma(NQ), dma(2, 2), dma(2, 2), dma(2, 2), dma(2, 2), one, one, one, one,
        dma(NR), dma(NR), dma(NR), dma(NR),
    ]
    return pl.pallas_call(
        kernel,
        out_shape=[
            shape((BLK, SEQ), BF),
            shape((BLK, SEQ), BF),
            shape((3, BLK, 256), F32),
            shape((BLK, 256), F32),
            shape((8, 384), F32),
        ],
        in_specs=[far, whole, whole, far, whole, whole, whole, whole],
        out_specs=[whole] * 5,
        scratch_shapes=scratch,
        compiler_params=pltpu.CompilerParams(
            collective_id=0, has_side_effects=True, vmem_limit_bytes=62 * 2**20
        ),
    )(*args)


def place_kernel(*refs):
    n = len(refs) // 2
    *refs, sems = refs
    copies = [pltpu.make_async_copy(refs[i], refs[n + i], sems.at[i]) for i in range(n)]
    for copy in copies:
        copy.start()
    for copy in copies:
        copy.wait()


def place(*arrays):
    far = pl.BlockSpec(memory_space=pl.ANY)
    return pl.pallas_call(
        place_kernel,
        out_shape=[jax.ShapeDtypeStruct(a.shape, a.dtype) for a in arrays],
        in_specs=[far] * len(arrays),
        out_specs=[far] * len(arrays),
        scratch_shapes=[dma(len(arrays))],
        compiler_params=pltpu.CompilerParams(vmem_limit_bytes=62 * 2**20),
    )(*arrays)


def local(
    residual_in,
    layernorm_gain,
    layernorm_bias,
    qkv_weight,
    out_weight,
    encoder,
    decoder,
    grad_output,
):
    residual_out, grad_input, grad_qkv, grad_out_weight, sums = sublayer(
        residual_in,
        layernorm_gain[None, :],
        layernorm_bias[None, :],
        qkv_weight,
        out_weight.T,
        encoder,
        decoder.T,
        grad_output.T,
    )
    residual_out, grad_input, grad_qkv, grad_out_weight = place(
        residual_out, grad_input, grad_qkv, grad_out_weight
    )
    return residual_out.T, grad_input.T, grad_qkv, grad_out_weight.T, sums[0, :BLK], sums[1, :BLK]


def solution(mesh):
    in_specs = (
        P("dp", None),
        P(),
        P(),
        P(None, "dp", "tensor"),
        P("tensor", "dp"),
        P("dp", None),
        P(None, "tensor"),
        P("dp", "tensor"),
    )
    out_specs = (
        P("dp", "tensor"),
        P("dp", "tensor"),
        P(None, "dp", "tensor"),
        P("tensor", "dp"),
        P("tensor"),
        P("tensor"),
    )
    return jax.shard_map(local, mesh=mesh, in_specs=in_specs, out_specs=out_specs, check_vma=False)
```

```python
import functools
from collections import deque

import jax
import jax.numpy as jnp
from jax import lax
from jax.experimental import pallas as pl
from jax.experimental.pallas import tpu as pltpu
from jax.sharding import PartitionSpec as P

HDIM = 128
EPS = 1e-05
MESH = pl.DeviceIdType.MESH
F32, BF = jnp.float32, jnp.bfloat16

NZ, NY, NQ, NR = 8, 4, 8, 16
SEQ, D, C, W3 = 512, 5120, 640, 768
BLK = 320
SLAB = 640
HB = BLK // 2


def rem(a, n):
    return lax.rem(a, n)


def rows(start, size):
    return pl.ds(pl.multiple_of(start, 16), size)


def dot(a, b):
    return lax.dot_general(a, b, (((1,), (0,)), ((), ())), preferred_element_type=F32)


def dot_nt(a, b):
    return lax.dot_general(a, b, (((1,), (1,)), ((), ())), preferred_element_type=F32)


def dot_tn(a, b):
    return lax.dot_general(a, b, (((0,), (0,)), ((), ())), preferred_element_type=F32)


def remote(src, dst, ssem, rsem, **device):
    return pltpu.make_async_remote_copy(
        src_ref=src, dst_ref=dst, send_sem=ssem, recv_sem=rsem, device_id=device, device_id_type=MESH
    )


def enter():
    barrier = pltpu.get_barrier_semaphore()
    for axis in ("dp", "tensor"):
        me = lax.axis_index(axis)
        for k in range(1, NR):
            pl.semaphore_signal(barrier, inc=1, device_id={axis: rem(me + k, NR)}, device_id_type=MESH)
    dp, tensor = lax.axis_index("dp"), lax.axis_index("tensor")
    across = {"dp": dp + 1 - 2 * rem(dp, 2), "tensor": tensor + 1 - 2 * rem(tensor, 2)}
    pl.semaphore_signal(barrier, inc=1, device_id=across, device_id_type=MESH)
    pl.semaphore_wait(barrier, 2 * (NR - 1) + 1)


class Sum:
    def __init__(self, axis, part, out, buffers):
        self.axis, self.part, self.out = axis, part, out
        self.got, self.half, self.ring, self.mid, self.mid_got, self.ssem, self.rsem = buffers
        index = lax.axis_index(axis)
        self.n = self.ring.shape[0]
        self.a = rem(index, 2)
        self.q = rem(index // 2, self.n)
        self.top = index // (2 * self.n)
        self.h = part.shape[0] // 2
        self.b = self.h // self.n
        self.sent = []

    def at(self, top, q, a):
        return {self.axis: (top * self.n + q) * 2 + a}

    def pair(self):
        return self.at(self.top, self.q, 1 - self.a)

    def peer(self, k):
        return self.at(self.top, rem(self.q + k, self.n), self.a)

    def over(self):
        return self.at(1 - self.top, self.q, self.a)

    def go(self, copy):
        copy.start()
        self.sent.append(copy)

    def first(self):
        src = self.part.at[rows((1 - self.a) * self.h, self.h), :]
        self.go(remote(src, self.got, self.ssem.at[0], self.rsem.at[0], **self.pair()))

    def second(self):
        remote(self.got, self.got, self.ssem.at[0], self.rsem.at[0], **self.pair()).wait_recv()
        mine = self.part[rows(self.a * self.h, self.h), :].astype(F32)
        self.half[...] = (mine + self.got[...].astype(F32)).astype(BF)
        for k in range(1, self.n):
            to = rem(self.q + k, self.n)
            src = self.half.at[rows(to * self.b, self.b), :]
            self.go(remote(src, self.ring.at[self.q], self.ssem.at[k], self.rsem.at[k], **self.peer(k)))

    def reduced(self):
        total = self.half[rows(self.q * self.b, self.b), :].astype(F32)
        for k in range(1, self.n):
            source = rem(self.q + self.n - k, self.n)
            slot = self.ring.at[source]
            remote(slot, slot, self.ssem.at[k], self.rsem.at[k], **self.peer(k)).wait_recv()
            total = total + self.ring[source].astype(F32)
        return total

    def spread(self, total):
        here = rows(self.a * self.h + self.q * self.b, self.b)
        self.out[here, :] = total.astype(BF)
        piece = self.out.at[here, :]
        for k in range(1, self.n):
            self.go(remote(piece, piece, self.ssem.at[7 + k], self.rsem.at[7 + k], **self.peer(k)))

    def third(self):
        if self.mid is None:
            self.spread(self.reduced())
        else:
            self.mid[...] = self.reduced().astype(BF)
            self.go(remote(self.mid, self.mid_got, self.ssem.at[16], self.rsem.at[16], **self.over()))

    def across(self):
        remote(self.mid, self.mid_got, self.ssem.at[16], self.rsem.at[16], **self.over()).wait_recv()
        self.spread(self.mid[...].astype(F32) + self.mid_got[...].astype(F32))

    def fourth(self):
        for k in range(1, self.n):
            source = rem(self.q + self.n - k, self.n)
            piece = self.out.at[rows(self.a * self.h + source * self.b, self.b), :]
            remote(piece, piece, self.ssem.at[7 + k], self.rsem.at[7 + k], **self.peer(k)).wait_recv()
        mine = self.out.at[rows(self.a * self.h, self.h), :]
        self.go(remote(mine, mine, self.ssem.at[15], self.rsem.at[15], **self.pair()))

    def last(self):
        other = self.out.at[rows((1 - self.a) * self.h, self.h), :]
        remote(other, other, self.ssem.at[15], self.rsem.at[15], **self.pair()).wait_recv()

    def drain(self):
        for copy in self.sent:
            copy.wait_send()


def dma(*shape):
    return pltpu.SemaphoreType.DMA(shape)


def sum_buffers(r, n):
    h = r // 2
    cut = pltpu.VMEM((h // n, C), BF)
    mids = [cut, cut] if n == NY else [None, None]
    return [pltpu.VMEM((h, C), BF), pltpu.VMEM((h, C), BF), pltpu.VMEM((n, h // n, C), BF)] + mids + [dma(17), dma(17)]


def add_rows(dst, src):
    @pl.loop(0, dst.shape[0] // 80)
    def _(i):
        here = rows(i * 80, 80)
        dst[here, :] = (dst[here, :].astype(F32) + src[here, :].astype(F32)).astype(BF)


def kernel(
    x_hbm, gain, bias, w_in, owt, enc, dect, got,
    ro_t, gi_t, gq, gow_t, gb,
    x, w, nb, no, acc, mu, rstd, xt, gcol, hat, st,
    cg_part, fo_part, cg, folded, ps, pr, qkvt, qkv, ag, attn, qg, qo, qgt, dkv, pp,
    con, rb1, rb, po, px, cr, ys, yh, yr, xs, xv, fs, fv, ng, lt, gs, cp_part, mx_part, code, mixing,
    t1, d1, t2, d2,
    x_sem, loc, a_ss, a_rs, n_ss, n_rs, f_ss, f_rs, p_ss, p_rs, q_ss, q_rs,
    r1_ss, r1_rs, r_ss, r_rs, cs_ss, cs_rs, yh_ss, yh_rs, y_ss, y_rs, xh_ss, xh_rs, fs_ss, fs_rs, lt_ss, lt_rs, gs_ss, gs_rs,
):
    dp, tensor = lax.axis_index("dp"), lax.axis_index("tensor")
    z, xl = dp // 2, rem(dp, 2)
    up, down = rem(z + 1, NZ) * 2 + xl, rem(z + NZ - 1, NZ) * 2 + xl
    other = z * 2 + 1 - xl
    core, q = rem(tensor, 2), tensor // 2
    xh, y = q // NY, rem(q, NY)
    sibling = q * 2 + 1 - core
    ways = ((0, up), (1, down))
    sent = []

    def go(copy):
        copy.start()
        sent.append(copy)

    x_copies = [
        pltpu.make_async_copy(x_hbm.at[pl.ds(i * 128, 128), :], x.at[pl.ds(i * 128, 128), :], x_sem.at[i])
        for i in range(4)
    ]
    for copy in x_copies:
        copy.start()
    enter()

    def block(j, zs, offset=0, size=BLK):
        return w.at[j, rows(zs * BLK + offset, size), :]

    mine = pltpu.make_async_copy(w_in, w.at[:, rows(z * BLK, BLK), :], loc)
    mine.start()

    def send_own(j):
        for way, to in ways:
            go(remote(w_in.at[j], block(j, z), a_ss.at[way, j, 0], a_rs.at[way, j, 0], dp=to))

    def relay(j, s):
        for way, to in ways:
            zs = rem(z + (NZ - s if way == 0 else s), NZ)
            if s < 4:
                part = block(j, zs)
                remote(part, part, a_ss.at[way, j, s - 1], a_rs.at[way, j, s - 1], dp=to).wait_recv()
                if s == 3:
                    part = block(j, zs, way * HB, HB)
                go(remote(part, part, a_ss.at[way, j, s], a_rs.at[way, j, s], dp=to))
            else:
                part = block(j, zs, way * HB, HB)
                remote(part, part, a_ss.at[way, j, 3], a_rs.at[way, j, 3], dp=to).wait_recv()

    send_own(0)
    send_own(1)
    sum_d = Sum("dp", fo_part, folded, d1)
    sum_t = Sum("tensor", cg_part, cg, t1)

    def start_folded():
        fo_part[...] = dot_tn(owt[...], enc[...]).astype(BF)
        sum_d.first()

    def start_code_grad():
        cg_part[...] = dot_tn(got[...], dect[...]).astype(BF)
        sum_t.first()

    def slab_cols(zs):
        return pl.ds(pl.multiple_of(zs * SLAB, 128), SLAB)

    def near(i):
        odd = rem(i, 2)
        return rem(z + odd * ((i + 1) // 2) + (1 - odd) * (NZ - i // 2), NZ)

    def tokens(r):
        return pl.ds(r * 128, 128)

    def cross(k, r):
        zs = near(2 * k + core)
        src, dst = nb.at[1, zs, :, tokens(r)], no.at[zs, :, tokens(r)]
        return remote(src, dst, n_ss.at[k, r], n_rs.at[k, r], dp=other)

    def pass_on(k, r):
        part = no.at[near(2 * k + core), :, tokens(r)]
        return remote(part, part, f_ss.at[k, r], f_rs.at[k, r], tensor=sibling)

    def norm(r, lo, hi):
        if lo == 0:
            x_copies[r].wait()
            xt[:, r * 128 : (r + 1) * 128] = x[r * 128 : (r + 1) * 128, slab_cols(q)].T

        @pl.loop(lo, hi)
        def _(i):
            here = rows(r * 128 + i * 16, 16)
            v = x[here, :].astype(F32)
            mean = jnp.sum(v, axis=1, keepdims=True) * (1.0 / D)
            v = v - mean
            var = jnp.sum(v * v, axis=1, keepdims=True) * (1.0 / D)
            scale = lax.rsqrt(var + EPS)
            mu[here, :] = jnp.broadcast_to(mean, (16, 128))
            rstd[here, :] = jnp.broadcast_to(scale, (16, 128))
            x[here, :] = (v * scale * gain[...] + bias[...]).astype(BF)

    def spread(r):
        @pl.loop(0, NZ)
        def _(zs):
            v = x[r * 128 : (r + 1) * 128, slab_cols(zs)].T
            nb[xl, zs, :, r * 128 : (r + 1) * 128] = v[0:BLK]
            nb[1 - xl, zs, :, r * 128 : (r + 1) * 128] = v[BLK:SLAB]

        for k in range(4):
            go(cross(k, r))

    def forward_on(r):
        for k in range(4):
            cross(k, r).wait_recv()
            go(pass_on(k, r))

    def use(j, i, part):
        zs = near(i)
        here = slice(j * 256, (j + 1) * 256)
        source = nb.at[0, zs] if part == 0 else no.at[zs]
        acc[part, here, :] += dot_tn(block(j, zs)[...], source[...])

    def use_all(j, lo, hi, part):
        @pl.loop(lo, hi)
        def _(i):
            use(j, i, part)

    def partial(j):
        here = pl.ds(j * 256, 256)
        return remote(ps.at[here, :], pr.at[here, :], p_ss.at[j], p_rs.at[j], dp=other)

    def give(j):
        here = slice(j * 256, (j + 1) * 256)
        ps[here, :] = acc[1, here, :].astype(BF)
        go(partial(j))

    def take(j):
        here = slice(j * 256, (j + 1) * 256)
        partial(j).wait_recv()
        qkvt[here, :] = (acc[0, here, :] + pr[here, :].astype(F32)).astype(BF)
        qkv[:, here] = qkvt[here, :].T

    def collect():
        for r in range(4):
            for k in range(4):
                part = no.at[near(2 * k + 1 - core), :, tokens(r)]
                remote(part, part, f_ss.at[k, r], f_rs.at[k, r], tensor=sibling).wait_recv()

    work = deque()

    def add(cost, f, *args):
        work.append((cost, functools.partial(f, *args)))

    def clear():
        acc[...] = jnp.zeros_like(acc)

    def relay_use(j, s):
        relay(j, s)
        lo, hi = (7, 8) if s == 4 else (2 * s - 1, 2 * s + 1)
        add(0.33 * (hi - lo), use_all, j, lo, hi, 0)

    def own_use():
        mine.wait()
        for j in range(3):
            add(0.33, use_all, j, 0, 1, 0)

    def far_use(j):
        use_all(j, 0, 8, 1)
        give(j)

    def far_begin():
        use_all(2, 0, 7, 1)

    def far_end():
        use_all(2, 7, 8, 1)
        give(2)

    add(1.2, start_folded)
    for r in range(4):
        add(1.3, norm, r, 0, 4)
        add(1.3, norm, r, 4, 8)
        add(1.1, spread, r)
        if r == 0:
            add(0.8, clear)
        if r == 2:
            add(1.5, start_code_grad)
    events = [
        (5.0, relay_use, 0, 1),
        (7.0, sum_d.second),
        (8.5, relay_use, 1, 1),
        (12.0, relay_use, 0, 2),
        (13.5, forward_on, 0),
        (15.5, relay_use, 1, 2),
        (15.6, send_own, 2),
        (19.0, relay_use, 0, 3),
        (19.5, sum_d.third),
        (20.5, forward_on, 1),
        (21.0, own_use),
        (21.5, sum_t.second),
        (24.0, relay_use, 2, 1),
        (25.5, sum_t.third),
        (28.0, relay_use, 1, 3),
        (28.0, forward_on, 2),
        (30.0, relay_use, 0, 4),
        (31.0, sum_d.fourth),
        (32.0, sum_t.across),
        (33.0, relay_use, 2, 2),
        (35.0, forward_on, 3),
        (36.0, relay_use, 1, 4),
        (37.5, collect),
        (38.0, far_use, 0),
        (39.0, relay_use, 2, 3),
        (39.5, far_use, 1),
        (42.0, far_begin),
        (43.0, relay_use, 2, 4),
        (43.0, far_end),
        (44.0, sum_t.fourth),
    ]
    now = 0.0
    for when, f, *args in events:
        while work and now + work[0][0] <= when + 0.3:
            cost, g = work.popleft()
            g()
            now += cost
        f(*args)
        now = max(now, when) + (2.5 if f in (far_use, far_begin) else 0.2)
    while work:
        work.popleft()[1]()
    mine_rows = rows(core * BLK, BLK)
    rs_row = rstd[...].T[0:1, :]
    hat[...] = (xt[mine_rows, :].astype(F32) - mu[...].T[0:1, :]) * rs_row
    st[0:1, :] = rs_row
    gcol[...] = jnp.broadcast_to(gain[0:1, slab_cols(q)], (128, SLAB)).T
    dkv[...] = jnp.zeros_like(dkv)
    take(0)
    take(1)

    rate = HDIM**-0.5
    blocks = [(h, r) for h in range(2) for r in range(4)]

    def cut(h, r):
        return slice(h * HDIM, (h + 1) * HDIM), slice(r * 128, (r + 1) * 128), 128 * (r + 1)

    def columns(j, h):
        return slice(j * 256 + h * HDIM, j * 256 + (h + 1) * HDIM)

    for h, r in blocks:
        _, here, n = cut(h, r)
        s = dot_nt(qkv[here, columns(0, h)], qkv[0:n, columns(1, h)]) * rate
        at_row = lax.broadcasted_iota(jnp.int32, (128, n), 0) + r * 128
        at_col = lax.broadcasted_iota(jnp.int32, (128, n), 1)
        s = jnp.where(at_col <= at_row, s, -1e30)
        e = jnp.exp(s - jnp.max(s, axis=1, keepdims=True))
        pp[h, here, 0:n] = e * (1.0 / jnp.sum(e, axis=1, keepdims=True))
    sum_t.last()
    sum_d.last()
    ag[...] = dot_nt(cg[...], folded[...]).astype(BF)
    take(2)
    for h, r in blocks:
        cq, here, n = cut(h, r)
        pb = pp[h, here, 0:n].astype(BF)
        attn[here, cq] = dot(pb, qkv[0:n, columns(2, h)]).astype(BF)
        dkv[0:n, columns(1, h)] += dot_tn(pb, ag[here, cq])
    qg[:, 512:768] = dkv[:, 256:512].astype(BF)

    def swap_grad(j):
        here = pl.ds(j * 256, 256)
        return remote(qg.at[:, here], qo.at[:, here], q_ss.at[j], q_rs.at[j], dp=other)

    go(swap_grad(2))
    for h, r in blocks:
        cq, here, n = cut(h, r)
        p, vb = pp[h, here, 0:n], qkv[0:n, columns(2, h)]
        dpr = dot_nt(ag[here, cq], vb).astype(BF).astype(F32)
        ds = p * (dpr - jnp.sum(p * dpr, axis=1, keepdims=True))
        ds = (ds * rate).astype(BF)
        qg[here, cq] = dot(ds, qkv[0:n, columns(1, h)]).astype(BF)
        dkv[0:n, cq] += dot_tn(ds, qkv[here, columns(0, h)])
    go(swap_grad(0))
    qg[:, 256:512] = dkv[:, 0:256].astype(BF)
    go(swap_grad(1))

    def contribute(j):
        @pl.loop(0, NZ)
        def _(zs):
            con[zs, j] = dot(nb[0, zs], qg[:, j * 256 : (j + 1) * 256]).astype(BF)

    def turn(part, source):
        @pl.loop(0, 6)
        def _(i):
            here = pl.ds(pl.multiple_of(i * 128, 128), 128)
            qgt[part, here, :] = source[:, here].T

    def term(zs, part):
        here = rows(zs * BLK, BLK)
        out = dot(w[0, here, :], qgt[part, 0:256, :])
        out = out + dot(w[1, here, :], qgt[part, 256:512, :])
        return out + dot(w[2, here, :], qgt[part, 512:768, :])

    def feature(i):
        return i % 2 * NY + rem(y + (2, 1, 3, 0)[i // 2], NY)

    keeps = core == xl

    def to_core(buffer, i):
        return remote(buffer.at[i], cr.at[i], cs_ss.at[i], cs_rs.at[i], tensor=sibling)

    def y_device(way):
        return (xh * NY + rem(y + 1 + 2 * way, NY)) * 2 + core

    def y_half(way, side):
        src = ys.at[side, pl.ds(way * HB, HB), :]
        return remote(src, yh.at[way, side], yh_ss.at[way, side], yh_rs.at[way, side], tensor=y_device(way))

    def y_full(way, side):
        src = ys.at[2 + 2 * way + side]
        return remote(src, yr.at[way, side], y_ss.at[way, side], y_rs.at[way, side], tensor=y_device(way))

    def join(buffer, i):
        to_core(buffer, i).wait_recv()
        ys[i] = (buffer[i].astype(F32) + cr[i].astype(F32)).astype(BF)
        if i < 2:
            for way in range(2):
                y_half(way, i).start()

    def y_second():
        for way in range(2):
            for side in range(2):
                y_half(way, side).wait_recv()
                add_rows(ys.at[2 + 2 * way + side, pl.ds(way * HB, HB), :], yh.at[way, side])
                y_full(way, side).start()

    def parts(buffer, part, sums, lo, hi):
        for i in range(lo, hi):
            buffer[i] = term(feature(i), part).astype(BF)

            @pl.when(sums)
            def _(i=i):
                if i > 0:
                    join(buffer, i - 1)
                if i == NQ - 1:
                    join(buffer, i)

            @pl.when(jnp.logical_not(sums))
            def _(i=i):
                to_core(buffer, i).start()

    def y_sum(which):
        total = ys[6 + which].astype(F32)
        for way in range(2):
            total = total + yr[way, which].astype(F32)
        return total

    swap = remote(xs, xv, xh_ss, xh_rs, tensor=((1 - xh) * NY + y) * 2 + core)

    def y_third():
        for way in range(2):
            for side in range(2):
                y_full(way, side).wait_recv()
        xs[...] = y_sum(1 - xh).astype(BF)
        swap.start()
        ng[...] = y_sum(xh)

    def x_last():
        swap.wait_recv()
        ng[...] = ng[...] + xv[...].astype(F32)

    away = jnp.logical_not(keeps)

    def complete(j):
        if j != 1:
            swap_grad(j).wait_recv()

        @pl.loop(0, NZ)
        def _(zs):
            here = slice(j * 256, (j + 1) * 256)
            con[zs, j] = (con[zs, j].astype(F32) + dot(no[zs], qo[:, here])).astype(BF)

    def ring(j, s):
        for way, to in ways:
            if s == 1:
                half = con.at[rem(z + 4, NZ), j, pl.ds(way * HB, HB), :]
                go(remote(half, rb1.at[j, way], r1_ss.at[j, way], r1_rs.at[j, way], dp=to))
                continue
            zs = rem(z + (5 - s if way == 0 else NZ + s - 5), NZ)
            if s == 2:
                remote(rb1.at[j, way], rb1.at[j, way], r1_ss.at[j, way], r1_rs.at[j, way], dp=to).wait_recv()
                add_rows(con.at[zs, j, pl.ds(way * HB, HB), :], rb1.at[j, way])
            else:
                slot = rb.at[j, way, s - 3]
                remote(slot, slot, r_ss.at[j, way, s - 3], r_rs.at[j, way, s - 3], dp=to).wait_recv()
                add_rows(con.at[zs, j], slot)
            if s < 5:
                slot = rb.at[j, way, s - 2]
                go(remote(con.at[zs, j], slot, r_ss.at[j, way, s - 2], r_rs.at[j, way, s - 2], dp=to))
        if s == 5:
            gq[j] = con[z, j].astype(F32) * (1.0 / NR)

    contribute(2)
    cp_part[...] = dot(attn[...], folded[...]).astype(BF)
    sum_t2 = Sum("tensor", cp_part, code, t2)
    sum_t2.first()
    turn(0, qg)
    complete(2)
    ring(2, 1)
    mx_part[...] = dot_tn(attn[...], cg[...]).astype(BF)
    sum_d2 = Sum("dp", mx_part, mixing, d2)
    sum_d2.first()
    parts(po, 0, keeps, 0, 4)
    sum_t2.second()
    ring(2, 2)
    parts(po, 0, keeps, 4, NQ)
    contribute(0)
    complete(0)
    ring(0, 1)
    ring(2, 3)
    sum_t2.third()

    @pl.when(keeps)
    def _():
        y_second()

    contribute(1)
    ring(0, 2)
    swap_grad(1).wait_recv()
    turn(1, qo)
    parts(px, 1, away, 0, 4)
    ring(2, 4)
    sum_t2.across()
    parts(px, 1, away, 4, NQ)
    ring(0, 3)
    complete(1)
    ring(1, 1)

    @pl.when(keeps)
    def _():
        y_third()

    @pl.when(away)
    def _():
        y_second()

    sum_d2.second()
    ring(2, 5)
    ring(1, 2)
    ring(0, 4)
    sum_t2.fourth()

    @pl.when(keeps)
    def _():
        x_last()

    @pl.when(away)
    def _():
        y_third()

    ring(1, 3)
    sum_d2.third()
    ring(0, 5)
    home = remote(fs, fv, fs_ss, fs_rs, dp=other, tensor=sibling)

    @pl.when(away)
    def _():
        x_last()
        fs[...] = ng[...].astype(BF)
        home.start()

    ring(1, 4)
    sum_d2.fourth()

    @pl.when(away)
    def _():
        home.wait_recv()
        ng[...] = fv[...].astype(F32)

    grad = ng[...]
    scaled = grad * gcol[mine_rows, 0:1]
    lt[tensor, 0:1, :] = jnp.sum(scaled, axis=0, keepdims=True)
    lt[tensor, 1:2, :] = jnp.sum(scaled * hat[...], axis=0, keepdims=True)
    slot = lt.at[tensor]
    for k in range(1, NR):
        go(remote(slot, slot, lt_ss.at[k], lt_rs.at[k], tensor=rem(tensor + k, NR)))

    def fold(v):
        v = v[:, 0:128] + v[:, 128:256] + v[:, 256:384] + v[:, 384:512]
        v = jnp.concatenate([v, jnp.zeros((64, 128), F32)], axis=0)
        return jnp.sum(v.T, axis=0, keepdims=True)

    gs[dp, 0:1, :] = fold(ng[...] * hat[...])
    gs[dp, 1:2, :] = fold(ng[...])
    slot = gs.at[dp]
    for k in range(1, NR):
        go(remote(slot, slot, gs_ss.at[k], gs_rs.at[k], dp=rem(dp + k, NR)))
    sum_t2.last()
    ro_t[...] = (xt[mine_rows, :].astype(F32) + dot_nt(dect[...], code[...])).astype(BF)

    for k in range(1, NR):
        slot = lt.at[rem(tensor + NR - k, NR)]
        remote(slot, slot, lt_ss.at[k], lt_rs.at[k], tensor=tensor).wait_recv()
    sums = jnp.sum(lt[...], axis=0)
    lead, trail = sums[0:1, :] * (1.0 / D), sums[1:2, :] * (1.0 / D)
    scaled = ng[...] * gcol[mine_rows, 0:1]
    gi_t[...] = (got[...].astype(F32) + st[0:1, :] * (scaled - lead - hat[...] * trail)).astype(BF)
    ring(1, 5)
    sum_d2.last()
    gow_t[...] = dot_nt(enc[...], mixing[...]) * (1.0 / NR)
    for k in range(1, NR):
        slot = gs.at[rem(dp + NR - k, NR)]
        remote(slot, slot, gs_ss.at[k], gs_rs.at[k], dp=dp).wait_recv()
    gb[...] = jnp.sum(gs[...], axis=0) * (1.0 / NR)

    for total in (sum_t, sum_d, sum_t2, sum_d2):
        total.drain()
    swap.wait_send()
    for copy in sent:
        copy.wait_send()

    @pl.when(jnp.logical_not(keeps))
    def _():
        home.wait_send()

    @pl.loop(0, NQ)
    def _(i):
        to_core(po, i).wait_send()

    for way in range(2):
        for side in range(2):
            y_half(way, side).wait_send()
            y_full(way, side).wait_send()


def sublayer(*args):
    def shape(dims, kind):
        return jax.ShapeDtypeStruct(dims, kind)

    def v(kind, *dims):
        return pltpu.VMEM(dims, kind)

    one = pltpu.SemaphoreType.DMA
    whole = pl.BlockSpec(memory_space=pltpu.VMEM)
    far = pl.BlockSpec(memory_space=pl.ANY)
    scratch = [
        v(BF, SEQ, D), v(BF, 3, NZ * BLK, 256), v(BF, 2, NZ, BLK, SEQ), v(BF, NZ, BLK, SEQ), v(F32, 2, W3, SEQ),
        v(F32, SEQ, 128), v(F32, SEQ, 128), v(BF, SLAB, SEQ), v(F32, SLAB, 128), v(F32, BLK, SEQ), v(F32, 8, SEQ),
        v(BF, SEQ, C), v(BF, 256, C), v(BF, SEQ, C), v(BF, 256, C), v(BF, W3, SEQ), v(BF, W3, SEQ), v(BF, W3, SEQ),
        v(BF, SEQ, W3), v(BF, SEQ, 256), v(BF, SEQ, 256), v(BF, SEQ, W3), v(BF, SEQ, W3), v(BF, 2, W3, SEQ),
        v(F32, SEQ, 512), v(F32, 2, SEQ, SEQ),
        v(BF, NZ, 3, BLK, 256), v(BF, 3, 2, HB, 256), v(BF, 3, 2, 3, BLK, 256),
        v(BF, NQ, BLK, SEQ), v(BF, NQ, BLK, SEQ), v(BF, NQ, BLK, SEQ), v(BF, NQ, BLK, SEQ), v(BF, 2, 2, HB, SEQ), v(BF, 2, 2, BLK, SEQ),
        v(BF, BLK, SEQ), v(BF, BLK, SEQ), v(BF, BLK, SEQ), v(BF, BLK, SEQ), v(F32, BLK, SEQ),
        v(F32, NR, 8, SEQ), v(F32, NR, 8, 384), v(BF, SEQ, C), v(BF, 256, C), v(BF, SEQ, C), v(BF, 256, C),
        sum_buffers(SEQ, NY), sum_buffers(256, NZ), sum_buffers(SEQ, NY), sum_buffers(256, NZ),
        dma(4), one, dma(2, 3, 4), dma(2, 3, 4), dma(4, 4), dma(4, 4), dma(4, 4), dma(4, 4), dma(3), dma(3), dma(3), dma(3),
        dma(3, 2), dma(3, 2), dma(3, 2, 3), dma(3, 2, 3), dma(NQ), dma(NQ), dma(2, 2), dma(2, 2), dma(2, 2), dma(2, 2), one, one, one, one,
        dma(NR), dma(NR), dma(NR), dma(NR),
    ]
    return pl.pallas_call(
        kernel,
        out_shape=[
            shape((BLK, SEQ), BF),
            shape((BLK, SEQ), BF),
            shape((3, BLK, 256), F32),
            shape((BLK, 256), F32),
            shape((8, 384), F32),
        ],
        in_specs=[far, whole, whole, far, whole, whole, whole, whole],
        out_specs=[whole] * 5,
        scratch_shapes=scratch,
        compiler_params=pltpu.CompilerParams(
            collective_id=0, has_side_effects=True, vmem_limit_bytes=62 * 2**20
        ),
    )(*args)


def place_kernel(*refs):
    n = len(refs) // 2
    *refs, sems = refs
    copies = [pltpu.make_async_copy(refs[i], refs[n + i], sems.at[i]) for i in range(n)]
    for copy in copies:
        copy.start()
    for copy in copies:
        copy.wait()


def place(*arrays):
    far = pl.BlockSpec(memory_space=pl.ANY)
    return pl.pallas_call(
        place_kernel,
        out_shape=[jax.ShapeDtypeStruct(a.shape, a.dtype) for a in arrays],
        in_specs=[pl.BlockSpec(memory_space=pltpu.VMEM)] * len(arrays),
        out_specs=[far] * len(arrays),
        scratch_shapes=[dma(len(arrays))],
    )(*arrays)


def local(
    residual_in,
    layernorm_gain,
    layernorm_bias,
    qkv_weight,
    out_weight,
    encoder,
    decoder,
    grad_output,
):
    residual_out, grad_input, grad_qkv, grad_out_weight, sums = sublayer(
        residual_in,
        layernorm_gain[None, :],
        layernorm_bias[None, :],
        qkv_weight,
        out_weight.T,
        encoder,
        decoder.T,
        grad_output.T,
    )
    residual_out, grad_input, grad_qkv, grad_out_weight = place(
        residual_out, grad_input, grad_qkv, grad_out_weight
    )
    return residual_out.T, grad_input.T, grad_qkv, grad_out_weight.T, sums[0, :BLK], sums[1, :BLK]


def solution(mesh):
    in_specs = (
        P("dp", None),
        P(),
        P(),
        P(None, "dp", "tensor"),
        P("tensor", "dp"),
        P("dp", None),
        P(None, "tensor"),
        P("dp", "tensor"),
    )
    out_specs = (
        P("dp", "tensor"),
        P("dp", "tensor"),
        P(None, "dp", "tensor"),
        P("tensor", "dp"),
        P("tensor"),
        P("tensor"),
    )
    return jax.shard_map(local, mesh=mesh, in_specs=in_specs, out_specs=out_specs, check_vma=False)
```

```python
import functools
from collections import deque

import jax
import jax.numpy as jnp
from jax import lax
from jax.experimental import pallas as pl
from jax.experimental.pallas import tpu as pltpu
from jax.sharding import PartitionSpec as P

HDIM = 128
EPS = 1e-05
MESH = pl.DeviceIdType.MESH
F32, BF = jnp.float32, jnp.bfloat16

NZ, NY, NQ, NR = 8, 4, 8, 16
SEQ, D, C, W3 = 512, 5120, 640, 768
BLK = 320
SLAB = 640
HB = BLK // 2


def rem(a, n):
    return lax.rem(a, n)


def rows(start, size):
    return pl.ds(pl.multiple_of(start, 16), size)


def dot(a, b):
    return lax.dot_general(a, b, (((1,), (0,)), ((), ())), preferred_element_type=F32)


def dot_nt(a, b):
    return lax.dot_general(a, b, (((1,), (1,)), ((), ())), preferred_element_type=F32)


def dot_tn(a, b):
    return lax.dot_general(a, b, (((0,), (0,)), ((), ())), preferred_element_type=F32)


def remote(src, dst, ssem, rsem, **device):
    return pltpu.make_async_remote_copy(
        src_ref=src, dst_ref=dst, send_sem=ssem, recv_sem=rsem, device_id=device, device_id_type=MESH
    )


def enter():
    barrier = pltpu.get_barrier_semaphore()
    for axis in ("dp", "tensor"):
        me = lax.axis_index(axis)
        for k in range(1, NR):
            pl.semaphore_signal(barrier, inc=1, device_id={axis: rem(me + k, NR)}, device_id_type=MESH)
    dp, tensor = lax.axis_index("dp"), lax.axis_index("tensor")
    flip = tensor + 1 - 2 * rem(tensor, 2)
    for there in (flip, rem(flip + 8, NR)):
        across = {"dp": dp + 1 - 2 * rem(dp, 2), "tensor": there}
        pl.semaphore_signal(barrier, inc=1, device_id=across, device_id_type=MESH)
    pl.semaphore_wait(barrier, 2 * NR)


class Sum:
    def __init__(self, axis, part, out, buffers):
        self.axis, self.part, self.out = axis, part, out
        self.got, self.half, self.ring, self.mid, self.mid_got, self.ssem, self.rsem = buffers
        index = lax.axis_index(axis)
        self.n = self.ring.shape[0]
        self.a = rem(index, 2)
        self.q = rem(index // 2, self.n)
        self.top = index // (2 * self.n)
        self.h = part.shape[0] // 2
        self.b = self.h // self.n
        self.sent = []

    def at(self, top, q, a):
        return {self.axis: (top * self.n + q) * 2 + a}

    def pair(self):
        return self.at(self.top, self.q, 1 - self.a)

    def peer(self, k):
        return self.at(self.top, rem(self.q + k, self.n), self.a)

    def over(self):
        return self.at(1 - self.top, self.q, self.a)

    def go(self, copy):
        copy.start()
        self.sent.append(copy)

    def first(self):
        src = self.part.at[rows((1 - self.a) * self.h, self.h), :]
        self.go(remote(src, self.got, self.ssem.at[0], self.rsem.at[0], **self.pair()))

    def second(self):
        remote(self.got, self.got, self.ssem.at[0], self.rsem.at[0], **self.pair()).wait_recv()
        mine = self.part[rows(self.a * self.h, self.h), :].astype(F32)
        self.half[...] = (mine + self.got[...].astype(F32)).astype(BF)
        for k in range(1, self.n):
            to = rem(self.q + k, self.n)
            src = self.half.at[rows(to * self.b, self.b), :]
            self.go(remote(src, self.ring.at[self.q], self.ssem.at[k], self.rsem.at[k], **self.peer(k)))

    def reduced(self):
        total = self.half[rows(self.q * self.b, self.b), :].astype(F32)
        for k in range(1, self.n):
            source = rem(self.q + self.n - k, self.n)
            slot = self.ring.at[source]
            remote(slot, slot, self.ssem.at[k], self.rsem.at[k], **self.peer(k)).wait_recv()
            total = total + self.ring[source].astype(F32)
        return total

    def spread(self, total):
        here = rows(self.a * self.h + self.q * self.b, self.b)
        self.out[here, :] = total.astype(BF)
        piece = self.out.at[here, :]
        for k in range(1, self.n):
            self.go(remote(piece, piece, self.ssem.at[7 + k], self.rsem.at[7 + k], **self.peer(k)))

    def third(self):
        if self.mid is None:
            self.spread(self.reduced())
        else:
            self.mid[...] = self.reduced().astype(BF)
            self.go(remote(self.mid, self.mid_got, self.ssem.at[16], self.rsem.at[16], **self.over()))

    def across(self):
        remote(self.mid, self.mid_got, self.ssem.at[16], self.rsem.at[16], **self.over()).wait_recv()
        self.spread(self.mid[...].astype(F32) + self.mid_got[...].astype(F32))

    def fourth(self):
        for k in range(1, self.n):
            source = rem(self.q + self.n - k, self.n)
            piece = self.out.at[rows(self.a * self.h + source * self.b, self.b), :]
            remote(piece, piece, self.ssem.at[7 + k], self.rsem.at[7 + k], **self.peer(k)).wait_recv()
        mine = self.out.at[rows(self.a * self.h, self.h), :]
        self.go(remote(mine, mine, self.ssem.at[15], self.rsem.at[15], **self.pair()))

    def last(self):
        other = self.out.at[rows((1 - self.a) * self.h, self.h), :]
        remote(other, other, self.ssem.at[15], self.rsem.at[15], **self.pair()).wait_recv()

    def drain(self):
        for copy in self.sent:
            copy.wait_send()


def dma(*shape):
    return pltpu.SemaphoreType.DMA(shape)


def sum_buffers(r, n):
    h = r // 2
    cut = pltpu.VMEM((h // n, C), BF)
    mids = [cut, cut] if n == NY else [None, None]
    return [pltpu.VMEM((h, C), BF), pltpu.VMEM((h, C), BF), pltpu.VMEM((n, h // n, C), BF)] + mids + [dma(17), dma(17)]


def add_rows(dst, src):
    @pl.loop(0, dst.shape[0] // 80)
    def _(i):
        here = rows(i * 80, 80)
        dst[here, :] = (dst[here, :].astype(F32) + src[here, :].astype(F32)).astype(BF)


def kernel(
    x_hbm, gain, bias, w_in, owt, enc, dect, got,
    ro_t, gi_t, gq, gow_t, gb,
    x, w, nb, no, acc, mu, rstd, xt, gcol, hat, st,
    cg_part, fo_part, cg, folded, ps, pr, qkv, ag, attn, qg, qo, qgt, dkv,
    con, rb1, rb, po, px, cr, ys, yh, yr, fs, fv, ng, lt, gs, code, mixing,
    t1, d1, t2, d2,
    x_sem, loc, a_ss, a_rs, n_ss, n_rs, g_ss, g_rs, f_ss, f_rs, p_ss, p_rs, q_ss, q_rs,
    r1_ss, r1_rs, r_ss, r_rs, cs_ss, cs_rs, yh_ss, yh_rs, y_ss, y_rs, xh_ss, xh_rs, fs_ss, fs_rs, lt_ss, lt_rs, gs_ss, gs_rs,
):
    dp, tensor = lax.axis_index("dp"), lax.axis_index("tensor")
    z, xl = dp // 2, rem(dp, 2)
    up, down = rem(z + 1, NZ) * 2 + xl, rem(z + NZ - 1, NZ) * 2 + xl
    other = z * 2 + 1 - xl
    core, q = rem(tensor, 2), tensor // 2
    xh, y = q // NY, rem(q, NY)
    sibling = q * 2 + 1 - core
    ways = ((0, up), (1, down))
    sent = []

    def go(copy):
        copy.start()
        sent.append(copy)

    x_copies = [
        pltpu.make_async_copy(x_hbm.at[pl.ds(i * 128, 128), :], x.at[pl.ds(i * 128, 128), :], x_sem.at[i])
        for i in range(4)
    ]
    for copy in x_copies:
        copy.start()
    enter()

    def block(j, zs, offset=0, size=BLK):
        return w.at[j, rows(zs * BLK + offset, size), :]

    mine = pltpu.make_async_copy(w_in, w.at[:, rows(z * BLK, BLK), :], loc)
    mine.start()

    def send_own(j):
        for way, to in ways:
            go(remote(w_in.at[j], block(j, z), a_ss.at[way, j, 0], a_rs.at[way, j, 0], dp=to))

    def relay(j, s):
        for way, to in ways:
            zs = rem(z + (NZ - s if way == 0 else s), NZ)
            if s < 4:
                part = block(j, zs)
                remote(part, part, a_ss.at[way, j, s - 1], a_rs.at[way, j, s - 1], dp=to).wait_recv()
                if s == 3:
                    part = block(j, zs, way * HB, HB)
                go(remote(part, part, a_ss.at[way, j, s], a_rs.at[way, j, s], dp=to))
            else:
                part = block(j, zs, way * HB, HB)
                remote(part, part, a_ss.at[way, j, 3], a_rs.at[way, j, 3], dp=to).wait_recv()

    send_own(0)
    send_own(1)
    sum_d = Sum("dp", fo_part, folded, d1)
    sum_t = Sum("tensor", cg_part, cg, t1)

    def start_folded():
        fo_part[...] = dot_tn(owt[...], enc[...]).astype(BF)
        sum_d.first()

    def start_code_grad():
        cg_part[...] = dot_tn(got[...], dect[...]).astype(BF)
        sum_t.first()

    def slab_cols(zs):
        return pl.ds(pl.multiple_of(zs * SLAB, 128), SLAB)

    def near(i):
        odd = rem(i, 2)
        return rem(z + odd * ((i + 1) // 2) + (1 - odd) * (NZ - i // 2), NZ)

    def tokens(r):
        return pl.ds(r * 128, 128)

    def piece(k, c, r):
        return no.at[near(2 * k + c), :, tokens(r)]

    def cross(r):
        src = nb.at[1, near(2 * y + core), :, tokens(r)]
        return remote(src, piece(y, core, r), n_ss.at[r], n_rs.at[r], dp=other)

    def along(k, r):
        part = piece(y, core, r)
        there = (xh * NY + rem(y + k, NY)) * 2 + core
        return remote(part, part, g_ss.at[k - 1, r], g_rs.at[k - 1, r], tensor=there)

    def pass_on(k, r):
        part = piece(rem(y + NY - k, NY), core, r)
        return remote(part, part, f_ss.at[k, r], f_rs.at[k, r], tensor=sibling)

    def norm(r, lo, hi):
        if lo == 0:
            x_copies[r].wait()
            xt[:, r * 128 : (r + 1) * 128] = x[r * 128 : (r + 1) * 128, slab_cols(q)].T

        @pl.loop(lo, hi)
        def _(i):
            here = rows(r * 128 + i * 16, 16)
            v = x[here, :].astype(F32)
            mean = jnp.sum(v, axis=1, keepdims=True) * (1.0 / D)
            v = v - mean
            var = jnp.sum(v * v, axis=1, keepdims=True) * (1.0 / D)
            scale = lax.rsqrt(var + EPS)
            mu[here, :] = jnp.broadcast_to(mean, (16, 128))
            rstd[here, :] = jnp.broadcast_to(scale, (16, 128))
            x[here, :] = (v * scale * gain[...] + bias[...]).astype(BF)

    def spread(r):
        @pl.loop(0, NZ)
        def _(zs):
            v = x[r * 128 : (r + 1) * 128, slab_cols(zs)].T
            nb[xl, zs, :, r * 128 : (r + 1) * 128] = v[0:BLK]
            nb[1 - xl, zs, :, r * 128 : (r + 1) * 128] = v[BLK:SLAB]

        go(cross(r))

    def forward_on(r):
        cross(r).wait_recv()
        for k in (2, 1, 3):
            go(along(k, r))
        go(pass_on(0, r))

    def share(r):
        for k in (1, 3, 2):
            part = piece(rem(y + NY - k, NY), core, r)
            remote(part, part, g_ss.at[k - 1, r], g_rs.at[k - 1, r], tensor=sibling).wait_recv()
            go(pass_on(k, r))

    def use(j, i, part):
        zs = near(i)
        here = slice(j * 256, (j + 1) * 256)
        source = nb.at[0, zs] if part == 0 else no.at[zs]
        acc[part, here, :] += dot_tn(block(j, zs)[...], source[...])

    def use_all(j, lo, hi, part):
        @pl.loop(lo, hi)
        def _(i):
            use(j, i, part)

    def partial(j):
        here = pl.ds(j * 256, 256)
        return remote(ps.at[here, :], pr.at[here, :], p_ss.at[j], p_rs.at[j], dp=other)

    def give(j):
        here = slice(j * 256, (j + 1) * 256)
        ps[here, :] = acc[1, here, :].astype(BF)
        go(partial(j))

    def take(j):
        here = slice(j * 256, (j + 1) * 256)
        partial(j).wait_recv()
        qkv[:, here] = (acc[0, here, :] + pr[here, :].astype(F32)).astype(BF).T

    def collect():
        for r in range(4):
            for k in range(4):
                part = piece(rem(y + NY - k, NY), 1 - core, r)
                remote(part, part, f_ss.at[k, r], f_rs.at[k, r], tensor=sibling).wait_recv()

    work = deque()

    def add(cost, f, *args):
        work.append((cost, f, args))

    def run():
        cost, f, args = work.popleft()
        f(*args)
        return cost

    def ahead(f, *args):
        while any(piece[1:] == (f, args) for piece in work):
            run()

    def clear():
        acc[...] = jnp.zeros_like(acc)

    def relay_use(j, s):
        relay(j, s)
        lo, hi = (7, 8) if s == 4 else (2 * s - 1, 2 * s + 1)
        add(0.33 * (hi - lo), use_all, j, lo, hi, 0)

    def own_use():
        mine.wait()
        for j in range(3):
            add(0.33, use_all, j, 0, 1, 0)

    def far_use(j):
        use_all(j, 0, 8, 1)
        give(j)

    def far_begin():
        use_all(2, 0, 7, 1)

    def far_end():
        use_all(2, 7, 8, 1)
        give(2)

    add(1.2, start_folded)
    for r in range(4):
        add(1.3, norm, r, 0, 4)
        add(1.3, norm, r, 4, 8)
        add(1.1, spread, r)
        if r == 0:
            add(0.8, clear)
        if r == 2:
            add(1.5, start_code_grad)
    events = [
        (5.0, relay_use, 0, 1),
        (7.0, sum_d.second),
        (8.3, forward_on, 0),
        (8.5, relay_use, 1, 1),
        (12.0, relay_use, 0, 2),
        (13.0, forward_on, 1),
        (13.2, share, 0),
        (15.5, relay_use, 1, 2),
        (15.6, send_own, 2),
        (17.0, forward_on, 2),
        (17.2, share, 1),
        (19.0, relay_use, 0, 3),
        (19.5, sum_d.third),
        (20.5, forward_on, 3),
        (21.0, own_use),
        (21.5, share, 2),
        (21.5, sum_t.second),
        (24.0, relay_use, 2, 1),
        (25.0, share, 3),
        (25.5, sum_t.third),
        (27.0, relay_use, 1, 3),
        (27.5, collect),
        (29.0, relay_use, 0, 4),
        (29.5, far_use, 0),
        (31.0, sum_d.fourth),
        (31.5, sum_t.across),
        (33.0, relay_use, 2, 2),
        (35.0, relay_use, 1, 4),
        (35.5, far_use, 1),
        (38.5, sum_t.fourth),
        (39.0, relay_use, 2, 3),
        (39.5, far_begin),
        (42.5, sum_t.last),
        (43.0, relay_use, 2, 4),
        (43.0, far_end),
    ]
    now = 0.0
    for when, f, *args in events:
        while work and now + work[0][0] <= when + 0.3:
            now += run()
        if f is forward_on:
            ahead(spread, *args)
        elif f == sum_d.second:
            ahead(start_folded)
        elif f == sum_t.second:
            ahead(start_code_grad)
        f(*args)
        now = max(now, when) + (2.5 if f in (far_use, far_begin) else 0.2)
    while work:
        run()
    mine_rows = rows(core * BLK, BLK)
    rs_row = rstd[...].T[0:1, :]
    hat[...] = (xt[mine_rows, :].astype(F32) - mu[...].T[0:1, :]) * rs_row
    st[0:1, :] = rs_row
    turned = jnp.broadcast_to(gain[0:1, slab_cols(q)], (128, SLAB)).T
    gcol[...] = jnp.where(core == 0, turned[0:BLK], turned[BLK:SLAB])
    dkv[...] = jnp.zeros_like(dkv)
    take(0)
    take(1)

    rate = HDIM**-0.5
    blocks = [(h, r) for h in range(2) for r in range(4)]

    def cut(h, r):
        return slice(h * HDIM, (h + 1) * HDIM), slice(r * 128, (r + 1) * 128), 128 * (r + 1)

    def columns(j, h):
        return slice(j * 256 + h * HDIM, j * 256 + (h + 1) * HDIM)

    for h, r in blocks:
        _, here, n = cut(h, r)
        s = dot_nt(qkv[here, columns(0, h)], qkv[0:n, columns(1, h)]) * rate
        at_row = lax.broadcasted_iota(jnp.int32, (128, n), 0) + r * 128
        at_col = lax.broadcasted_iota(jnp.int32, (128, n), 1)
        s = jnp.where(at_col <= at_row, s, -1e30)
        e = jnp.exp(s - jnp.max(s, axis=1, keepdims=True))
        acc[h, here, 0:n] = e * (1.0 / jnp.sum(e, axis=1, keepdims=True))
    sum_d.last()
    ag[...] = dot_nt(cg[...], folded[...]).astype(BF)
    for h, r in blocks:
        cq, here, n = cut(h, r)
        dkv[0:n, columns(1, h)] += dot_tn(acc[h, here, 0:n].astype(BF), ag[here, cq])
    qg[:, 512:768] = dkv[:, 256:512].astype(BF)

    def swap_grad(j):
        here = pl.ds(j * 256, 256)
        return remote(qg.at[:, here], qo.at[:, here], q_ss.at[j], q_rs.at[j], dp=other)

    go(swap_grad(2))

    def contribute(j):
        @pl.loop(0, NZ)
        def _(zs):
            con[zs, j] = dot(nb[0, zs], qg[:, j * 256 : (j + 1) * 256]).astype(BF)

    contribute(2)
    take(2)
    for h, r in blocks:
        cq, here, n = cut(h, r)
        p, vb = acc[h, here, 0:n], qkv[0:n, columns(2, h)]
        attn[here, cq] = dot(p.astype(BF), vb).astype(BF)
        dpr = dot_nt(ag[here, cq], vb).astype(BF).astype(F32)
        ds = p * (dpr - jnp.sum(p * dpr, axis=1, keepdims=True))
        ds = (ds * rate).astype(BF)
        qg[here, cq] = dot(ds, qkv[0:n, columns(1, h)]).astype(BF)
        dkv[0:n, cq] += dot_tn(ds, qkv[here, columns(0, h)])
    go(swap_grad(0))
    qg[:, 256:512] = dkv[:, 0:256].astype(BF)
    go(swap_grad(1))

    def turn(part, source):
        @pl.loop(0, 6)
        def _(i):
            here = pl.ds(pl.multiple_of(i * 128, 128), 128)
            qgt[part, here, :] = source[:, here].T

    def term(zs, part):
        here = rows(zs * BLK, BLK)
        out = dot(w[0, here, :], qgt[part, 0:256, :])
        out = out + dot(w[1, here, :], qgt[part, 256:512, :])
        return out + dot(w[2, here, :], qgt[part, 512:768, :])

    def feature(i):
        return i % 2 * NY + rem(y + (2, 1, 3, 0)[i // 2], NY)

    keeps = core == xl

    def to_core(buffer, i):
        return remote(buffer.at[i], cr.at[i], cs_ss.at[i], cs_rs.at[i], tensor=sibling)

    def y_device(way):
        return (xh * NY + rem(y + 1 + 2 * way, NY)) * 2 + core

    def y_half(way, side):
        src = ys.at[side, pl.ds(way * HB, HB), :]
        return remote(src, yh.at[way, side], yh_ss.at[way, side], yh_rs.at[way, side], tensor=y_device(way))

    def y_full(way, side):
        src = ys.at[2 + 2 * way + side]
        return remote(src, yr.at[way, side], y_ss.at[way, side], y_rs.at[way, side], tensor=y_device(way))

    def join(buffer, i):
        to_core(buffer, i).wait_recv()
        ys[i] = (buffer[i].astype(F32) + cr[i].astype(F32)).astype(BF)
        if i < 2:
            for way in range(2):
                y_half(way, i).start()

    def y_second():
        for way in range(2):
            for side in range(2):
                y_half(way, side).wait_recv()
                add_rows(ys.at[2 + 2 * way + side, pl.ds(way * HB, HB), :], yh.at[way, side])
                y_full(way, side).start()

    def parts(buffer, part, sums, lo, hi):
        for i in range(lo, hi):
            buffer[i] = term(feature(i), part).astype(BF)

            @pl.when(sums)
            def _(i=i):
                if i > 0:
                    join(buffer, i - 1)
                if i == NQ - 1:
                    join(buffer, i)

            @pl.when(jnp.logical_not(sums))
            def _(i=i):
                to_core(buffer, i).start()

    def y_sum(which):
        total = ys[6 + which].astype(F32)
        for way in range(2):
            total = total + yr[way, which].astype(F32)
        return total

    swap = remote(fs.at[0], fv.at[0], xh_ss, xh_rs, tensor=((1 - xh) * NY + y) * 2 + core)

    def y_third():
        for way in range(2):
            for side in range(2):
                y_full(way, side).wait_recv()
        fs[0] = y_sum(1 - xh).astype(BF)
        swap.start()
        ng[...] = y_sum(xh)

    def home(which):
        there = (xh * (1 - which) + (1 - xh) * which) * NY + y
        return remote(
            fs.at[which], fv.at[which], fs_ss.at[which], fs_rs.at[which], dp=other, tensor=there * 2 + 1 - core
        )

    def y_home():
        for way in range(2):
            for side in range(2):
                y_full(way, side).wait_recv()
        for which in range(2):
            fs[which] = y_sum(xh * (1 - which) + (1 - xh) * which).astype(BF)
            home(which).start()

    def x_last():
        swap.wait_recv()
        ng[...] = ng[...] + fv[0].astype(F32)

    away = jnp.logical_not(keeps)

    z4 = rem(z + 4, NZ)

    def complete(j, lo, hi):
        @pl.loop(lo, hi)
        def _(i):
            zs = rem(z4 + i, NZ)
            here = slice(j * 256, (j + 1) * 256)
            con[zs, j] = (con[zs, j].astype(F32) + dot(no[zs], qo[:, here])).astype(BF)

    def open_ring(j):
        swap_grad(j).wait_recv()
        complete(j, 0, 1)
        ring(j, 1)

    def ring(j, s):
        for way, to in ways:
            if s == 1:
                half = con.at[z4, j, pl.ds(way * HB, HB), :]
                go(remote(half, rb1.at[j, way], r1_ss.at[j, way], r1_rs.at[j, way], dp=to))
                continue
            zs = rem(z + (5 - s if way == 0 else NZ + s - 5), NZ)
            if s == 2:
                remote(rb1.at[j, way], rb1.at[j, way], r1_ss.at[j, way], r1_rs.at[j, way], dp=to).wait_recv()
                add_rows(con.at[zs, j, pl.ds(way * HB, HB), :], rb1.at[j, way])
            else:
                slot = rb.at[j, way, s - 3]
                remote(slot, slot, r_ss.at[j, way, s - 3], r_rs.at[j, way, s - 3], dp=to).wait_recv()
                add_rows(con.at[zs, j], slot)
            if s < 5:
                slot = rb.at[j, way, s - 2]
                go(remote(con.at[zs, j], slot, r_ss.at[j, way, s - 2], r_rs.at[j, way, s - 2], dp=to))
        if s == 5:
            gq[j] = con[z, j].astype(F32) * (1.0 / NR)

    sum_t.drain()
    cg_part[...] = dot(attn[...], folded[...]).astype(BF)
    sum_t2 = Sum("tensor", cg_part, code, t2)
    sum_t2.first()
    turn(0, qg)
    parts(po, 0, keeps, 0, 2)
    open_ring(2)
    complete(2, 1, NZ)
    sum_d.drain()
    fo_part[...] = dot_tn(attn[...], cg[...]).astype(BF)
    sum_d2 = Sum("dp", fo_part, mixing, d2)
    sum_d2.first()
    parts(po, 0, keeps, 2, 5)
    sum_t2.second()
    ring(2, 2)
    parts(po, 0, keeps, 5, NQ)
    contribute(0)
    open_ring(0)
    complete(0, 1, NZ)
    ring(2, 3)

    @pl.when(keeps)
    def _():
        y_second()

    sum_t2.third()
    contribute(1)
    open_ring(1)
    ring(0, 2)
    turn(1, qo)
    parts(px, 1, away, 0, 4)
    complete(1, 1, NZ)
    ring(2, 4)
    parts(px, 1, away, 4, NQ)
    ring(0, 3)
    ring(1, 2)

    @pl.when(away)
    def _():
        y_second()

    @pl.when(keeps)
    def _():
        y_third()

    sum_t2.across()
    sum_d2.second()
    ring(2, 5)
    ring(0, 4)

    @pl.when(away)
    def _():
        y_home()

    @pl.when(keeps)
    def _():
        x_last()

    ring(1, 3)
    sum_t2.fourth()
    sum_d2.third()
    ring(0, 5)

    @pl.when(away)
    def _():
        for which in range(2):
            home(which).wait_recv()
        ng[...] = fv[0].astype(F32) + fv[1].astype(F32)

    grad = ng[...]
    scaled = grad * gcol[:, 0:1]
    lt[tensor, 0:1, :] = jnp.sum(scaled, axis=0, keepdims=True)
    lt[tensor, 1:2, :] = jnp.sum(scaled * hat[...], axis=0, keepdims=True)
    slot = lt.at[tensor]
    for k in range(1, NR):
        go(remote(slot, slot, lt_ss.at[k], lt_rs.at[k], tensor=rem(tensor + k, NR)))

    def fold(v):
        v = v[:, 0:128] + v[:, 128:256] + v[:, 256:384] + v[:, 384:512]
        v = jnp.concatenate([v, jnp.zeros((64, 128), F32)], axis=0)
        return jnp.sum(v.T, axis=0, keepdims=True)

    gs[dp, 0:1, :] = fold(ng[...] * hat[...])
    gs[dp, 1:2, :] = fold(ng[...])
    slot = gs.at[dp]
    for k in range(1, NR):
        go(remote(slot, slot, gs_ss.at[k], gs_rs.at[k], dp=rem(dp + k, NR)))
    ring(1, 4)
    sum_t2.last()
    ro_t[...] = (xt[mine_rows, :].astype(F32) + dot_nt(dect[...], code[...])).astype(BF)

    for k in range(1, NR):
        slot = lt.at[rem(tensor + NR - k, NR)]
        remote(slot, slot, lt_ss.at[k], lt_rs.at[k], tensor=tensor).wait_recv()
    sums = jnp.sum(lt[...], axis=0)
    lead, trail = sums[0:1, :] * (1.0 / D), sums[1:2, :] * (1.0 / D)
    scaled = ng[...] * gcol[:, 0:1]
    gi_t[...] = (got[...].astype(F32) + st[0:1, :] * (scaled - lead - hat[...] * trail)).astype(BF)
    sum_d2.fourth()
    ring(1, 5)
    sum_d2.last()
    gow_t[...] = dot_nt(enc[...], mixing[...]) * (1.0 / NR)
    for k in range(1, NR):
        slot = gs.at[rem(dp + NR - k, NR)]
        remote(slot, slot, gs_ss.at[k], gs_rs.at[k], dp=dp).wait_recv()
    gb[...] = jnp.sum(gs[...], axis=0) * (1.0 / NR)

    for total in (sum_t2, sum_d2):
        total.drain()
    for copy in sent:
        copy.wait_send()

    @pl.when(keeps)
    def _():
        swap.wait_send()

    @pl.when(away)
    def _():
        for which in range(2):
            home(which).wait_send()

    @pl.loop(0, NQ)
    def _(i):
        to_core(po, i).wait_send()

    for way in range(2):
        for side in range(2):
            y_half(way, side).wait_send()
            y_full(way, side).wait_send()


def sublayer(*args):
    def shape(dims, kind):
        return jax.ShapeDtypeStruct(dims, kind)

    def v(kind, *dims):
        return pltpu.VMEM(dims, kind)

    one = pltpu.SemaphoreType.DMA
    whole = pl.BlockSpec(memory_space=pltpu.VMEM)
    far = pl.BlockSpec(memory_space=pl.ANY)
    scratch = [
        v(BF, SEQ, D), v(BF, 3, NZ * BLK, 256), v(BF, 2, NZ, BLK, SEQ), v(BF, NZ, BLK, SEQ), v(F32, 2, W3, SEQ),
        v(F32, SEQ, 128), v(F32, SEQ, 128), v(BF, SLAB, SEQ), v(F32, BLK, 128), v(F32, BLK, SEQ), v(F32, 8, SEQ),
        v(BF, SEQ, C), v(BF, 256, C), v(BF, SEQ, C), v(BF, 256, C), v(BF, W3, SEQ), v(BF, W3, SEQ),
        v(BF, SEQ, W3), v(BF, SEQ, 256), v(BF, SEQ, 256), v(BF, SEQ, W3), v(BF, SEQ, W3), v(BF, 2, W3, SEQ),
        v(F32, SEQ, 512),
        v(BF, NZ, 3, BLK, 256), v(BF, 3, 2, HB, 256), v(BF, 3, 2, 3, BLK, 256),
        v(BF, NQ, BLK, SEQ), v(BF, NQ, BLK, SEQ), v(BF, NQ, BLK, SEQ), v(BF, NQ, BLK, SEQ), v(BF, 2, 2, HB, SEQ), v(BF, 2, 2, BLK, SEQ),
        v(BF, 2, BLK, SEQ), v(BF, 2, BLK, SEQ), v(F32, BLK, SEQ),
        v(F32, NR, 8, SEQ), v(F32, NR, 8, 384), v(BF, SEQ, C), v(BF, 256, C),
        sum_buffers(SEQ, NY), sum_buffers(256, NZ), sum_buffers(SEQ, NY), sum_buffers(256, NZ),
        dma(4), one, dma(2, 3, 4), dma(2, 3, 4), dma(4), dma(4), dma(3, 4), dma(3, 4), dma(4, 4), dma(4, 4), dma(3), dma(3), dma(3), dma(3),
        dma(3, 2), dma(3, 2), dma(3, 2, 3), dma(3, 2, 3), dma(NQ), dma(NQ), dma(2, 2), dma(2, 2), dma(2, 2), dma(2, 2), one, one, dma(2), dma(2),
        dma(NR), dma(NR), dma(NR), dma(NR),
    ]
    return pl.pallas_call(
        kernel,
        out_shape=[
            shape((BLK, SEQ), BF),
            shape((BLK, SEQ), BF),
            shape((3, BLK, 256), F32),
            shape((BLK, 256), F32),
            shape((8, 384), F32),
        ],
        in_specs=[far, whole, whole, far, whole, whole, whole, whole],
        out_specs=[whole] * 5,
        scratch_shapes=scratch,
        compiler_params=pltpu.CompilerParams(
            collective_id=0, has_side_effects=True, vmem_limit_bytes=62 * 2**20
        ),
    )(*args)


def place_kernel(*refs):
    n = len(refs) // 2
    *refs, sems = refs
    copies = [pltpu.make_async_copy(refs[i], refs[n + i], sems.at[i]) for i in range(n)]
    for copy in copies:
        copy.start()
    for copy in copies:
        copy.wait()


def place(*arrays):
    far = pl.BlockSpec(memory_space=pl.ANY)
    return pl.pallas_call(
        place_kernel,
        out_shape=[jax.ShapeDtypeStruct(a.shape, a.dtype) for a in arrays],
        in_specs=[pl.BlockSpec(memory_space=pltpu.VMEM)] * len(arrays),
        out_specs=[far] * len(arrays),
        scratch_shapes=[dma(len(arrays))],
    )(*arrays)


def local(
    residual_in,
    layernorm_gain,
    layernorm_bias,
    qkv_weight,
    out_weight,
    encoder,
    decoder,
    grad_output,
):
    residual_out, grad_input, grad_qkv, grad_out_weight, sums = sublayer(
        residual_in,
        layernorm_gain[None, :],
        layernorm_bias[None, :],
        qkv_weight,
        out_weight.T,
        encoder,
        decoder.T,
        grad_output.T,
    )
    residual_out, grad_input, grad_qkv, grad_out_weight = place(
        residual_out, grad_input, grad_qkv, grad_out_weight
    )
    return residual_out.T, grad_input.T, grad_qkv, grad_out_weight.T, sums[0, :BLK], sums[1, :BLK]


def solution(mesh):
    in_specs = (
        P("dp", None),
        P(),
        P(),
        P(None, "dp", "tensor"),
        P("tensor", "dp"),
        P("dp", None),
        P(None, "tensor"),
        P("dp", "tensor"),
    )
    out_specs = (
        P("dp", "tensor"),
        P("dp", "tensor"),
        P(None, "dp", "tensor"),
        P("tensor", "dp"),
        P("tensor"),
        P("tensor"),
    )
    return jax.shard_map(local, mesh=mesh, in_specs=in_specs, out_specs=out_specs, check_vma=False)
```

```python
import functools
from collections import deque

import jax
import jax.numpy as jnp
from jax import lax
from jax.experimental import pallas as pl
from jax.experimental.pallas import tpu as pltpu
from jax.sharding import PartitionSpec as P

HDIM = 128
EPS = 1e-05
MESH = pl.DeviceIdType.MESH
F32, BF = jnp.float32, jnp.bfloat16

NZ, NY, NQ, NR = 8, 4, 8, 16
SEQ, D, C, W3 = 512, 5120, 640, 768
BLK = 320
SLAB = 640
HB = BLK // 2


def rem(a, n):
    return lax.rem(a, n)


def rows(start, size):
    return pl.ds(pl.multiple_of(start, 16), size)


def dot(a, b):
    return lax.dot_general(a, b, (((1,), (0,)), ((), ())), preferred_element_type=F32)


def dot_nt(a, b):
    return lax.dot_general(a, b, (((1,), (1,)), ((), ())), preferred_element_type=F32)


def dot_tn(a, b):
    return lax.dot_general(a, b, (((0,), (0,)), ((), ())), preferred_element_type=F32)


def remote(src, dst, ssem, rsem, **device):
    return pltpu.make_async_remote_copy(
        src_ref=src, dst_ref=dst, send_sem=ssem, recv_sem=rsem, device_id=device, device_id_type=MESH
    )


def enter():
    barrier = pltpu.get_barrier_semaphore()
    for axis in ("dp", "tensor"):
        me = lax.axis_index(axis)
        for k in range(1, NR):
            pl.semaphore_signal(barrier, inc=1, device_id={axis: rem(me + k, NR)}, device_id_type=MESH)
    dp, tensor = lax.axis_index("dp"), lax.axis_index("tensor")
    flip = tensor + 1 - 2 * rem(tensor, 2)
    for there in (flip, rem(flip + 8, NR)):
        across = {"dp": dp + 1 - 2 * rem(dp, 2), "tensor": there}
        pl.semaphore_signal(barrier, inc=1, device_id=across, device_id_type=MESH)
    pl.semaphore_wait(barrier, 2 * NR)


class Sum:
    def __init__(self, axis, part, out, buffers):
        self.axis, self.part, self.out = axis, part, out
        self.got, self.half, self.ring, self.mid, self.mid_got, self.ssem, self.rsem = buffers
        index = lax.axis_index(axis)
        self.n = self.ring.shape[0]
        self.a = rem(index, 2)
        self.q = rem(index // 2, self.n)
        self.top = index // (2 * self.n)
        self.h = part.shape[0] // 2
        self.b = self.h // self.n
        self.sent = []

    def at(self, top, q, a):
        return {self.axis: (top * self.n + q) * 2 + a}

    def pair(self):
        return self.at(self.top, self.q, 1 - self.a)

    def peer(self, k):
        return self.at(self.top, rem(self.q + k, self.n), self.a)

    def over(self):
        return self.at(1 - self.top, self.q, self.a)

    def go(self, copy):
        copy.start()
        self.sent.append(copy)

    def first(self):
        src = self.part.at[rows((1 - self.a) * self.h, self.h), :]
        self.go(remote(src, self.got, self.ssem.at[0], self.rsem.at[0], **self.pair()))

    def second(self):
        remote(self.got, self.got, self.ssem.at[0], self.rsem.at[0], **self.pair()).wait_recv()
        mine = self.part[rows(self.a * self.h, self.h), :].astype(F32)
        self.half[...] = (mine + self.got[...].astype(F32)).astype(BF)
        for k in range(1, self.n):
            to = rem(self.q + k, self.n)
            src = self.half.at[rows(to * self.b, self.b), :]
            self.go(remote(src, self.ring.at[self.q], self.ssem.at[k], self.rsem.at[k], **self.peer(k)))

    def reduced(self):
        total = self.half[rows(self.q * self.b, self.b), :].astype(F32)
        for k in range(1, self.n):
            source = rem(self.q + self.n - k, self.n)
            slot = self.ring.at[source]
            remote(slot, slot, self.ssem.at[k], self.rsem.at[k], **self.peer(k)).wait_recv()
            total = total + self.ring[source].astype(F32)
        return total

    def spread(self, total):
        here = rows(self.a * self.h + self.q * self.b, self.b)
        self.out[here, :] = total.astype(BF)
        piece = self.out.at[here, :]
        for k in range(1, self.n):
            self.go(remote(piece, piece, self.ssem.at[7 + k], self.rsem.at[7 + k], **self.peer(k)))

    def third(self):
        if self.mid is None:
            self.spread(self.reduced())
        else:
            self.mid[...] = self.reduced().astype(BF)
            self.go(remote(self.mid, self.mid_got, self.ssem.at[16], self.rsem.at[16], **self.over()))

    def across(self):
        remote(self.mid, self.mid_got, self.ssem.at[16], self.rsem.at[16], **self.over()).wait_recv()
        self.spread(self.mid[...].astype(F32) + self.mid_got[...].astype(F32))

    def fourth(self):
        for k in range(1, self.n):
            source = rem(self.q + self.n - k, self.n)
            piece = self.out.at[rows(self.a * self.h + source * self.b, self.b), :]
            remote(piece, piece, self.ssem.at[7 + k], self.rsem.at[7 + k], **self.peer(k)).wait_recv()
        mine = self.out.at[rows(self.a * self.h, self.h), :]
        self.go(remote(mine, mine, self.ssem.at[15], self.rsem.at[15], **self.pair()))

    def last(self):
        other = self.out.at[rows((1 - self.a) * self.h, self.h), :]
        remote(other, other, self.ssem.at[15], self.rsem.at[15], **self.pair()).wait_recv()

    def drain(self):
        for copy in self.sent:
            copy.wait_send()


def dma(*shape):
    return pltpu.SemaphoreType.DMA(shape)


def sum_buffers(r, n):
    h = r // 2
    cut = pltpu.VMEM((h // n, C), BF)
    mids = [cut, cut] if n == NY else [None, None]
    return [pltpu.VMEM((h, C), BF), pltpu.VMEM((h, C), BF), pltpu.VMEM((n, h // n, C), BF)] + mids + [dma(17), dma(17)]


def add_rows(dst, src):
    @pl.loop(0, dst.shape[0] // 80)
    def _(i):
        here = rows(i * 80, 80)
        dst[here, :] = (dst[here, :].astype(F32) + src[here, :].astype(F32)).astype(BF)


def kernel(
    x_hbm, gain, bias, w_in, owt, enc, dect, got,
    ro_t, gi_t, gq, gow_t, gb,
    x, w, nb, no, acc, mu, rstd, xt, gcol, hat, st,
    cg_part, fo_part, cg, folded, ps, pr, qkv, ag, attn, qg, qo, qgt, dkv,
    con, rb1, rb, po, px, cr, ys, yh, yr, fs, fv, ng, lt, gs, code, mixing,
    t1, d1, t2, d2,
    x_sem, loc, a_ss, a_rs, n_ss, n_rs, g_ss, g_rs, f_ss, f_rs, p_ss, p_rs, q_ss, q_rs,
    r1_ss, r1_rs, r_ss, r_rs, cs_ss, cs_rs, yh_ss, yh_rs, y_ss, y_rs, xh_ss, xh_rs, fs_ss, fs_rs, lt_ss, lt_rs, gs_ss, gs_rs,
):
    dp, tensor = lax.axis_index("dp"), lax.axis_index("tensor")
    z, xl = dp // 2, rem(dp, 2)
    up, down = rem(z + 1, NZ) * 2 + xl, rem(z + NZ - 1, NZ) * 2 + xl
    other = z * 2 + 1 - xl
    core, q = rem(tensor, 2), tensor // 2
    xh, y = q // NY, rem(q, NY)
    sibling = q * 2 + 1 - core
    ways = ((0, up), (1, down))
    sent = []

    def go(copy):
        copy.start()
        sent.append(copy)

    x_copies = [
        pltpu.make_async_copy(x_hbm.at[pl.ds(i * 128, 128), :], x.at[pl.ds(i * 128, 128), :], x_sem.at[i])
        for i in range(4)
    ]
    for copy in x_copies:
        copy.start()
    enter()

    def block(j, zs, offset=0, size=BLK):
        return w.at[j, rows(zs * BLK + offset, size), :]

    mine = pltpu.make_async_copy(w_in, w.at[:, rows(z * BLK, BLK), :], loc)
    mine.start()

    def send_own(j):
        for way, to in ways:
            go(remote(w_in.at[j], block(j, z), a_ss.at[way, j, 0], a_rs.at[way, j, 0], dp=to))

    def relay(j, s):
        for way, to in ways:
            zs = rem(z + (NZ - s if way == 0 else s), NZ)
            if s < 4:
                part = block(j, zs)
                remote(part, part, a_ss.at[way, j, s - 1], a_rs.at[way, j, s - 1], dp=to).wait_recv()
                if s == 3:
                    part = block(j, zs, way * HB, HB)
                go(remote(part, part, a_ss.at[way, j, s], a_rs.at[way, j, s], dp=to))
            else:
                part = block(j, zs, way * HB, HB)
                remote(part, part, a_ss.at[way, j, 3], a_rs.at[way, j, 3], dp=to).wait_recv()

    send_own(0)
    send_own(1)
    sum_d = Sum("dp", fo_part, folded, d1)
    sum_t = Sum("tensor", cg_part, cg, t1)

    def start_folded():
        fo_part[...] = dot_tn(owt[...], enc[...]).astype(BF)
        sum_d.first()

    def start_code_grad():
        cg_part[...] = dot_tn(got[...], dect[...]).astype(BF)
        sum_t.first()

    def slab_cols(zs):
        return pl.ds(pl.multiple_of(zs * SLAB, 128), SLAB)

    def near(i):
        odd = rem(i, 2)
        return rem(z + odd * ((i + 1) // 2) + (1 - odd) * (NZ - i // 2), NZ)

    def tokens(r):
        return pl.ds(r * 128, 128)

    def piece(k, c, r):
        return no.at[near(2 * k + c), :, tokens(r)]

    def cross(r):
        src = nb.at[1, near(2 * y + core), :, tokens(r)]
        return remote(src, piece(y, core, r), n_ss.at[r], n_rs.at[r], dp=other)

    def along(k, r):
        part = piece(y, core, r)
        there = (xh * NY + rem(y + k, NY)) * 2 + core
        return remote(part, part, g_ss.at[k - 1, r], g_rs.at[k - 1, r], tensor=there)

    def pass_on(k, r):
        part = piece(rem(y + NY - k, NY), core, r)
        return remote(part, part, f_ss.at[k, r], f_rs.at[k, r], tensor=sibling)

    def norm(r, lo, hi):
        if lo == 0:
            x_copies[r].wait()
            xt[:, r * 128 : (r + 1) * 128] = x[r * 128 : (r + 1) * 128, slab_cols(q)].T

        @pl.loop(lo, hi)
        def _(i):
            here = rows(r * 128 + i * 16, 16)
            v = x[here, :].astype(F32)
            mean = jnp.sum(v, axis=1, keepdims=True) * (1.0 / D)
            v = v - mean
            var = jnp.sum(v * v, axis=1, keepdims=True) * (1.0 / D)
            scale = lax.rsqrt(var + EPS)
            mu[here, :] = jnp.broadcast_to(mean, (16, 128))
            rstd[here, :] = jnp.broadcast_to(scale, (16, 128))
            x[here, :] = (v * scale * gain[...] + bias[...]).astype(BF)

    def spread(r):
        @pl.loop(0, NZ)
        def _(zs):
            v = x[r * 128 : (r + 1) * 128, slab_cols(zs)].T
            nb[xl, zs, :, r * 128 : (r + 1) * 128] = v[0:BLK]
            nb[1 - xl, zs, :, r * 128 : (r + 1) * 128] = v[BLK:SLAB]

        go(cross(r))

    def forward_on(r):
        cross(r).wait_recv()
        for k in (2, 1, 3):
            go(along(k, r))
        go(pass_on(0, r))

    def share(r):
        for k in (1, 3, 2):
            part = piece(rem(y + NY - k, NY), core, r)
            remote(part, part, g_ss.at[k - 1, r], g_rs.at[k - 1, r], tensor=sibling).wait_recv()
            go(pass_on(k, r))

    def use(j, i, part):
        zs = near(i)
        here = slice(j * 256, (j + 1) * 256)
        source = nb.at[0, zs] if part == 0 else no.at[zs]
        acc[part, here, :] += dot_tn(block(j, zs)[...], source[...])

    def use_all(j, lo, hi, part):
        @pl.loop(lo, hi)
        def _(i):
            use(j, i, part)

    def partial(j):
        here = pl.ds(j * 256, 256)
        return remote(ps.at[here, :], pr.at[here, :], p_ss.at[j], p_rs.at[j], dp=other)

    def give(j):
        here = slice(j * 256, (j + 1) * 256)
        ps[here, :] = acc[1, here, :].astype(BF)
        go(partial(j))

    def take(j):
        here = slice(j * 256, (j + 1) * 256)
        partial(j).wait_recv()
        qkv[:, here] = (acc[0, here, :] + pr[here, :].astype(F32)).astype(BF).T

    def collect():
        for r in range(4):
            for k in range(4):
                part = piece(rem(y + NY - k, NY), 1 - core, r)
                remote(part, part, f_ss.at[k, r], f_rs.at[k, r], tensor=sibling).wait_recv()

    work = deque()

    def add(cost, f, *args):
        work.append((cost, f, args))

    def run():
        cost, f, args = work.popleft()
        f(*args)
        return cost

    def ahead(f, *args):
        while any(piece[1:] == (f, args) for piece in work):
            run()

    def clear():
        acc[...] = jnp.zeros_like(acc)

    def relay_use(j, s):
        relay(j, s)
        lo, hi = (7, 8) if s == 4 else (2 * s - 1, 2 * s + 1)
        add(0.33 * (hi - lo), use_all, j, lo, hi, 0)

    def own_use():
        mine.wait()
        for j in range(3):
            add(0.33, use_all, j, 0, 1, 0)

    def far_use(j):
        use_all(j, 0, 8, 1)
        give(j)

    def far_begin():
        use_all(2, 0, 7, 1)

    def far_end():
        use_all(2, 7, 8, 1)
        give(2)

    add(1.2, start_folded)
    for r in range(4):
        add(1.3, norm, r, 0, 4)
        add(1.3, norm, r, 4, 8)
        add(1.1, spread, r)
        if r == 0:
            add(0.8, clear)
        if r == 2:
            add(1.5, start_code_grad)
    events = [
        (5.0, relay_use, 0, 1),
        (7.0, sum_d.second),
        (8.3, forward_on, 0),
        (8.5, relay_use, 1, 1),
        (12.0, relay_use, 0, 2),
        (13.0, forward_on, 1),
        (13.2, share, 0),
        (15.5, relay_use, 1, 2),
        (15.6, send_own, 2),
        (17.0, forward_on, 2),
        (17.2, share, 1),
        (19.0, relay_use, 0, 3),
        (19.5, sum_d.third),
        (20.5, forward_on, 3),
        (21.0, own_use),
        (21.5, share, 2),
        (21.5, sum_t.second),
        (24.0, relay_use, 2, 1),
        (25.0, share, 3),
        (25.5, sum_t.third),
        (27.0, relay_use, 1, 3),
        (27.5, collect),
        (29.0, relay_use, 0, 4),
        (29.5, far_use, 0),
        (31.0, sum_d.fourth),
        (31.5, sum_t.across),
        (33.0, relay_use, 2, 2),
        (35.0, relay_use, 1, 4),
        (35.5, far_use, 1),
        (38.5, sum_t.fourth),
        (39.0, relay_use, 2, 3),
        (39.5, far_begin),
        (42.5, sum_t.last),
        (43.0, relay_use, 2, 4),
        (43.0, far_end),
    ]
    now = 0.0
    for when, f, *args in events:
        while work and now + work[0][0] <= when + 0.3:
            now += run()
        if f is forward_on:
            ahead(spread, *args)
        elif f == sum_d.second:
            ahead(start_folded)
        elif f == sum_t.second:
            ahead(start_code_grad)
        f(*args)
        now = max(now, when) + (2.5 if f in (far_use, far_begin) else 0.2)
    while work:
        run()
    mine_rows = rows(core * BLK, BLK)
    rs_row = rstd[...].T[0:1, :]
    hat[...] = (xt[mine_rows, :].astype(F32) - mu[...].T[0:1, :]) * rs_row
    st[0:1, :] = rs_row
    turned = jnp.broadcast_to(gain[0:1, slab_cols(q)], (128, SLAB)).T
    gcol[...] = jnp.where(core == 0, turned[0:BLK], turned[BLK:SLAB])
    dkv[...] = jnp.zeros_like(dkv)
    take(0)
    take(1)

    rate = HDIM**-0.5
    blocks = [(h, r) for h in range(2) for r in range(4)]

    def cut(h, r):
        return slice(h * HDIM, (h + 1) * HDIM), slice(r * 128, (r + 1) * 128), 128 * (r + 1)

    def columns(j, h):
        return slice(j * 256 + h * HDIM, j * 256 + (h + 1) * HDIM)

    for h, r in blocks:
        _, here, n = cut(h, r)
        s = dot_nt(qkv[here, columns(0, h)], qkv[0:n, columns(1, h)]) * rate
        at_row = lax.broadcasted_iota(jnp.int32, (128, n), 0) + r * 128
        at_col = lax.broadcasted_iota(jnp.int32, (128, n), 1)
        s = jnp.where(at_col <= at_row, s, -1e30)
        e = jnp.exp(s - jnp.max(s, axis=1, keepdims=True))
        acc[h, here, 0:n] = e * (1.0 / jnp.sum(e, axis=1, keepdims=True))
    sum_d.last()
    ag[...] = dot_nt(cg[...], folded[...]).astype(BF)
    for h, r in blocks:
        cq, here, n = cut(h, r)
        dkv[0:n, columns(1, h)] += dot_tn(acc[h, here, 0:n].astype(BF), ag[here, cq])
    qg[:, 512:768] = dkv[:, 256:512].astype(BF)

    def swap_grad(j):
        here = pl.ds(j * 256, 256)
        return remote(qg.at[:, here], qo.at[:, here], q_ss.at[j], q_rs.at[j], dp=other)

    go(swap_grad(2))

    def contribute(j):
        @pl.loop(0, NZ)
        def _(zs):
            con[zs, j] = dot(nb[0, zs], qg[:, j * 256 : (j + 1) * 256]).astype(BF)

    contribute(2)
    take(2)
    for h, r in blocks:
        cq, here, n = cut(h, r)
        p, vb = acc[h, here, 0:n], qkv[0:n, columns(2, h)]
        attn[here, cq] = dot(p.astype(BF), vb).astype(BF)
        dpr = dot_nt(ag[here, cq], vb).astype(BF).astype(F32)
        ds = p * (dpr - jnp.sum(p * dpr, axis=1, keepdims=True))
        ds = (ds * rate).astype(BF)
        qg[here, cq] = dot(ds, qkv[0:n, columns(1, h)]).astype(BF)
        dkv[0:n, cq] += dot_tn(ds, qkv[here, columns(0, h)])
    go(swap_grad(0))
    qg[:, 256:512] = dkv[:, 0:256].astype(BF)
    go(swap_grad(1))

    def turn(part, source):
        @pl.loop(0, 6)
        def _(i):
            here = pl.ds(pl.multiple_of(i * 128, 128), 128)
            qgt[part, here, :] = source[:, here].T

    def term(zs, part):
        here = rows(zs * BLK, BLK)
        out = dot(w[0, here, :], qgt[part, 0:256, :])
        out = out + dot(w[1, here, :], qgt[part, 256:512, :])
        return out + dot(w[2, here, :], qgt[part, 512:768, :])

    def feature(i):
        return i % 2 * NY + rem(y + (2, 1, 3, 0)[i // 2], NY)

    keeps = core == xl

    def to_core(buffer, i):
        return remote(buffer.at[i], cr.at[i], cs_ss.at[i], cs_rs.at[i], tensor=sibling)

    def y_device(way):
        return (xh * NY + rem(y + 1 + 2 * way, NY)) * 2 + core

    def y_half(way, side):
        src = ys.at[side, pl.ds(way * HB, HB), :]
        return remote(src, yh.at[way, side], yh_ss.at[way, side], yh_rs.at[way, side], tensor=y_device(way))

    def y_full(way, side):
        src = ys.at[2 + 2 * way + side]
        return remote(src, yr.at[way, side], y_ss.at[way, side], y_rs.at[way, side], tensor=y_device(way))

    def join(buffer, i):
        to_core(buffer, i).wait_recv()
        ys[i] = (buffer[i].astype(F32) + cr[i].astype(F32)).astype(BF)
        if i < 2:
            for way in range(2):
                y_half(way, i).start()

    def y_second():
        for way in range(2):
            for side in range(2):
                y_half(way, side).wait_recv()
                add_rows(ys.at[2 + 2 * way + side, pl.ds(way * HB, HB), :], yh.at[way, side])
                y_full(way, side).start()

    def parts(buffer, part, sums, lo, hi):
        for i in range(lo, hi):
            buffer[i] = term(feature(i), part).astype(BF)

            @pl.when(sums)
            def _(i=i):
                if i > 0:
                    join(buffer, i - 1)
                if i == NQ - 1:
                    join(buffer, i)

            @pl.when(jnp.logical_not(sums))
            def _(i=i):
                to_core(buffer, i).start()

    def y_sum(which):
        total = ys[6 + which].astype(F32)
        for way in range(2):
            total = total + yr[way, which].astype(F32)
        return total

    swap = remote(fs.at[0], fv.at[0], xh_ss, xh_rs, tensor=((1 - xh) * NY + y) * 2 + core)

    def y_third():
        for way in range(2):
            for side in range(2):
                y_full(way, side).wait_recv()
        fs[0] = y_sum(1 - xh).astype(BF)
        swap.start()
        ng[...] = y_sum(xh)

    def home(which):
        there = (xh * (1 - which) + (1 - xh) * which) * NY + y
        return remote(
            fs.at[which], fv.at[which], fs_ss.at[which], fs_rs.at[which], dp=other, tensor=there * 2 + 1 - core
        )

    def y_home():
        for way in range(2):
            for side in range(2):
                y_full(way, side).wait_recv()
        for which in range(2):
            fs[which] = y_sum(xh * (1 - which) + (1 - xh) * which).astype(BF)
            home(which).start()

    def x_last():
        swap.wait_recv()
        ng[...] = ng[...] + fv[0].astype(F32)

    away = jnp.logical_not(keeps)

    z4 = rem(z + 4, NZ)

    def complete(j, lo, hi):
        @pl.loop(lo, hi)
        def _(i):
            zs = rem(z4 + i, NZ)
            here = slice(j * 256, (j + 1) * 256)
            con[zs, j] = (con[zs, j].astype(F32) + dot(no[zs], qo[:, here])).astype(BF)

    def open_ring(j):
        swap_grad(j).wait_recv()
        complete(j, 0, 1)
        ring(j, 1)

    def ring(j, s):
        for way, to in ways:
            if s == 1:
                half = con.at[z4, j, pl.ds(way * HB, HB), :]
                go(remote(half, rb1.at[j, way], r1_ss.at[j, way], r1_rs.at[j, way], dp=to))
                continue
            zs = rem(z + (5 - s if way == 0 else NZ + s - 5), NZ)
            if s == 2:
                remote(rb1.at[j, way], rb1.at[j, way], r1_ss.at[j, way], r1_rs.at[j, way], dp=to).wait_recv()
                add_rows(con.at[zs, j, pl.ds(way * HB, HB), :], rb1.at[j, way])
            else:
                slot = rb.at[j, way, s - 3]
                remote(slot, slot, r_ss.at[j, way, s - 3], r_rs.at[j, way, s - 3], dp=to).wait_recv()
                add_rows(con.at[zs, j], slot)
            if s < 5:
                slot = rb.at[j, way, s - 2]
                go(remote(con.at[zs, j], slot, r_ss.at[j, way, s - 2], r_rs.at[j, way, s - 2], dp=to))
        if s == 5:
            gq[j] = con[z, j].astype(F32) * (1.0 / NR)

    sum_t.drain()
    cg_part[...] = dot(attn[...], folded[...]).astype(BF)
    sum_t2 = Sum("tensor", cg_part, code, t2)
    sum_t2.first()
    turn(0, qg)
    parts(po, 0, keeps, 0, 2)
    open_ring(2)
    complete(2, 1, NZ)
    sum_t2.second()
    sum_d.drain()
    fo_part[...] = dot_tn(attn[...], cg[...]).astype(BF)
    sum_d2 = Sum("dp", fo_part, mixing, d2)
    sum_d2.first()
    parts(po, 0, keeps, 2, 4)
    ring(2, 2)
    sum_t2.third()
    parts(po, 0, keeps, 4, 6)
    contribute(0)
    open_ring(0)
    parts(po, 0, keeps, 6, NQ)
    complete(0, 1, NZ)
    ring(2, 3)
    sum_t2.across()
    contribute(1)
    open_ring(1)
    ring(0, 2)
    turn(1, qo)
    parts(px, 1, away, 0, 2)

    @pl.when(keeps)
    def _():
        y_second()

    ring(2, 4)
    complete(1, 1, NZ)
    parts(px, 1, away, 2, 4)
    ring(0, 3)
    sum_t2.fourth()
    parts(px, 1, away, 4, 6)
    ring(1, 2)
    ring(2, 5)
    parts(px, 1, away, 6, NQ)

    @pl.when(away)
    def _():
        y_second()

    ring(0, 4)
    sum_d2.second()
    ring(1, 3)

    @pl.when(keeps)
    def _():
        y_third()

    ring(0, 5)
    ring(1, 4)

    @pl.when(away)
    def _():
        y_home()

    @pl.when(keeps)
    def _():
        x_last()

    sum_d2.third()
    ring(1, 5)

    @pl.when(away)
    def _():
        for which in range(2):
            home(which).wait_recv()
        ng[...] = fv[0].astype(F32) + fv[1].astype(F32)

    grad = ng[...]
    scaled = grad * gcol[:, 0:1]
    lt[tensor, 0:1, :] = jnp.sum(scaled, axis=0, keepdims=True)
    lt[tensor, 1:2, :] = jnp.sum(scaled * hat[...], axis=0, keepdims=True)
    slot = lt.at[tensor]
    for k in range(1, NR):
        go(remote(slot, slot, lt_ss.at[k], lt_rs.at[k], tensor=rem(tensor + k, NR)))

    def fold(v):
        v = v[:, 0:128] + v[:, 128:256] + v[:, 256:384] + v[:, 384:512]
        v = jnp.concatenate([v, jnp.zeros((64, 128), F32)], axis=0)
        return jnp.sum(v.T, axis=0, keepdims=True)

    gs[dp, 0:1, :] = fold(ng[...] * hat[...])
    gs[dp, 1:2, :] = fold(ng[...])
    slot = gs.at[dp]
    for k in range(1, NR):
        go(remote(slot, slot, gs_ss.at[k], gs_rs.at[k], dp=rem(dp + k, NR)))
    sum_d2.fourth()
    sum_t2.last()
    ro_t[...] = (xt[mine_rows, :].astype(F32) + dot_nt(dect[...], code[...])).astype(BF)

    for k in range(1, NR):
        slot = lt.at[rem(tensor + NR - k, NR)]
        remote(slot, slot, lt_ss.at[k], lt_rs.at[k], tensor=tensor).wait_recv()
    sums = jnp.sum(lt[...], axis=0)
    lead, trail = sums[0:1, :] * (1.0 / D), sums[1:2, :] * (1.0 / D)
    scaled = ng[...] * gcol[:, 0:1]
    gi_t[...] = (got[...].astype(F32) + st[0:1, :] * (scaled - lead - hat[...] * trail)).astype(BF)
    sum_d2.last()
    gow_t[...] = dot_nt(enc[...], mixing[...]) * (1.0 / NR)
    for k in range(1, NR):
        slot = gs.at[rem(dp + NR - k, NR)]
        remote(slot, slot, gs_ss.at[k], gs_rs.at[k], dp=dp).wait_recv()
    gb[...] = jnp.sum(gs[...], axis=0) * (1.0 / NR)

    for total in (sum_t2, sum_d2):
        total.drain()
    for copy in sent:
        copy.wait_send()

    @pl.when(keeps)
    def _():
        swap.wait_send()

    @pl.when(away)
    def _():
        for which in range(2):
            home(which).wait_send()

    @pl.loop(0, NQ)
    def _(i):
        to_core(po, i).wait_send()

    for way in range(2):
        for side in range(2):
            y_half(way, side).wait_send()
            y_full(way, side).wait_send()


def sublayer(*args):
    def shape(dims, kind):
        return jax.ShapeDtypeStruct(dims, kind)

    def v(kind, *dims):
        return pltpu.VMEM(dims, kind)

    one = pltpu.SemaphoreType.DMA
    whole = pl.BlockSpec(memory_space=pltpu.VMEM)
    far = pl.BlockSpec(memory_space=pl.ANY)
    scratch = [
        v(BF, SEQ, D), v(BF, 3, NZ * BLK, 256), v(BF, 2, NZ, BLK, SEQ), v(BF, NZ, BLK, SEQ), v(F32, 2, W3, SEQ),
        v(F32, SEQ, 128), v(F32, SEQ, 128), v(BF, SLAB, SEQ), v(F32, BLK, 128), v(F32, BLK, SEQ), v(F32, 8, SEQ),
        v(BF, SEQ, C), v(BF, 256, C), v(BF, SEQ, C), v(BF, 256, C), v(BF, W3, SEQ), v(BF, W3, SEQ),
        v(BF, SEQ, W3), v(BF, SEQ, 256), v(BF, SEQ, 256), v(BF, SEQ, W3), v(BF, SEQ, W3), v(BF, 2, W3, SEQ),
        v(F32, SEQ, 512),
        v(BF, NZ, 3, BLK, 256), v(BF, 3, 2, HB, 256), v(BF, 3, 2, 3, BLK, 256),
        v(BF, NQ, BLK, SEQ), v(BF, NQ, BLK, SEQ), v(BF, NQ, BLK, SEQ), v(BF, NQ, BLK, SEQ), v(BF, 2, 2, HB, SEQ), v(BF, 2, 2, BLK, SEQ),
        v(BF, 2, BLK, SEQ), v(BF, 2, BLK, SEQ), v(F32, BLK, SEQ),
        v(F32, NR, 8, SEQ), v(F32, NR, 8, 384), v(BF, SEQ, C), v(BF, 256, C),
        sum_buffers(SEQ, NY), sum_buffers(256, NZ), sum_buffers(SEQ, NY), sum_buffers(256, NZ),
        dma(4), one, dma(2, 3, 4), dma(2, 3, 4), dma(4), dma(4), dma(3, 4), dma(3, 4), dma(4, 4), dma(4, 4), dma(3), dma(3), dma(3), dma(3),
        dma(3, 2), dma(3, 2), dma(3, 2, 3), dma(3, 2, 3), dma(NQ), dma(NQ), dma(2, 2), dma(2, 2), dma(2, 2), dma(2, 2), one, one, dma(2), dma(2),
        dma(NR), dma(NR), dma(NR), dma(NR),
    ]
    return pl.pallas_call(
        kernel,
        out_shape=[
            shape((BLK, SEQ), BF),
            shape((BLK, SEQ), BF),
            shape((3, BLK, 256), F32),
            shape((BLK, 256), F32),
            shape((8, 384), F32),
        ],
        in_specs=[far, whole, whole, far, whole, whole, whole, whole],
        out_specs=[whole] * 5,
        scratch_shapes=scratch,
        compiler_params=pltpu.CompilerParams(
            collective_id=0, has_side_effects=True, vmem_limit_bytes=62 * 2**20
        ),
    )(*args)


def place_kernel(*refs):
    n = len(refs) // 2
    *refs, sems = refs
    copies = [pltpu.make_async_copy(refs[i], refs[n + i], sems.at[i]) for i in range(n)]
    for copy in copies:
        copy.start()
    for copy in copies:
        copy.wait()


def place(*arrays):
    far = pl.BlockSpec(memory_space=pl.ANY)
    return pl.pallas_call(
        place_kernel,
        out_shape=[jax.ShapeDtypeStruct(a.shape, a.dtype) for a in arrays],
        in_specs=[pl.BlockSpec(memory_space=pltpu.VMEM)] * len(arrays),
        out_specs=[far] * len(arrays),
        scratch_shapes=[dma(len(arrays))],
    )(*arrays)


def local(
    residual_in,
    layernorm_gain,
    layernorm_bias,
    qkv_weight,
    out_weight,
    encoder,
    decoder,
    grad_output,
):
    residual_out, grad_input, grad_qkv, grad_out_weight, sums = sublayer(
        residual_in,
        layernorm_gain[None, :],
        layernorm_bias[None, :],
        qkv_weight,
        out_weight.T,
        encoder,
        decoder.T,
        grad_output.T,
    )
    residual_out, grad_input, grad_qkv, grad_out_weight = place(
        residual_out, grad_input, grad_qkv, grad_out_weight
    )
    return residual_out.T, grad_input.T, grad_qkv, grad_out_weight.T, sums[0, :BLK], sums[1, :BLK]


def solution(mesh):
    in_specs = (
        P("dp", None),
        P(),
        P(),
        P(None, "dp", "tensor"),
        P("tensor", "dp"),
        P("dp", None),
        P(None, "tensor"),
        P("dp", "tensor"),
    )
    out_specs = (
        P("dp", "tensor"),
        P("dp", "tensor"),
        P(None, "dp", "tensor"),
        P("tensor", "dp"),
        P("tensor"),
        P("tensor"),
    )
    return jax.shard_map(local, mesh=mesh, in_specs=in_specs, out_specs=out_specs, check_vma=False)
```

```python
import functools
from collections import deque

import jax
import jax.numpy as jnp
from jax import lax
from jax.experimental import pallas as pl
from jax.experimental.pallas import tpu as pltpu
from jax.sharding import PartitionSpec as P

HDIM = 128
EPS = 1e-05
MESH = pl.DeviceIdType.MESH
F32, BF = jnp.float32, jnp.bfloat16

NZ, NY, NQ, NR = 8, 4, 8, 16
SEQ, D, C, W3 = 512, 5120, 640, 768
BLK = 320
SLAB = 640
HB = BLK // 2


def rem(a, n):
    return lax.rem(a, n)


def rows(start, size):
    return pl.ds(pl.multiple_of(start, 16), size)


def dot(a, b):
    return lax.dot_general(a, b, (((1,), (0,)), ((), ())), preferred_element_type=F32)


def dot_nt(a, b):
    return lax.dot_general(a, b, (((1,), (1,)), ((), ())), preferred_element_type=F32)


def dot_tn(a, b):
    return lax.dot_general(a, b, (((0,), (0,)), ((), ())), preferred_element_type=F32)


def remote(src, dst, ssem, rsem, **device):
    return pltpu.make_async_remote_copy(
        src_ref=src, dst_ref=dst, send_sem=ssem, recv_sem=rsem, device_id=device, device_id_type=MESH
    )


def enter():
    barrier = pltpu.get_barrier_semaphore()
    for axis in ("dp", "tensor"):
        me = lax.axis_index(axis)
        for k in range(1, NR):
            pl.semaphore_signal(barrier, inc=1, device_id={axis: rem(me + k, NR)}, device_id_type=MESH)
    dp, tensor = lax.axis_index("dp"), lax.axis_index("tensor")
    flip = tensor + 1 - 2 * rem(tensor, 2)
    for there in (flip, rem(flip + 8, NR)):
        across = {"dp": dp + 1 - 2 * rem(dp, 2), "tensor": there}
        pl.semaphore_signal(barrier, inc=1, device_id=across, device_id_type=MESH)
    pl.semaphore_wait(barrier, 2 * NR)


class Sum:
    def __init__(self, axis, part, out, buffers):
        self.axis, self.part, self.out = axis, part, out
        self.got, self.half, self.ring, self.mid, self.mid_got, self.ssem, self.rsem = buffers
        index = lax.axis_index(axis)
        self.n = self.ring.shape[0]
        self.a = rem(index, 2)
        self.q = rem(index // 2, self.n)
        self.top = index // (2 * self.n)
        self.h = part.shape[0] // 2
        self.b = self.h // self.n
        self.sent = []

    def at(self, top, q, a):
        return {self.axis: (top * self.n + q) * 2 + a}

    def pair(self):
        return self.at(self.top, self.q, 1 - self.a)

    def peer(self, k):
        return self.at(self.top, rem(self.q + k, self.n), self.a)

    def over(self):
        return self.at(1 - self.top, self.q, self.a)

    def go(self, copy):
        copy.start()
        self.sent.append(copy)

    def first(self):
        src = self.part.at[rows((1 - self.a) * self.h, self.h), :]
        self.go(remote(src, self.got, self.ssem.at[0], self.rsem.at[0], **self.pair()))

    def second(self):
        remote(self.got, self.got, self.ssem.at[0], self.rsem.at[0], **self.pair()).wait_recv()
        mine = self.part[rows(self.a * self.h, self.h), :].astype(F32)
        self.half[...] = (mine + self.got[...].astype(F32)).astype(BF)
        for k in range(1, self.n):
            to = rem(self.q + k, self.n)
            src = self.half.at[rows(to * self.b, self.b), :]
            self.go(remote(src, self.ring.at[self.q], self.ssem.at[k], self.rsem.at[k], **self.peer(k)))

    def reduced(self):
        total = self.half[rows(self.q * self.b, self.b), :].astype(F32)
        for k in range(1, self.n):
            source = rem(self.q + self.n - k, self.n)
            slot = self.ring.at[source]
            remote(slot, slot, self.ssem.at[k], self.rsem.at[k], **self.peer(k)).wait_recv()
            total = total + self.ring[source].astype(F32)
        return total

    def spread(self, total):
        here = rows(self.a * self.h + self.q * self.b, self.b)
        self.out[here, :] = total.astype(BF)
        piece = self.out.at[here, :]
        for k in range(1, self.n):
            self.go(remote(piece, piece, self.ssem.at[7 + k], self.rsem.at[7 + k], **self.peer(k)))

    def third(self):
        if self.mid is None:
            self.spread(self.reduced())
        else:
            self.mid[...] = self.reduced().astype(BF)
            self.go(remote(self.mid, self.mid_got, self.ssem.at[16], self.rsem.at[16], **self.over()))

    def across(self):
        remote(self.mid, self.mid_got, self.ssem.at[16], self.rsem.at[16], **self.over()).wait_recv()
        self.spread(self.mid[...].astype(F32) + self.mid_got[...].astype(F32))

    def fourth(self):
        for k in range(1, self.n):
            source = rem(self.q + self.n - k, self.n)
            piece = self.out.at[rows(self.a * self.h + source * self.b, self.b), :]
            remote(piece, piece, self.ssem.at[7 + k], self.rsem.at[7 + k], **self.peer(k)).wait_recv()
        mine = self.out.at[rows(self.a * self.h, self.h), :]
        self.go(remote(mine, mine, self.ssem.at[15], self.rsem.at[15], **self.pair()))

    def last(self):
        other = self.out.at[rows((1 - self.a) * self.h, self.h), :]
        remote(other, other, self.ssem.at[15], self.rsem.at[15], **self.pair()).wait_recv()

    def drain(self):
        for copy in self.sent:
            copy.wait_send()


def dma(*shape):
    return pltpu.SemaphoreType.DMA(shape)


def sum_buffers(r, n):
    h = r // 2
    cut = pltpu.VMEM((h // n, C), BF)
    mids = [cut, cut] if n == NY else [None, None]
    return [pltpu.VMEM((h, C), BF), pltpu.VMEM((h, C), BF), pltpu.VMEM((n, h // n, C), BF)] + mids + [dma(17), dma(17)]


def add_rows(dst, src):
    @pl.loop(0, dst.shape[0] // 80)
    def _(i):
        here = rows(i * 80, 80)
        dst[here, :] = (dst[here, :].astype(F32) + src[here, :].astype(F32)).astype(BF)


def kernel(
    x_hbm, gain, bias, w_in, owt, enc, dect, got,
    ro_t, gi_t, gq, gow_t, gb,
    x, w, nb, no, acc, mu, rstd, xt, gcol, hat, st,
    cg_part, fo_part, cg, folded, ps, pr, qkv, ag, attn, qg, qo, qgt, dkv,
    con, rb1, rb, po, px, cr, ys, yh, yr, fs, fv, ng, lt, gs, code, mixing,
    t1, d1, t2, d2,
    x_sem, loc, a_ss, a_rs, n_ss, n_rs, g_ss, g_rs, f_ss, f_rs, p_ss, p_rs, q_ss, q_rs,
    r1_ss, r1_rs, r_ss, r_rs, cs_ss, cs_rs, yh_ss, yh_rs, y_ss, y_rs, xh_ss, xh_rs, fs_ss, fs_rs, lt_ss, lt_rs, gs_ss, gs_rs,
):
    dp, tensor = lax.axis_index("dp"), lax.axis_index("tensor")
    z, xl = dp // 2, rem(dp, 2)
    up, down = rem(z + 1, NZ) * 2 + xl, rem(z + NZ - 1, NZ) * 2 + xl
    other = z * 2 + 1 - xl
    core, q = rem(tensor, 2), tensor // 2
    xh, y = q // NY, rem(q, NY)
    sibling = q * 2 + 1 - core
    ways = ((0, up), (1, down))
    sent = []

    def go(copy):
        copy.start()
        sent.append(copy)

    x_copies = [
        pltpu.make_async_copy(x_hbm.at[pl.ds(i * 128, 128), :], x.at[pl.ds(i * 128, 128), :], x_sem.at[i])
        for i in range(4)
    ]
    for copy in x_copies:
        copy.start()
    enter()

    def block(j, zs, offset=0, size=BLK):
        return w.at[j, rows(zs * BLK + offset, size), :]

    mine = pltpu.make_async_copy(w_in, w.at[:, rows(z * BLK, BLK), :], loc)
    mine.start()

    def send_own(j):
        for way, to in ways:
            go(remote(w_in.at[j], block(j, z), a_ss.at[way, j, 0], a_rs.at[way, j, 0], dp=to))

    def relay(j, s):
        for way, to in ways:
            zs = rem(z + (NZ - s if way == 0 else s), NZ)
            if s < 4:
                part = block(j, zs)
                remote(part, part, a_ss.at[way, j, s - 1], a_rs.at[way, j, s - 1], dp=to).wait_recv()
                if s == 3:
                    part = block(j, zs, way * HB, HB)
                go(remote(part, part, a_ss.at[way, j, s], a_rs.at[way, j, s], dp=to))
            else:
                part = block(j, zs, way * HB, HB)
                remote(part, part, a_ss.at[way, j, 3], a_rs.at[way, j, 3], dp=to).wait_recv()

    send_own(0)
    send_own(1)
    sum_d = Sum("dp", fo_part, folded, d1)
    sum_t = Sum("tensor", cg_part, cg, t1)

    def start_folded():
        fo_part[...] = dot_tn(owt[...], enc[...]).astype(BF)
        sum_d.first()

    def start_code_grad():
        cg_part[...] = dot_tn(got[...], dect[...]).astype(BF)
        sum_t.first()

    def slab_cols(zs):
        return pl.ds(pl.multiple_of(zs * SLAB, 128), SLAB)

    def near(i):
        odd = rem(i, 2)
        return rem(z + odd * ((i + 1) // 2) + (1 - odd) * (NZ - i // 2), NZ)

    def tokens(r):
        return pl.ds(r * 128, 128)

    def piece(k, c, r):
        return no.at[near(2 * k + c), :, tokens(r)]

    def cross(r):
        src = nb.at[1, near(2 * y + core), :, tokens(r)]
        return remote(src, piece(y, core, r), n_ss.at[r], n_rs.at[r], dp=other)

    def along(k, r):
        part = piece(y, core, r)
        there = (xh * NY + rem(y + k, NY)) * 2 + core
        return remote(part, part, g_ss.at[k - 1, r], g_rs.at[k - 1, r], tensor=there)

    def pass_on(k, r):
        part = piece(rem(y + NY - k, NY), core, r)
        return remote(part, part, f_ss.at[k, r], f_rs.at[k, r], tensor=sibling)

    def norm(r, lo, hi):
        if lo == 0:
            x_copies[r].wait()
            xt[:, r * 128 : (r + 1) * 128] = x[r * 128 : (r + 1) * 128, slab_cols(q)].T

        @pl.loop(lo, hi)
        def _(i):
            here = rows(r * 128 + i * 16, 16)
            v = x[here, :].astype(F32)
            mean = jnp.sum(v, axis=1, keepdims=True) * (1.0 / D)
            v = v - mean
            var = jnp.sum(v * v, axis=1, keepdims=True) * (1.0 / D)
            scale = lax.rsqrt(var + EPS)
            mu[here, :] = jnp.broadcast_to(mean, (16, 128))
            rstd[here, :] = jnp.broadcast_to(scale, (16, 128))
            x[here, :] = (v * scale * gain[...] + bias[...]).astype(BF)

    def spread(r):
        @pl.loop(0, NZ)
        def _(zs):
            v = x[r * 128 : (r + 1) * 128, slab_cols(zs)].T
            nb[xl, zs, :, r * 128 : (r + 1) * 128] = v[0:BLK]
            nb[1 - xl, zs, :, r * 128 : (r + 1) * 128] = v[BLK:SLAB]

        go(cross(r))

    def forward_on(r):
        cross(r).wait_recv()
        for k in (2, 1, 3):
            go(along(k, r))
        go(pass_on(0, r))

    def share(r):
        for k in (1, 3, 2):
            part = piece(rem(y + NY - k, NY), core, r)
            remote(part, part, g_ss.at[k - 1, r], g_rs.at[k - 1, r], tensor=sibling).wait_recv()
            go(pass_on(k, r))

    def use(j, i, part):
        zs = near(i)
        here = slice(j * 256, (j + 1) * 256)
        source = nb.at[0, zs] if part == 0 else no.at[zs]
        acc[part, here, :] += dot_tn(block(j, zs)[...], source[...])

    def use_all(j, lo, hi, part):
        @pl.loop(lo, hi)
        def _(i):
            use(j, i, part)

    def partial(j):
        here = pl.ds(j * 256, 256)
        return remote(ps.at[here, :], pr.at[here, :], p_ss.at[j], p_rs.at[j], dp=other)

    def give(j):
        here = slice(j * 256, (j + 1) * 256)
        ps[here, :] = acc[1, here, :].astype(BF)
        go(partial(j))

    def take(j):
        here = slice(j * 256, (j + 1) * 256)
        partial(j).wait_recv()
        qkv[:, here] = (acc[0, here, :] + pr[here, :].astype(F32)).astype(BF).T

    def collect():
        for r in range(4):
            for k in range(4):
                part = piece(rem(y + NY - k, NY), 1 - core, r)
                remote(part, part, f_ss.at[k, r], f_rs.at[k, r], tensor=sibling).wait_recv()

    work = deque()

    def add(cost, f, *args):
        work.append((cost, f, args))

    def run():
        cost, f, args = work.popleft()
        f(*args)
        return cost

    def ahead(f, *args):
        while any(piece[1:] == (f, args) for piece in work):
            run()

    def clear():
        acc[...] = jnp.zeros_like(acc)

    def relay_use(j, s):
        relay(j, s)
        lo, hi = (7, 8) if s == 4 else (2 * s - 1, 2 * s + 1)
        add(0.33 * (hi - lo), use_all, j, lo, hi, 0)

    def own_use():
        mine.wait()
        for j in range(3):
            add(0.33, use_all, j, 0, 1, 0)

    def far_use(j):
        use_all(j, 0, 8, 1)
        give(j)

    def far_begin():
        use_all(2, 0, 7, 1)

    def far_end():
        use_all(2, 7, 8, 1)
        give(2)

    add(1.2, start_folded)
    for r in range(4):
        add(1.3, norm, r, 0, 4)
        add(1.3, norm, r, 4, 8)
        add(1.1, spread, r)
        if r == 0:
            add(0.8, clear)
        if r == 2:
            add(1.5, start_code_grad)
    events = [
        (5.0, relay_use, 0, 1),
        (7.0, sum_d.second),
        (8.3, forward_on, 0),
        (8.5, relay_use, 1, 1),
        (12.0, relay_use, 0, 2),
        (13.0, forward_on, 1),
        (13.2, share, 0),
        (15.5, relay_use, 1, 2),
        (15.6, send_own, 2),
        (17.0, forward_on, 2),
        (17.2, share, 1),
        (19.0, relay_use, 0, 3),
        (19.5, sum_d.third),
        (20.5, forward_on, 3),
        (21.0, own_use),
        (21.5, share, 2),
        (21.5, sum_t.second),
        (24.0, relay_use, 2, 1),
        (25.0, share, 3),
        (25.5, sum_t.third),
        (27.0, relay_use, 1, 3),
        (27.5, collect),
        (29.0, relay_use, 0, 4),
        (29.5, far_use, 0),
        (31.0, sum_d.fourth),
        (31.5, sum_t.across),
        (33.0, relay_use, 2, 2),
        (35.0, relay_use, 1, 4),
        (35.5, far_use, 1),
        (38.5, sum_t.fourth),
        (39.0, relay_use, 2, 3),
        (39.5, far_begin),
        (42.5, sum_t.last),
        (43.0, relay_use, 2, 4),
        (43.0, far_end),
    ]
    now = 0.0
    for when, f, *args in events:
        while work and now + work[0][0] <= when + 0.3:
            now += run()
        if f is forward_on:
            ahead(spread, *args)
        elif f == sum_d.second:
            ahead(start_folded)
        elif f == sum_t.second:
            ahead(start_code_grad)
        f(*args)
        now = max(now, when) + (2.5 if f in (far_use, far_begin) else 0.2)
    while work:
        run()
    mine_rows = rows(core * BLK, BLK)
    rs_row = rstd[...].T[0:1, :]
    hat[...] = (xt[mine_rows, :].astype(F32) - mu[...].T[0:1, :]) * rs_row
    st[0:1, :] = rs_row
    turned = jnp.broadcast_to(gain[0:1, slab_cols(q)], (128, SLAB)).T
    gcol[...] = jnp.where(core == 0, turned[0:BLK], turned[BLK:SLAB])
    dkv[...] = jnp.zeros_like(dkv)
    take(0)
    take(1)

    rate = HDIM**-0.5
    blocks = [(h, r) for h in range(2) for r in range(4)]

    def cut(h, r):
        return slice(h * HDIM, (h + 1) * HDIM), slice(r * 128, (r + 1) * 128), 128 * (r + 1)

    def columns(j, h):
        return slice(j * 256 + h * HDIM, j * 256 + (h + 1) * HDIM)

    for h, r in blocks:
        _, here, n = cut(h, r)
        s = dot_nt(qkv[here, columns(0, h)], qkv[0:n, columns(1, h)]) * rate
        at_row = lax.broadcasted_iota(jnp.int32, (128, n), 0) + r * 128
        at_col = lax.broadcasted_iota(jnp.int32, (128, n), 1)
        s = jnp.where(at_col <= at_row, s, -1e30)
        e = jnp.exp(s - jnp.max(s, axis=1, keepdims=True))
        acc[h, here, 0:n] = e * (1.0 / jnp.sum(e, axis=1, keepdims=True))
    sum_d.last()
    ag[...] = dot_nt(cg[...], folded[...]).astype(BF)
    for h, r in blocks:
        cq, here, n = cut(h, r)
        dkv[0:n, columns(1, h)] += dot_tn(acc[h, here, 0:n].astype(BF), ag[here, cq])
    qg[:, 512:768] = dkv[:, 256:512].astype(BF)

    def swap_grad(j):
        here = pl.ds(j * 256, 256)
        return remote(qg.at[:, here], qo.at[:, here], q_ss.at[j], q_rs.at[j], dp=other)

    go(swap_grad(2))

    def contribute(j):
        @pl.loop(0, NZ)
        def _(zs):
            con[zs, j] = dot(nb[0, zs], qg[:, j * 256 : (j + 1) * 256]).astype(BF)

    contribute(2)
    take(2)
    for h, r in blocks:
        cq, here, n = cut(h, r)
        p, vb = acc[h, here, 0:n], qkv[0:n, columns(2, h)]
        attn[here, cq] = dot(p.astype(BF), vb).astype(BF)
        dpr = dot_nt(ag[here, cq], vb).astype(BF).astype(F32)
        ds = p * (dpr - jnp.sum(p * dpr, axis=1, keepdims=True))
        ds = (ds * rate).astype(BF)
        qg[here, cq] = dot(ds, qkv[0:n, columns(1, h)]).astype(BF)
        dkv[0:n, cq] += dot_tn(ds, qkv[here, columns(0, h)])
    go(swap_grad(0))
    qg[:, 256:512] = dkv[:, 0:256].astype(BF)
    go(swap_grad(1))

    def turn(part, source):
        @pl.loop(0, 6)
        def _(i):
            here = pl.ds(pl.multiple_of(i * 128, 128), 128)
            qgt[part, here, :] = source[:, here].T

    def term(zs, part):
        here = rows(zs * BLK, BLK)
        out = dot(w[0, here, :], qgt[part, 0:256, :])
        out = out + dot(w[1, here, :], qgt[part, 256:512, :])
        return out + dot(w[2, here, :], qgt[part, 512:768, :])

    def feature(i):
        return i % 2 * NY + rem(y + (2, 1, 3, 0)[i // 2], NY)

    keeps = core == xl

    def to_core(buffer, i):
        return remote(buffer.at[i], cr.at[i], cs_ss.at[i], cs_rs.at[i], tensor=sibling)

    def y_device(way):
        return (xh * NY + rem(y + 1 + 2 * way, NY)) * 2 + core

    def y_half(way, side):
        src = ys.at[side, pl.ds(way * HB, HB), :]
        return remote(src, yh.at[way, side], yh_ss.at[way, side], yh_rs.at[way, side], tensor=y_device(way))

    def y_full(way, side):
        src = ys.at[2 + 2 * way + side]
        return remote(src, yr.at[way, side], y_ss.at[way, side], y_rs.at[way, side], tensor=y_device(way))

    def join(buffer, i):
        to_core(buffer, i).wait_recv()
        ys[i] = (buffer[i].astype(F32) + cr[i].astype(F32)).astype(BF)
        if i < 2:
            for way in range(2):
                y_half(way, i).start()

    def y_second():
        for way in range(2):
            for side in range(2):
                y_half(way, side).wait_recv()
                add_rows(ys.at[2 + 2 * way + side, pl.ds(way * HB, HB), :], yh.at[way, side])
                y_full(way, side).start()

    def parts(buffer, part, sums, lo, hi):
        for i in range(lo, hi):
            buffer[i] = term(feature(i), part).astype(BF)

            @pl.when(sums)
            def _(i=i):
                if i > 0:
                    join(buffer, i - 1)
                if i == NQ - 1:
                    join(buffer, i)

            @pl.when(jnp.logical_not(sums))
            def _(i=i):
                to_core(buffer, i).start()

    def y_sum(which):
        total = ys[6 + which].astype(F32)
        for way in range(2):
            total = total + yr[way, which].astype(F32)
        return total

    swap = remote(fs.at[0], fv.at[0], xh_ss, xh_rs, tensor=((1 - xh) * NY + y) * 2 + core)

    def y_third():
        for way in range(2):
            for side in range(2):
                y_full(way, side).wait_recv()
        fs[0] = y_sum(1 - xh).astype(BF)
        swap.start()
        ng[...] = y_sum(xh)

    def home(which):
        there = (xh * (1 - which) + (1 - xh) * which) * NY + y
        return remote(
            fs.at[which], fv.at[which], fs_ss.at[which], fs_rs.at[which], dp=other, tensor=there * 2 + 1 - core
        )

    def y_home():
        for way in range(2):
            for side in range(2):
                y_full(way, side).wait_recv()
        for which in range(2):
            fs[which] = y_sum(xh * (1 - which) + (1 - xh) * which).astype(BF)
            home(which).start()

    def x_last():
        swap.wait_recv()
        ng[...] = ng[...] + fv[0].astype(F32)

    away = jnp.logical_not(keeps)

    z4 = rem(z + 4, NZ)

    def complete(j, lo, hi):
        @pl.loop(lo, hi)
        def _(i):
            zs = rem(z4 + i, NZ)
            here = slice(j * 256, (j + 1) * 256)
            con[zs, j] = (con[zs, j].astype(F32) + dot(no[zs], qo[:, here])).astype(BF)

    def open_ring(j):
        swap_grad(j).wait_recv()
        complete(j, 0, 1)
        ring(j, 1)

    def ring(j, s):
        for way, to in ways:
            if s == 1:
                half = con.at[z4, j, pl.ds(way * HB, HB), :]
                go(remote(half, rb1.at[j, way], r1_ss.at[j, way], r1_rs.at[j, way], dp=to))
                continue
            zs = rem(z + (5 - s if way == 0 else NZ + s - 5), NZ)
            if s == 2:
                remote(rb1.at[j, way], rb1.at[j, way], r1_ss.at[j, way], r1_rs.at[j, way], dp=to).wait_recv()
                add_rows(con.at[zs, j, pl.ds(way * HB, HB), :], rb1.at[j, way])
            else:
                slot = rb.at[j, way, s - 3]
                remote(slot, slot, r_ss.at[j, way, s - 3], r_rs.at[j, way, s - 3], dp=to).wait_recv()
                add_rows(con.at[zs, j], slot)
            if s < 5:
                slot = rb.at[j, way, s - 2]
                go(remote(con.at[zs, j], slot, r_ss.at[j, way, s - 2], r_rs.at[j, way, s - 2], dp=to))
        if s == 5:
            gq[j] = con[z, j].astype(F32) * (1.0 / NR)

    sum_t.drain()
    cg_part[...] = dot(attn[...], folded[...]).astype(BF)
    sum_t2 = Sum("tensor", cg_part, code, t2)
    sum_t2.first()
    turn(0, qg)
    parts(po, 0, keeps, 0, 2)
    open_ring(2)
    complete(2, 1, NZ)
    sum_d.drain()
    fo_part[...] = dot_tn(attn[...], cg[...]).astype(BF)
    sum_d2 = Sum("dp", fo_part, mixing, d2)
    sum_d2.first()
    parts(po, 0, keeps, 2, 5)
    sum_t2.second()
    ring(2, 2)
    parts(po, 0, keeps, 5, NQ)
    contribute(0)
    open_ring(0)
    complete(0, 1, NZ)
    ring(2, 3)

    @pl.when(keeps)
    def _():
        y_second()

    sum_t2.third()
    contribute(1)
    open_ring(1)
    ring(0, 2)
    turn(1, qo)
    parts(px, 1, away, 0, 4)
    complete(1, 1, NZ)
    ring(2, 4)
    parts(px, 1, away, 4, NQ)
    ring(0, 3)
    ring(1, 2)

    @pl.when(away)
    def _():
        y_second()

    @pl.when(keeps)
    def _():
        y_third()

    sum_t2.across()
    sum_d2.second()
    ring(2, 5)
    ring(0, 4)

    @pl.when(away)
    def _():
        y_home()

    @pl.when(keeps)
    def _():
        x_last()

    ring(1, 3)
    sum_t2.fourth()
    sum_d2.third()
    ring(0, 5)

    @pl.when(away)
    def _():
        for which in range(2):
            home(which).wait_recv()
        ng[...] = fv[0].astype(F32) + fv[1].astype(F32)

    grad = ng[...]
    scaled = grad * gcol[:, 0:1]
    lt[tensor, 0:1, :] = jnp.sum(scaled, axis=0, keepdims=True)
    lt[tensor, 1:2, :] = jnp.sum(scaled * hat[...], axis=0, keepdims=True)
    slot = lt.at[tensor]
    for k in range(1, NR):
        go(remote(slot, slot, lt_ss.at[k], lt_rs.at[k], tensor=rem(tensor + k, NR)))

    def fold(v):
        v = v[:, 0:128] + v[:, 128:256] + v[:, 256:384] + v[:, 384:512]
        v = jnp.concatenate([v, jnp.zeros((64, 128), F32)], axis=0)
        return jnp.sum(v.T, axis=0, keepdims=True)

    gs[dp, 0:1, :] = fold(ng[...] * hat[...])
    gs[dp, 1:2, :] = fold(ng[...])
    slot = gs.at[dp]
    for k in range(1, NR):
        go(remote(slot, slot, gs_ss.at[k], gs_rs.at[k], dp=rem(dp + k, NR)))
    ring(1, 4)
    sum_d2.fourth()
    sum_t2.last()
    ro_t[...] = (xt[mine_rows, :].astype(F32) + dot_nt(dect[...], code[...])).astype(BF)

    for k in range(1, NR):
        slot = lt.at[rem(tensor + NR - k, NR)]
        remote(slot, slot, lt_ss.at[k], lt_rs.at[k], tensor=tensor).wait_recv()
    sums = jnp.sum(lt[...], axis=0)
    lead, trail = sums[0:1, :] * (1.0 / D), sums[1:2, :] * (1.0 / D)
    scaled = ng[...] * gcol[:, 0:1]
    gi_t[...] = (got[...].astype(F32) + st[0:1, :] * (scaled - lead - hat[...] * trail)).astype(BF)
    ring(1, 5)
    sum_d2.last()
    gow_t[...] = dot_nt(enc[...], mixing[...]) * (1.0 / NR)
    for k in range(1, NR):
        slot = gs.at[rem(dp + NR - k, NR)]
        remote(slot, slot, gs_ss.at[k], gs_rs.at[k], dp=dp).wait_recv()
    gb[...] = jnp.sum(gs[...], axis=0) * (1.0 / NR)

    for total in (sum_t2, sum_d2):
        total.drain()
    for copy in sent:
        copy.wait_send()

    @pl.when(keeps)
    def _():
        swap.wait_send()

    @pl.when(away)
    def _():
        for which in range(2):
            home(which).wait_send()

    @pl.loop(0, NQ)
    def _(i):
        to_core(po, i).wait_send()

    for way in range(2):
        for side in range(2):
            y_half(way, side).wait_send()
            y_full(way, side).wait_send()


def sublayer(*args):
    def shape(dims, kind):
        return jax.ShapeDtypeStruct(dims, kind)

    def v(kind, *dims):
        return pltpu.VMEM(dims, kind)

    one = pltpu.SemaphoreType.DMA
    whole = pl.BlockSpec(memory_space=pltpu.VMEM)
    far = pl.BlockSpec(memory_space=pl.ANY)
    scratch = [
        v(BF, SEQ, D), v(BF, 3, NZ * BLK, 256), v(BF, 2, NZ, BLK, SEQ), v(BF, NZ, BLK, SEQ), v(F32, 2, W3, SEQ),
        v(F32, SEQ, 128), v(F32, SEQ, 128), v(BF, SLAB, SEQ), v(F32, BLK, 128), v(F32, BLK, SEQ), v(F32, 8, SEQ),
        v(BF, SEQ, C), v(BF, 256, C), v(BF, SEQ, C), v(BF, 256, C), v(BF, W3, SEQ), v(BF, W3, SEQ),
        v(BF, SEQ, W3), v(BF, SEQ, 256), v(BF, SEQ, 256), v(BF, SEQ, W3), v(BF, SEQ, W3), v(BF, 2, W3, SEQ),
        v(F32, SEQ, 512),
        v(BF, NZ, 3, BLK, 256), v(BF, 3, 2, HB, 256), v(BF, 3, 2, 3, BLK, 256),
        v(BF, NQ, BLK, SEQ), v(BF, NQ, BLK, SEQ), v(BF, NQ, BLK, SEQ), v(BF, NQ, BLK, SEQ), v(BF, 2, 2, HB, SEQ), v(BF, 2, 2, BLK, SEQ),
        v(BF, 2, BLK, SEQ), v(BF, 2, BLK, SEQ), v(F32, BLK, SEQ),
        v(F32, NR, 8, SEQ), v(F32, NR, 8, 384), v(BF, SEQ, C), v(BF, 256, C),
        sum_buffers(SEQ, NY), sum_buffers(256, NZ), sum_buffers(SEQ, NY), sum_buffers(256, NZ),
        dma(4), one, dma(2, 3, 4), dma(2, 3, 4), dma(4), dma(4), dma(3, 4), dma(3, 4), dma(4, 4), dma(4, 4), dma(3), dma(3), dma(3), dma(3),
        dma(3, 2), dma(3, 2), dma(3, 2, 3), dma(3, 2, 3), dma(NQ), dma(NQ), dma(2, 2), dma(2, 2), dma(2, 2), dma(2, 2), one, one, dma(2), dma(2),
        dma(NR), dma(NR), dma(NR), dma(NR),
    ]
    return pl.pallas_call(
        kernel,
        out_shape=[
            shape((BLK, SEQ), BF),
            shape((BLK, SEQ), BF),
            shape((3, BLK, 256), F32),
            shape((BLK, 256), F32),
            shape((8, 384), F32),
        ],
        in_specs=[far, whole, whole, far, whole, whole, whole, whole],
        out_specs=[whole] * 5,
        scratch_shapes=scratch,
        compiler_params=pltpu.CompilerParams(
            collective_id=0, has_side_effects=True, vmem_limit_bytes=62 * 2**20
        ),
    )(*args)


def place_kernel(*refs):
    n = len(refs) // 2
    *refs, sems = refs
    copies = [pltpu.make_async_copy(refs[i], refs[n + i], sems.at[i]) for i in range(n)]
    for copy in copies:
        copy.start()
    for copy in copies:
        copy.wait()


def place(*arrays):
    far = pl.BlockSpec(memory_space=pl.ANY)
    return pl.pallas_call(
        place_kernel,
        out_shape=[jax.ShapeDtypeStruct(a.shape, a.dtype) for a in arrays],
        in_specs=[pl.BlockSpec(memory_space=pltpu.VMEM)] * len(arrays),
        out_specs=[far] * len(arrays),
        scratch_shapes=[dma(len(arrays))],
    )(*arrays)


def local(
    residual_in,
    layernorm_gain,
    layernorm_bias,
    qkv_weight,
    out_weight,
    encoder,
    decoder,
    grad_output,
):
    residual_out, grad_input, grad_qkv, grad_out_weight, sums = sublayer(
        residual_in,
        layernorm_gain[None, :],
        layernorm_bias[None, :],
        qkv_weight,
        out_weight.T,
        encoder,
        decoder.T,
        grad_output.T,
    )
    residual_out, grad_input, grad_qkv, grad_out_weight = place(
        residual_out, grad_input, grad_qkv, grad_out_weight
    )
    return residual_out.T, grad_input.T, grad_qkv, grad_out_weight.T, sums[0, :BLK], sums[1, :BLK]


def solution(mesh):
    in_specs = (
        P("dp", None),
        P(),
        P(),
        P(None, "dp", "tensor"),
        P("tensor", "dp"),
        P("dp", None),
        P(None, "tensor"),
        P("dp", "tensor"),
    )
    out_specs = (
        P("dp", "tensor"),
        P("dp", "tensor"),
        P(None, "dp", "tensor"),
        P("tensor", "dp"),
        P("tensor"),
        P("tensor"),
    )
    return jax.shard_map(local, mesh=mesh, in_specs=in_specs, out_specs=out_specs, check_vma=False)
```
